32 devices in a mesh: dp: 8 (over z, y), seq: 4 (over x, core).
Axes of the slice: x: 2, y: 2, z: 4, core: 2. Of those that a mesh axis runs over, the one named last changes fastest.
Arguments:
- queries: bfloat16 [8, 512, 1024], P('dp', 'seq'), may hold values from -6 to 6
- key_rows: bfloat16 [8, 512, 1024], P('dp', 'seq'), may hold values from -6 to 6
- value_rows: bfloat16 [8, 512, 1024], P('dp', 'seq'), may hold values from -6 to 6
- inputs: bfloat16 [8, 512, 1024], P('dp', 'seq'), may hold values from -6 to 6
- w_gate: float32 [1024, 32], replicated, may hold values from -0.1875 to 0.1875
- poly_coef: float32 [1024], replicated, may hold values from -0.6 to 0.6
- decay_rate: float32 [16], replicated, may hold values from 0.0003 to 0.05
- cotangent: bfloat16 [8, 512, 1024], P('dp', 'seq'), may hold values from -6 to 6
Outputs:
- grad_queries: bfloat16 [8, 512, 1024], P('dp', 'seq')
- grad_keys: bfloat16 [8, 512, 1024], P('dp', 'seq')
- grad_values: bfloat16 [8, 512, 1024], P('dp', 'seq')
- grad_inputs: bfloat16 [8, 512, 1024], P('dp', 'seq')
- grad_gate: float32 [1024, 32], replicated
- grad_coef: float32 [1024], replicated
- grad_rate: float32 [16], replicated
The draws below stay inside these ranges and needn't reach their ends.
All inputs are finite; a program needn't handle non-finite values.
Results may differ from the reference program's by a relative error of at most 0.02.
Values may be sent and summed in bfloat16 or wider, within the bound.
No kernel may reach another device: no remote copies, remote signals or barrier semaphores. Data moves between devices by JAX's collectives and lax.ppermute only.
A program may use at most 64 MiB of HBM per device.

```python
import math
import jax
import jax.numpy as jnp
from jax import lax

D = 1024
H = 16
DH = 64
WINDOW = 64
WIDTH = 1024
SEQS = 8
LENGTH = 512


def block_levels(key, shape, pieces, smallest, high):
    loudness = 1.0
    for position, shards_of in pieces:
        steps = jax.random.uniform(jax.random.fold_in(jax.random.fold_in(key, 6), position), (shards_of,), jnp.float32, smallest / len(pieces), high / len(pieces))
        loudness = loudness * jnp.repeat(jnp.exp(steps), shape[position] // shards_of).reshape((-1,) + (1,) * (len(shape) - 1 - position))
    return loudness


def centred(key, extent, deviation, most, pieces=(), dtype=jnp.bfloat16):
    entries = deviation * jax.random.normal(key, extent, jnp.float32)
    if pieces:
        entries = entries * block_levels(key, extent, pieces, -0.22, 0.18)
    return jnp.clip(entries, -most, most).astype(dtype)


def setup_inputs(seed: int = 0) -> dict:
    key_list = jax.random.split(jax.random.key(seed), 9)
    return {
        "queries": centred(key_list[0], (SEQS, LENGTH, WIDTH), 1.0, 6.0, ((0, 8), (1, 4))),
        "key_rows": centred(key_list[1], (SEQS, LENGTH, WIDTH), 1.0, 6.0, ((0, 8), (1, 4))),
        "value_rows": centred(key_list[2], (SEQS, LENGTH, WIDTH), 1.0, 6.0, ((0, 8), (1, 4))),
        "inputs": centred(key_list[3], (SEQS, LENGTH, D), 1.0, 6.0, ((0, 8), (1, 4))),
        "w_gate": centred(key_list[4], (D, 2 * H), D ** -0.5, 0.1875, (), jnp.float32),
        "poly_coef": jnp.clip(jax.random.uniform(key_list[5], (WIDTH,), jnp.float32, -0.6, 0.6), -0.6, 0.6),
        "decay_rate": jnp.clip(jnp.exp(jax.random.uniform(key_list[6], (H,), jnp.float32, math.log(0.0003), math.log(0.05))), 0.0003, 0.05),
        "cotangent": centred(key_list[7], (SEQS, LENGTH, WIDTH), 1.0, 6.0, ((0, 8), (1, 4))),
    }


highest = lax.Precision.HIGHEST

def features(raw, poly_coef):
    as_float = raw.astype(jnp.float32)
    return 0.125 * (as_float + poly_coef * as_float * as_float)

def block_step(memory, block_in):
    q_block, key_pairs, value_pairs, decay_log = block_in
    window = q_block.shape[0]
    head_count = decay_log.shape[1]
    head_dim = q_block.shape[1] // head_count
    log_decay = jnp.cumsum(decay_log, axis=0)
    row_ids = lax.broadcasted_iota(jnp.int32, (window, window), 0)
    col_ids = lax.broadcasted_iota(jnp.int32, (window, window), 1)
    causal = col_ids <= row_ids
    gap_log = jnp.where(causal[:, :, None], log_decay[:, None, :] - log_decay[None, :, :], 0.0)
    decay_mat = jnp.where(causal[:, :, None], jnp.exp(gap_log), 0.0)
    step_ids = lax.broadcasted_iota(jnp.int32, (window, 2 * window), 0)
    slot_ids = lax.broadcasted_iota(jnp.int32, (window, 2 * window), 1)
    offset = step_ids - slot_ids + window
    window_mask = ((offset >= 0) & (offset < window)).astype(jnp.float32)
    kernel = jnp.einsum('tsh,si->hti', decay_mat, window_mask, precision=highest)
    q_heads = q_block.reshape(window, head_count, head_dim).astype(jnp.float32)
    key_heads = key_pairs.reshape(2 * window, head_count, head_dim)
    value_heads = value_pairs.reshape(2 * window, head_count, head_dim).astype(jnp.float32)
    scores = jnp.einsum('thd,ihd->hti', q_heads, key_heads.astype(jnp.float32), precision=highest)
    weights = (scores * kernel).astype(jnp.bfloat16)
    inside = jnp.einsum('hti,ihd->thd', weights.astype(jnp.float32), value_heads, precision=highest)
    carried_out = jnp.einsum('thd,hde->the', q_heads, memory, precision=highest) * jnp.exp(log_decay)[:, :, None]
    last_row = kernel[:, window - 1, :]
    carried = (key_heads.astype(jnp.float32) * jnp.transpose(last_row)[:, :, None]).astype(jnp.bfloat16)
    update = jnp.einsum('ihd,ihe->hde', carried.astype(jnp.float32), value_heads, precision=highest)
    memory_next = jnp.exp(log_decay[window - 1])[:, None, None] * memory + update
    return (memory_next, (inside + carried_out).reshape(window, head_count * head_dim))

def local_forward(queries, key_rows, value_rows, inputs, w_gate, poly_coef, decay_rate, key_rim, value_rim, input_rim, memory):
    length = queries.shape[0]
    window = key_rim.shape[0]
    head_count = decay_rate.shape[0]
    width_all = queries.shape[1]
    head_dim = width_all // head_count
    blocks = length // window
    all_inputs = jnp.concatenate([input_rim, inputs], axis=0)
    logits = jnp.dot(all_inputs.astype(jnp.float32), w_gate, precision=highest)
    decay_log = -decay_rate * jax.nn.softplus(logits[window:, :head_count])
    gamma = jax.nn.sigmoid(logits[:, head_count:]) / window
    all_keys = jnp.concatenate([key_rim, key_rows], axis=0)
    all_values = jnp.concatenate([value_rim, value_rows], axis=0)
    weighted = (features(all_keys, poly_coef).reshape(-1, head_count, head_dim) * gamma[:, :, None]).astype(jnp.bfloat16).reshape(-1, width_all)
    query_feat = features(queries, poly_coef).astype(jnp.bfloat16)
    key_pairs = jnp.concatenate([weighted[:length].reshape(blocks, window, width_all), weighted[window:].reshape(blocks, window, width_all)], axis=1)
    value_pairs = jnp.concatenate([all_values[:length].reshape(blocks, window, width_all), all_values[window:].reshape(blocks, window, width_all)], axis=1)
    memory_end, outputs = lax.scan(block_step, memory, (query_feat.reshape(blocks, window, width_all), key_pairs, value_pairs, decay_log.reshape(blocks, window, head_count)))
    return (outputs.reshape(length, width_all), memory_end, lax.optimization_barrier(jnp.sum(decay_log, axis=0)))

def reference(queries, key_rows, value_rows, inputs, w_gate, poly_coef, decay_rate, cotangent):

    def one_sequence(items):
        q_seq, k_seq, v_seq, x_seq, g_seq = items
        width_all = q_seq.shape[1]
        key_rim = jnp.zeros((WINDOW, width_all), jnp.bfloat16)
        value_rim = jnp.zeros((WINDOW, width_all), jnp.bfloat16)
        input_rim = jnp.zeros((WINDOW, D), jnp.bfloat16)
        memory = jnp.zeros((H, DH, DH), jnp.float32)
        primal, pullback = jax.vjp(local_forward, q_seq, k_seq, v_seq, x_seq, w_gate, poly_coef, decay_rate, key_rim, value_rim, input_rim, memory)
        grads = pullback((g_seq.astype(jnp.float32), jnp.zeros_like(primal[1]), jnp.zeros_like(primal[2])))
        return (grads[0], grads[1], grads[2], grads[3], grads[4], grads[5], grads[6])
    results = lax.map(one_sequence, (queries, key_rows, value_rows, inputs, cotangent))
    return (results[0], results[1], results[2], results[3], lax.optimization_barrier(jnp.sum(results[4], axis=0)), lax.optimization_barrier(jnp.sum(results[5], axis=0)), lax.optimization_barrier(jnp.sum(results[6], axis=0)))
```

```python
import functools

import jax
import jax.numpy as jnp
from jax import lax
from jax.experimental import pallas as pl
from jax.experimental.pallas import tpu as pltpu
from jax.sharding import PartitionSpec as P

WINDOW = 64
LANES = 128
BAND = 16
F32 = jnp.float32
BF16 = jnp.bfloat16


def iota(shape, dim):
    return lax.broadcasted_iota(jnp.int32, shape, dim)


def split(z, count):
    parts = []
    for _ in range(count):
        high = z.astype(BF16)
        parts.append(high)
        z = z - high.astype(F32)
    return parts


def dot(a, b):
    return lax.dot_general(a, b, (((1,), (0,)), ((), ())), preferred_element_type=F32)


def dot_nt(a, b):
    return lax.dot_general(a, b, (((1,), (1,)), ((), ())), preferred_element_type=F32)


def dot_tn(a, b):
    return lax.dot_general(a, b, (((0,), (0,)), ((), ())), preferred_element_type=F32)


def mask_dot(mask, z, count):
    return sum(dot(mask, part) for part in split(z, count))


def head_table(heads, width):
    per_head = width // heads
    return (iota((heads, width), 1) // per_head == iota((heads, width), 0)).astype(BF16)


def expand(z, table, count=1):
    return sum(dot(part, table) for part in split(z, count))


def head_sum(z, table, count=1):
    return sum(dot_nt(part, table) for part in split(z, count))


def half_masks():
    lane = iota((1, LANES), 1)
    return (lane < LANES // 2).astype(BF16), (lane >= LANES // 2).astype(BF16)


def stacked(z, masks):
    return jnp.concatenate([z * masks[0], z * masks[1]], axis=0)


def one_above(z):
    columns = z.shape[1] // 2
    return jnp.concatenate([z[:, :columns], z[:, columns:]], axis=0)


def folded(z):
    rows = z.shape[0] // 2
    return jnp.where(iota((rows, LANES), 1) < LANES // 2, z[:rows], z[rows:])


def window_own(length):
    gap = iota((length, length), 0) - iota((length, length), 1)
    return ((gap >= 0) & (gap < WINDOW)).astype(BF16)


def window_own_t(length):
    gap = iota((length, length), 1) - iota((length, length), 0)
    return ((gap >= 0) & (gap < WINDOW)).astype(BF16)


def window_rim():
    return (iota((WINDOW, WINDOW), 0) < iota((WINDOW, WINDOW), 1)).astype(BF16)


def window_rim_t():
    return (iota((WINDOW, WINDOW), 1) < iota((WINDOW, WINDOW), 0)).astype(BF16)


def phi(raw, coef):
    return 0.125 * (raw + coef * raw * raw)


def is_odd(me_ref):
    return jax.lax.rem(me_ref[0], 2) == 1


def everywhere(flag, shape):
    return jnp.full(shape, flag.astype(jnp.int32)) == 1


def prep_kernel(heads, count, me_ref, q_ref, k_ref, v_ref, x_ref, g_ref, w_ref, coef_ref, rate_ref,
                wk_ref, qf_ref, small_ref, near_ref, far_ref, memory_ref, adjoint_ref,
                q_buf, k_buf, v_buf, x_buf, g_buf, w_buf, coef_buf, rate_buf, sems):
    length, width = x_ref.shape
    late = length - WINDOW
    copies = [
        pltpu.make_async_copy(source, target, sems.at[i])
        for i, (source, target) in enumerate(
            [
                (x_ref, x_buf), (w_ref, w_buf), (rate_ref, rate_buf), (k_ref, k_buf),
                (coef_ref, coef_buf), (q_ref, q_buf), (v_ref, v_buf), (g_ref, g_buf),
            ]
        )
    ]
    for copy in copies:
        copy.start()
    table = head_table(heads, width)
    lower = (iota((length, length), 1) <= iota((length, length), 0)).astype(BF16)
    copies[0].wait()
    copies[1].wait()
    x = x_buf[...]
    logits = sum(dot_nt(x, part) for part in split(w_buf[...], 2))
    decay_logit = logits[:, :heads]
    soft = jnp.maximum(decay_logit, 0.0) + jnp.log1p(jnp.exp(-jnp.abs(decay_logit)))
    slope = jax.nn.sigmoid(decay_logit)
    gamma = jax.nn.sigmoid(logits[:, heads:]) * (1.0 / WINDOW)
    copies[2].wait()
    total = mask_dot(lower, -rate_buf[...] * soft, 3)
    small_ref[...] = jnp.concatenate(
        [total, gamma, soft, slope, jnp.zeros((length, LANES - 4 * heads), F32)], axis=1
    )
    info = jnp.concatenate(
        [part.astype(F32) for part in split(total[:WINDOW], 3)]
        + [jnp.zeros((WINDOW, LANES - 3 * heads), F32)],
        axis=1,
    ).astype(BF16)
    copies[3].wait()
    copies[4].wait()
    coef = coef_buf[...]
    wk = (phi(k_buf[...].astype(F32), coef) * expand(gamma, table)).astype(BF16)
    wk_ref[...] = wk
    copies[5].wait()
    qf = phi(q_buf[...].astype(F32), coef).astype(BF16)
    qf_ref[...] = qf
    copies[6].wait()
    copies[7].wait()
    kept = mask_dot(window_own_t(length), jnp.exp(total[length - 1:] - total), 2)
    faded = jnp.exp(total[late:] - total[late - 1:late])
    scale = expand(jnp.concatenate([kept, faded], axis=0), table)
    carried = (wk.astype(F32) * scale[:length]).astype(BF16)
    faded = (g_buf[late:].astype(F32) * scale[length:]).astype(BF16)
    memory, adjoint = [], []
    for pair in range(width // LANES):
        at = slice(pair * LANES, (pair + 1) * LANES)
        memory.append(folded(dot_tn(carried[:, at], v_buf[:, at])))
        adjoint.append(folded(dot_tn(qf[late:, at], faded[:, at])))
    memory, adjoint = jnp.concatenate(memory, axis=1), jnp.concatenate(adjoint, axis=1)
    memory_ref[...] = memory
    adjoint_ref[...] = adjoint

    def pack(onward, back):
        onward[:WINDOW] = wk[late:]
        onward[WINDOW:2 * WINDOW] = v_buf[late:]
        back[:WINDOW] = qf[:WINDOW]
        back[WINDOW:2 * WINDOW] = g_buf[:WINDOW]
        onward[2 * WINDOW:2 * WINDOW + BAND] = jnp.zeros((BAND, width), BF16)
        back[2 * WINDOW:2 * WINDOW + BAND] = jnp.zeros((BAND, width), BF16)
        for step in range(WINDOW // BAND):
            band = info[step * BAND:(step + 1) * BAND]
            back[2 * WINDOW:2 * WINDOW + BAND, step * LANES:(step + 1) * LANES] = band

    odd = is_odd(me_ref)
    pl.when(odd)(lambda: pack(far_ref, near_ref))
    pl.when(jnp.logical_not(odd))(lambda: pack(near_ref, far_ref))
    near_ref[2 * WINDOW + BAND:] = jnp.where(everywhere(odd, memory.shape), adjoint, memory).astype(BF16)

    @pl.when((me_ref[0] == 0) | (me_ref[0] == count - 1))
    def _():
        far_ref[...] = jnp.zeros_like(far_ref)


def received(me_ref, near_ref, far_ref, fwd_ref, bwd_ref):
    odd = is_odd(me_ref)

    def keep(before, after):
        fwd_ref[...] = before[:2 * WINDOW + BAND]
        bwd_ref[...] = after[:2 * WINDOW + BAND]

    pl.when(odd)(lambda: keep(near_ref, far_ref))
    pl.when(jnp.logical_not(odd))(lambda: keep(far_ref, near_ref))


def next_decay(rim_ref, heads):
    info = jnp.concatenate(
        [
            rim_ref[2 * WINDOW:2 * WINDOW + BAND, step * LANES:(step + 1) * LANES]
            for step in range(WINDOW // BAND)
        ],
        axis=0,
    ).astype(F32)
    return info[:, :heads] + info[:, heads:2 * heads] + info[:, 2 * heads:3 * heads]


def join_kernel(heads, count, before_if_odd, me_ref, own_ref, edge_ref, small_ref, memory_ref, adjoint_ref, rim_ref,
                *rest):
    state_ref, part_ref, out_ref = rest if len(rest) == 3 else (None, *rest)
    width = rim_ref.shape[1]
    length = small_ref.shape[0]
    table = head_table(heads, width)
    total = small_ref[:, :heads]
    last = total[length - 1:]
    middle = total[length - WINDOW - 1:length - WINDOW]
    next_total = next_decay(rim_ref, heads)
    before = is_odd(me_ref) if before_if_odd else jnp.logical_not(is_odd(me_ref))
    kept = mask_dot(window_rim_t(), jnp.exp(middle - total[:WINDOW]), 2)
    scale = jnp.where(everywhere(before, kept.shape), kept, jnp.exp(next_total))
    fade = jnp.exp(last - middle)
    weight = jnp.where(
        everywhere(before, fade.shape), jnp.exp(last), fade * jnp.exp(next_total[WINDOW - 1:])
    )
    scale = expand(jnp.concatenate([scale, fade, weight], axis=0), table)
    scaled = (rim_ref[WINDOW:2 * WINDOW].astype(F32) * scale[:WINDOW]).astype(BF16)
    fade, weight = scale[WINDOW:WINDOW + 1], scale[WINDOW + 1:]
    if state_ref is None:
        state = rim_ref[2 * WINDOW + BAND:].astype(F32)
    else:
        edge = (me_ref[0] == 0) | (me_ref[0] == count - 1)
        state = jnp.where(everywhere(edge, state_ref.shape), 0.0, state_ref[...].astype(F32))
    base = jnp.where(everywhere(before, memory_ref.shape), memory_ref[...], adjoint_ref[...])
    base = base + weight * state
    for pair in range(width // LANES):
        at = slice(pair * LANES, (pair + 1) * LANES)
        part = folded(dot_tn(rim_ref[:WINDOW, at], scaled[:, at]))
        part_ref[:, at] = part
        out_ref[:, at] = (base[:, at] + fade[:, at] * part).astype(BF16)


def decays(column_pair, row_pair, keep):
    gap = jnp.where(keep, column_pair - row_pair, -1e30)
    return jnp.exp(gap)


def own_kernel(heads, me_ref, small_ref, wk_ref, qf_ref, v_ref, g_ref, dq_ref, dwk_ref, dv_ref, dl_ref):
    length, width = wk_ref.shape
    table = head_table(heads, width)
    masks = half_masks()
    small = small_ref[...]
    total = small[:, :heads]
    total_t = jnp.transpose(small)[:heads]
    keep = iota((length, length), 1) <= iota((length, length), 0)
    own = window_own(length).astype(F32)
    empty = jnp.zeros_like(own)
    windows = jnp.concatenate(
        [jnp.concatenate([own, empty], axis=1), jnp.concatenate([empty, own], axis=1)], axis=0
    ).astype(BF16)
    pairs = [slice(pair * LANES, (pair + 1) * LANES) for pair in range(width // LANES)]
    held = []
    for pair, at in enumerate(pairs):
        decay = jnp.concatenate(
            [decays(total[:, i:i + 1], total_t[i:i + 1], keep) for i in (2 * pair, 2 * pair + 1)], axis=1
        )
        kernel = dot(decay.astype(BF16), windows)
        scores = dot_nt(qf_ref[:, at], stacked(wk_ref[:, at], masks))
        lifted = dot_nt(g_ref[:, at], stacked(v_ref[:, at], masks))
        held.append(
            (
                decay,
                (scores * kernel).astype(BF16),
                (lifted * kernel).astype(BF16),
                (lifted * scores).astype(BF16),
            )
        )
    columns = []
    products = []
    for (decay, weights, d_scores, d_kernel), at in zip(held, pairs):
        q, g = qf_ref[:, at], g_ref[:, at]
        products.append(dot(weights, stacked(v_ref[:, at], masks)) * g.astype(F32))
        dq_ref[:, at] = dot(d_scores, stacked(wk_ref[:, at], masks))
        dwk_ref[:, at] = dot_tn(one_above(d_scores), stacked(q, masks))
        dv_ref[:, at] = dot_tn(one_above(weights), stacked(g, masks))
        column = jnp.sum(dot_nt(d_kernel, windows) * decay, axis=0, keepdims=True)
        columns += [column[:, :length], column[:, length:]]
    column = jnp.concatenate(columns + [jnp.zeros((LANES - heads, length), F32)], axis=0)
    rows = head_sum(jnp.concatenate(products, axis=1), table)
    dl_ref[...] = rows - jnp.transpose(column)[:, :heads]


def edge_decay(total, heads):
    lane = iota((WINDOW, LANES), 1)
    first = lane < LANES // 2
    keep = jnp.where(first, lane, lane - LANES // 2) <= iota((WINDOW, LANES), 0)
    doubled = jnp.concatenate([total, total], axis=0)
    doubled = jnp.concatenate([doubled, jnp.zeros((2 * WINDOW, LANES - heads), F32)], axis=1)
    rows = jnp.transpose(doubled)[:heads]
    return lambda h: decays(
        jnp.where(first, total[:, h:h + 1], total[:, h + 1:h + 2]),
        jnp.where(first, rows[h:h + 1], rows[h + 1:h + 2]),
        keep,
    )


def scales_of(heads, small_ref, scales_ref):
    length = small_ref.shape[0]
    late = length - WINDOW
    total, gamma = small_ref[:, :heads], small_ref[:, heads:2 * heads]
    last, middle = total[length - 1:], total[late - 1:late]
    own = mask_dot(window_own_t(length), jnp.exp(last - total), 2)
    grown = jnp.exp(jnp.concatenate([total[:late], total[late:] - middle], axis=0))
    rest = [jnp.exp(middle), jnp.exp(last - middle), jnp.zeros((BAND - 2, heads), F32)]
    scales = jnp.concatenate([own, grown, gamma] + rest, axis=0)
    scales_ref[...] = expand(scales, head_table(heads, scales_ref.shape[1]))


def edge_kernel(heads, before_if_odd, me_ref, small_ref, wk_ref, qf_ref, v_ref, g_ref, rim_ref,
                first_ref, second_ref, dl_ref, *rest):
    length, width = wk_ref.shape
    late = length - WINDOW
    table = head_table(heads, width)
    masks = half_masks()
    pairs = [slice(pair * LANES, (pair + 1) * LANES) for pair in range(width // LANES)]
    cell = (iota((LANES, LANES), 0), iota((LANES, LANES), 1))
    same = (cell[0] < WINDOW) == (cell[1] < WINDOW)
    windows = (same & (cell[0] < cell[1])).astype(BF16)
    before = is_odd(me_ref) if before_if_odd else jnp.logical_not(is_odd(me_ref))
    if rest:
        scales_of(heads, small_ref, rest[0])

    @pl.when(before)
    def _():
        decay_at = edge_decay(small_ref[:WINDOW, :heads], heads)
        held = []
        for pair, at in enumerate(pairs):
            keys, values = stacked(rim_ref[:WINDOW, at], masks), stacked(rim_ref[WINDOW:2 * WINDOW, at], masks)
            decay = decay_at(2 * pair)
            kernel = dot(decay.astype(BF16), windows)
            scores = dot_nt(qf_ref[:WINDOW, at], keys)
            lifted = dot_nt(g_ref[:WINDOW, at], values)
            held.append(
                (
                    keys,
                    values,
                    decay,
                    (scores * kernel).astype(BF16),
                    (lifted * kernel).astype(BF16),
                    (lifted * scores).astype(BF16),
                )
            )
        columns, products = [], []
        for (keys, values, decay, weights, d_scores, d_kernel), at in zip(held, pairs):
            products.append(dot(weights, values) * g_ref[:WINDOW, at].astype(F32))
            first_ref[:, at] = dot(d_scores, keys)
            column = jnp.sum(dot_nt(d_kernel, windows) * decay, axis=0, keepdims=True)
            columns += [column[:, :WINDOW], column[:, WINDOW:]]
        column = jnp.concatenate(columns + [jnp.zeros((LANES - heads, WINDOW), F32)], axis=0)
        column = jnp.concatenate([column, jnp.zeros((LANES, LANES - WINDOW), F32)], axis=1)
        rows = head_sum(jnp.concatenate(products, axis=1), table)
        dl_ref[...] = rows - jnp.transpose(column)[:WINDOW, :heads]

    @pl.when(jnp.logical_not(before))
    def _():
        decay_at = edge_decay(next_decay(rim_ref, heads), heads)
        held = []
        for pair, at in enumerate(pairs):
            q, g = rim_ref[:WINDOW, at], rim_ref[WINDOW:2 * WINDOW, at]
            keys, values = stacked(wk_ref[late:, at], masks), stacked(v_ref[late:, at], masks)
            kernel = dot(decay_at(2 * pair).astype(BF16), windows)
            held.append(
                (q, g, (dot_nt(q, keys) * kernel).astype(BF16), (dot_nt(g, values) * kernel).astype(BF16))
            )
        for (q, g, weights, d_scores), at in zip(held, pairs):
            first_ref[:, at] = dot_tn(one_above(d_scores), stacked(q, masks))
            second_ref[:, at] = dot_tn(one_above(weights), stacked(g, masks))


def finish_kernel(heads, count, me_ref, q_ref, k_ref, x_ref, v_ref, g_ref, coef_ref, rate_ref,
                  small_ref, wk_ref, qf_ref, near_ref, far_ref, adjoint_ref,
                  dqf_ref, dwk_ref, dvl_ref, dl_ref, scales_ref,
                  near_first_ref, near_second_ref, near_dl_ref, far_first_ref, far_second_ref, far_dl_ref,
                  near_part_ref, far_part_ref, cross_ref, passed_ref,
                  dq_out, dk_out, dv_out, logits_ref, keep_ref, give_ref,
                  fwd_ref, bwd_ref, rim_dq_ref, rim_dwk_ref, rim_dv_ref, rim_dl_ref,
                  dq_ref, dk_ref, dv_ref, sems):
    length, width = wk_ref.shape
    late = length - WINDOW
    pairs = width // LANES
    received(me_ref, near_ref, far_ref, fwd_ref, bwd_ref)

    def edges(dq, dl, dwk, dv):
        rim_dq_ref[...], rim_dl_ref[...] = dq[...], dl[...]
        rim_dwk_ref[...], rim_dv_ref[...] = dwk[...], dv[...]

    far_edge = (far_first_ref, far_dl_ref, near_first_ref, near_second_ref)
    near_edge = (near_first_ref, near_dl_ref, far_first_ref, far_second_ref)
    pl.when(is_odd(me_ref))(lambda: edges(*near_edge))
    pl.when(jnp.logical_not(is_odd(me_ref)))(lambda: edges(*far_edge))
    table = head_table(heads, width)
    masks = half_masks()
    small = small_ref[...]
    total, gamma, soft, slope = (small[:, i * heads:(i + 1) * heads] for i in range(4))
    last, middle = total[length - 1:], total[late - 1:late]
    tail = jnp.exp(last - total)
    own = mask_dot(window_own_t(length), tail, 2)
    next_total = next_decay(bwd_ref, heads)
    next_middle = next_total[WINDOW - 1:]
    onward = mask_dot(window_rim_t(), jnp.exp(next_middle - next_total), 2)
    grown = jnp.exp(jnp.concatenate([total[:late], total[late:] - middle], axis=0))
    fade = jnp.exp(last - middle)
    onward_x = expand(jnp.concatenate([onward, jnp.exp(next_middle)], axis=0), table)
    onward_x, next_x = onward_x[:WINDOW], onward_x[WINDOW:]
    own_x, grown_x, gamma_x = (scales_ref.at[i * length:(i + 1) * length] for i in range(3))
    middle_x, fade_x = (scales_ref[i:i + 1] for i in range(3 * length, 3 * length + 2))

    me = me_ref[0]
    shape = (WINDOW, width)
    odd = everywhere(is_odd(me_ref), shape)
    edge = everywhere((me == 0) | (me == count - 1), shape)
    cross = jnp.where(edge, 0.0, cross_ref[...].astype(F32))
    passed = passed_ref[...].astype(F32)
    near_part, far_part = near_part_ref[...], far_part_ref[...]
    start = jnp.where(odd, passed, cross)
    later = jnp.where(odd, cross, passed)
    after = jnp.where(odd, far_part, near_part) + next_x * later
    halfway = middle_x * start + jnp.where(odd, near_part, far_part)
    half_after = adjoint_ref[...] + fade_x * after
    d_state = jnp.sum(head_sum(after * halfway, table, 2), axis=0, keepdims=True)
    start, later, after, halfway, half_after = (
        z.astype(BF16) for z in (start, later, after, halfway, half_after)
    )

    own_products, rim_products, out_products, key_products, d_coef = [], [], [], [], []
    coef = coef_ref[...]
    for pair in range(pairs):
        at = slice(pair * LANES, (pair + 1) * LANES)
        m0, m1, a1, a0, b0 = (stacked(z[:, at], masks) for z in (start, halfway, after, half_after, later))
        qf, g, wk, v = qf_ref[:, at], g_ref[:, at], wk_ref[:, at], v_ref[:, at]
        from_q = jnp.concatenate([dot(qf[:late], m0), dot(qf[late:], m1)], axis=0)
        out_products.append(from_q * g.astype(F32))
        from_g = jnp.concatenate([dot_nt(g[:late], m0), dot_nt(g[late:], m1)], axis=0)
        dqf = dqf_ref[:, at] + grown_x[:, at] * from_g
        dqf = jnp.concatenate([dqf[:late] + rim_dq_ref[:, at], dqf[late:]], axis=0)
        from_keys = dot(wk, a1)
        own_products.append(from_keys * v.astype(F32))
        rim_products.append(dot(fwd_ref[:WINDOW, at], a0) * fwd_ref[WINDOW:2 * WINDOW, at].astype(F32))
        dwk = dwk_ref[:, at] + own_x[:, at] * dot_nt(v, a1)
        dv = dvl_ref[:, at] + own_x[:, at] * from_keys
        dwk = jnp.concatenate(
            [dwk[:late], dwk[late:] + rim_dwk_ref[:, at] + onward_x[:, at] * dot_nt(v[late:], b0)], axis=0
        )
        dv_ref[:late, at] = dv[:late].astype(BF16)
        dv_ref[late:, at] = (
            dv[late:] + rim_dv_ref[:, at] + onward_x[:, at] * dot(wk[late:], b0)
        ).astype(BF16)
        q, k = q_ref[:, at].astype(F32), k_ref[:, at].astype(F32)
        c = coef[:, at]
        key_products.append(dwk * phi(k, c))
        d_phi = dwk * gamma_x[:, at]
        dq_ref[:, at] = (dqf * (0.125 + 0.25 * c * q)).astype(BF16)
        dk_ref[:, at] = (d_phi * (0.125 + 0.25 * c * k)).astype(BF16)
        d_coef.append(jnp.sum(dqf * (0.125 * q * q) + d_phi * (0.125 * k * k), axis=0, keepdims=True))

    copies = [
        pltpu.make_async_copy(source, target, sems.at[i])
        for i, (source, target) in enumerate([(dq_ref, dq_out), (dk_ref, dk_out), (dv_ref, dv_out)])
    ]
    for copy in copies:
        copy.start()
    sums = jnp.concatenate(
        [
            jnp.concatenate(z, axis=1).astype(BF16)
            for z in (own_products, out_products, key_products, rim_products)
        ],
        axis=0,
    )
    sums = dot_nt(sums, table)
    d_own, d_out, d_gamma = (sums[i * length:(i + 1) * length] for i in range(3))
    d_rim = sums[3 * length:]
    d_tail = tail * mask_dot(window_own(length), d_own, 2)
    rim_tail = jnp.exp(middle - total[:late]) * mask_dot(window_rim(), d_rim, 2)
    at_end = jnp.sum(own * d_own, axis=0, keepdims=True) + fade * d_state
    d_total = dl_ref[...] + grown * d_out - d_tail
    d_total = jnp.concatenate([d_total[:late] + rim_dl_ref[...] - rim_tail, d_total[late:]], axis=0)
    d_total = d_total + jnp.where(iota((length, heads), 0) == length - 1, at_end, 0.0)
    upper = (iota((length, length), 1) >= iota((length, length), 0)).astype(BF16)
    d_decay = mask_dot(upper, d_total, 3)
    d_rate = -jnp.sum(d_decay * soft, axis=0, keepdims=True)
    d_logits = jnp.concatenate(
        [-rate_ref[...] * d_decay * slope, d_gamma * gamma * (1.0 - WINDOW * gamma)], axis=1
    )
    logits_ref[...] = d_logits
    gate = dot_tn(d_logits.astype(BF16), x_ref[...])
    d_rate = jnp.concatenate([d_rate, jnp.zeros((1, LANES - heads), F32)], axis=1)
    halves = []
    for half in range(2):
        blocks = range(half * pairs // 2, (half + 1) * pairs // 2)
        rest = [d_coef[i] for i in blocks] + [d_rate, jnp.zeros((BAND - 1 - len(blocks), LANES), F32)]
        rows = [gate[:, i * LANES:(i + 1) * LANES] for i in blocks]
        halves.append(jnp.concatenate(rows + rest, axis=0).astype(BF16))

    def give(mine, theirs):
        keep_ref[...] = mine
        give_ref[...] = theirs

    pl.when(is_odd(me_ref))(lambda: give(halves[1], halves[0]))
    pl.when(jnp.logical_not(is_odd(me_ref)))(lambda: give(halves[0], halves[1]))
    for copy in copies:
        copy.wait()


def inputs_kernel(me_ref, logits_ref, w_ref, dx_ref):
    high, low = (part.astype(F32) for part in split(logits_ref[...], 2))
    w_high, w_low = split(w_ref[...], 2)
    dx_ref[...] = dot(
        jnp.concatenate([high, low, high], axis=1).astype(BF16),
        jnp.concatenate([w_high, w_high, w_low], axis=0),
    ).astype(BF16)


def last_kernel(heads, me_ref, mine_ref, theirs_ref, gate_ref, coef_ref, rate_ref):
    odd = jnp.full(mine_ref.shape, jax.lax.rem(me_ref[0], 2)) == 1
    mine, theirs = mine_ref[...], theirs_ref[...]
    halves = [jnp.where(odd, theirs, mine), jnp.where(odd, mine, theirs)]
    blocks = gate_ref.shape[1] // LANES // 2
    for half in range(2):
        for i in range(blocks):
            at = slice((half * blocks + i) * LANES, (half * blocks + i + 1) * LANES)
            gate_ref[:, at] = halves[half][i * 2 * heads:(i + 1) * 2 * heads]
            coef_ref[:, at] = halves[half][blocks * 2 * heads + i:blocks * 2 * heads + i + 1]
    at = blocks * (2 * heads + 1)
    rate_ref[...] = halves[0][at:at + 1, :heads]


def call(kernel, outs, operands, name, scratch=(), in_place=(), outside=(), flops=10**8, moved=3 * 10**6):
    specs = [pl.BlockSpec(memory_space=pltpu.SMEM)]
    specs += [
        pl.BlockSpec(memory_space=pltpu.HBM if i in in_place else pltpu.VMEM)
        for i in range(1, len(operands))
    ]
    operands = [
        pltpu.with_memory_space_constraint(z, pltpu.HBM) if i in in_place else z
        for i, z in enumerate(operands)
    ]
    return pl.pallas_call(
        kernel,
        out_shape=tuple(jax.ShapeDtypeStruct(*out) for out in outs),
        in_specs=specs,
        out_specs=tuple(
            pl.BlockSpec(memory_space=pltpu.HBM if i in outside else pltpu.VMEM) for i in range(len(outs))
        ),
        scratch_shapes=list(scratch),
        compiler_params=pltpu.CompilerParams(vmem_limit_bytes=32 * 2**20),
        cost_estimate=pl.CostEstimate(flops=flops, bytes_accessed=moved, transcendentals=10**6),
        name=name,
    )(*operands)


EVERYONE = ("dp", "seq")


def swapped(value, axis, distance):
    return lax.ppermute(value, axis, [(i, i ^ distance) for i in range(lax.axis_size(axis))])


def inner_swapped(value):
    dp, seq = (lax.axis_size(axis) for axis in EVERYONE)
    pairs = []
    for i in range(dp):
        for j in range(seq):
            inner = 0 < j < seq - 1
            pairs.append((i * seq + j, i * seq + seq - 1 - j if inner else (i ^ 1) * seq + j))
    return lax.ppermute(value, EVERYONE, pairs)


def on_device(queries, key_rows, value_rows, inputs, w_gate, poly_coef, decay_rate, cotangent):
    q, k, v, x, g = (z[0] for z in (queries, key_rows, value_rows, inputs, cotangent))
    length, width = x.shape
    heads = decay_rate.shape[0]
    count = lax.axis_size("seq")
    assert count == 4 and length == 2 * WINDOW
    me = lax.axis_index("seq").astype(jnp.int32).reshape(1)
    wide, small = ((length, width), BF16), ((length, LANES), F32)
    full, half, gain = ((length, width), F32), ((WINDOW, width), F32), ((length, heads), F32)
    rim, sent = ((2 * WINDOW + BAND, width), BF16), ((WINDOW, width), BF16)
    wk, qf, gates, near, far, memory, adjoint, q, k, v, x, g, wt, coef, rate = call(
        functools.partial(prep_kernel, heads, count),
        [wide, wide, small, ((3 * WINDOW + BAND, width), BF16), rim, half, half]
        + [wide] * 5
        + [((2 * heads, width), F32), ((1, width), F32), ((1, heads), F32)],
        (me, q, k, v, x, g, w_gate.T, poly_coef.reshape(1, width), decay_rate.reshape(1, heads)),
        "prep",
        scratch=[pltpu.SemaphoreType.DMA((8,))],
        in_place=range(1, 9),
    )
    near = swapped(near, "seq", 1)
    far = inner_swapped(far)
    near_part, cross = call(
        functools.partial(join_kernel, heads, count, True),
        [half, sent],
        (me, gates, gates, gates, memory, adjoint, near),
        "join_near",
    )
    cross = inner_swapped(cross)
    own = call(
        functools.partial(own_kernel, heads),
        [full, full, full, gain],
        (me, gates, wk, qf, v, g),
        "own",
        flops=7 * 10**8,
        moved=7 * 10**6,
    )
    edge = [half, half, ((WINDOW, heads), F32)]
    *near_edge, scales = call(
        functools.partial(edge_kernel, heads, True),
        edge + [((3 * length + BAND, width), F32)],
        (me, gates, wk, qf, v, g, near),
        "edge_near",
        flops=2 * 10**8,
        moved=5 * 10**6,
    )
    far_part, passed = call(
        functools.partial(join_kernel, heads, count, False),
        [half, sent],
        (me, own[3], near_edge[2], gates, memory, adjoint, far, cross),
        "join_far",
    )
    passed = swapped(passed, "seq", 1)
    far_edge = call(
        functools.partial(edge_kernel, heads, False),
        edge,
        (me, gates, wk, qf, v, g, far),
        "edge_far",
        flops=2 * 10**8,
        moved=3 * 10**6,
    )
    half_sums = ((width // LANES // 2 * 2 * heads + BAND, LANES), BF16)
    dq, dk, dv, d_logits, keep, give = call(
        functools.partial(finish_kernel, heads, count),
        [wide, wide, wide, ((length, 2 * heads), F32), half_sums, half_sums],
        (me, q, k, x, v, g, coef, rate, gates, wk, qf, near, far, adjoint, *own, scales, *near_edge, *far_edge,
         near_part, far_part, cross, passed),
        "finish",
        scratch=[pltpu.VMEM(*z) for z in (rim, rim, half, half, half, edge[2], wide, wide, wide)]
        + [pltpu.SemaphoreType.DMA((3,))],
        outside=range(3),
    )
    dx = call(inputs_kernel, [wide], (me, d_logits, wt), "inputs")[0]
    sums = keep.astype(F32) + swapped(give, EVERYONE, 1).astype(F32)
    distance = 2
    while distance < lax.axis_size(EVERYONE):
        sums = sums.astype(BF16)
        if 2 * distance < lax.axis_size(EVERYONE):
            far, mid, one = (swapped(sums, EVERYONE, i * distance).astype(F32) for i in (3, 2, 1))
            sums = (sums.astype(F32) + one) + (mid + far)
        else:
            sums = sums.astype(F32) + swapped(sums, EVERYONE, distance).astype(F32)
        if distance == 2:
            sums, dx = lax.optimization_barrier((sums, dx))
        distance *= 4
    gate, d_coef, d_rate = call(
        functools.partial(last_kernel, heads),
        [((2 * heads, width), F32), ((1, width), F32), ((1, heads), F32)],
        (me, sums, swapped(sums, "seq", 1)),
        "last",
    )
    return (dq[None], dk[None], dv[None], dx[None], gate.T, d_coef.reshape(width), d_rate.reshape(heads))


def solution(mesh):
    rows = P("dp", "seq", None)
    return jax.shard_map(
        on_device,
        mesh=mesh,
        in_specs=(rows, rows, rows, rows, P(), P(), P(), rows),
        out_specs=(rows, rows, rows, rows, P(), P(), P()),
        check_vma=False,
    )
```

```python
import functools

import jax
import jax.numpy as jnp
from jax import lax
from jax.experimental import pallas as pl
from jax.experimental.pallas import tpu as pltpu
from jax.sharding import PartitionSpec as P

WINDOW = 64
LANES = 128
BAND = 16
F32 = jnp.float32
BF16 = jnp.bfloat16


def iota(shape, dim):
    return lax.broadcasted_iota(jnp.int32, shape, dim)


def split(z, count):
    parts = []
    for _ in range(count):
        high = z.astype(BF16)
        parts.append(high)
        z = z - high.astype(F32)
    return parts


def dot(a, b):
    return lax.dot_general(a, b, (((1,), (0,)), ((), ())), preferred_element_type=F32)


def dot_nt(a, b):
    return lax.dot_general(a, b, (((1,), (1,)), ((), ())), preferred_element_type=F32)


def dot_tn(a, b):
    return lax.dot_general(a, b, (((0,), (0,)), ((), ())), preferred_element_type=F32)


def mask_dot(mask, z, count):
    return sum(dot(mask, part) for part in split(z, count))


def head_table(heads, width):
    per_head = width // heads
    return (iota((heads, width), 1) // per_head == iota((heads, width), 0)).astype(BF16)


def expand(z, table, count=1):
    return sum(dot(part, table) for part in split(z, count))


def head_sum(z, table, count=1):
    return sum(dot_nt(part, table) for part in split(z, count))


def half_masks():
    lane = iota((1, LANES), 1)
    return (lane < LANES // 2).astype(BF16), (lane >= LANES // 2).astype(BF16)


def stacked(z, masks):
    return jnp.concatenate([z * masks[0], z * masks[1]], axis=0)


def stacked_group(z):
    head = iota((1, z.shape[1]), 1) // WINDOW
    return jnp.concatenate([z * (head == i).astype(BF16) for i in range(z.shape[1] // WINDOW)], axis=0)


def one_above(z):
    columns = z.shape[1] // 2
    return jnp.concatenate([z[:, :columns], z[:, columns:]], axis=0)


def folded(z):
    rows = z.shape[0] // 2
    return jnp.where(iota((rows, LANES), 1) < LANES // 2, z[:rows], z[rows:])


def window_own(length):
    gap = iota((length, length), 0) - iota((length, length), 1)
    return ((gap >= 0) & (gap < WINDOW)).astype(BF16)


def window_own_t(length):
    gap = iota((length, length), 1) - iota((length, length), 0)
    return ((gap >= 0) & (gap < WINDOW)).astype(BF16)


def window_rim():
    return (iota((WINDOW, WINDOW), 0) < iota((WINDOW, WINDOW), 1)).astype(BF16)


def window_rim_t():
    return (iota((WINDOW, WINDOW), 1) < iota((WINDOW, WINDOW), 0)).astype(BF16)


def phi(raw, coef):
    return 0.125 * (raw + coef * raw * raw)


def is_odd(me_ref):
    return jax.lax.rem(me_ref[0], 2) == 1


def everywhere(flag, shape):
    return jnp.full(shape, flag.astype(jnp.int32)) == 1


def prep_kernel(heads, count, me_ref, q_ref, k_ref, v_ref, x_ref, g_ref, w_ref, coef_ref, rate_ref,
                wk_ref, qf_ref, small_ref, near_ref, far_ref, memory_ref, adjoint_ref,
                q_buf, k_buf, v_buf, x_buf, g_buf, w_buf, coef_buf, rate_buf, sems):
    length, width = x_ref.shape
    late = length - WINDOW
    copies = [
        pltpu.make_async_copy(source, target, sems.at[i])
        for i, (source, target) in enumerate(
            [
                (x_ref, x_buf), (w_ref, w_buf), (rate_ref, rate_buf), (k_ref, k_buf),
                (coef_ref, coef_buf), (q_ref, q_buf), (v_ref, v_buf), (g_ref, g_buf),
            ]
        )
    ]
    for copy in copies:
        copy.start()
    table = head_table(heads, width)
    lower = (iota((length, length), 1) <= iota((length, length), 0)).astype(BF16)
    copies[0].wait()
    copies[1].wait()
    x = x_buf[...]
    logits = sum(dot_nt(x, part) for part in split(w_buf[...], 2))
    decay_logit = logits[:, :heads]
    soft = jnp.maximum(decay_logit, 0.0) + jnp.log1p(jnp.exp(-jnp.abs(decay_logit)))
    slope = jax.nn.sigmoid(decay_logit)
    gamma = jax.nn.sigmoid(logits[:, heads:]) * (1.0 / WINDOW)
    copies[2].wait()
    total = mask_dot(lower, -rate_buf[...] * soft, 3)
    small_ref[...] = jnp.concatenate(
        [total, gamma, soft, slope, jnp.zeros((length, LANES - 4 * heads), F32)], axis=1
    )
    info = jnp.concatenate(
        [part.astype(F32) for part in split(total[:WINDOW], 3)]
        + [jnp.zeros((WINDOW, LANES - 3 * heads), F32)],
        axis=1,
    ).astype(BF16)
    copies[3].wait()
    copies[4].wait()
    coef = coef_buf[...]
    wk = (phi(k_buf[...].astype(F32), coef) * expand(gamma, table)).astype(BF16)
    wk_ref[...] = wk
    copies[5].wait()
    qf = phi(q_buf[...].astype(F32), coef).astype(BF16)
    qf_ref[...] = qf
    copies[6].wait()
    copies[7].wait()
    kept = mask_dot(window_own_t(length), jnp.exp(total[length - 1:] - total), 2)
    faded = jnp.exp(total[late:] - total[late - 1:late])
    scale = expand(jnp.concatenate([kept, faded], axis=0), table)
    carried = (wk.astype(F32) * scale[:length]).astype(BF16)
    faded = (g_buf[late:].astype(F32) * scale[length:]).astype(BF16)
    memory, adjoint = [], []
    for pair in range(width // LANES):
        at = slice(pair * LANES, (pair + 1) * LANES)
        memory.append(folded(dot_tn(carried[:, at], v_buf[:, at])))
        adjoint.append(folded(dot_tn(qf[late:, at], faded[:, at])))
    memory, adjoint = jnp.concatenate(memory, axis=1), jnp.concatenate(adjoint, axis=1)
    memory_ref[...] = memory
    adjoint_ref[...] = adjoint

    def pack(onward, back):
        onward[:WINDOW] = wk[late:]
        onward[WINDOW:2 * WINDOW] = v_buf[late:]
        back[:WINDOW] = qf[:WINDOW]
        back[WINDOW:2 * WINDOW] = g_buf[:WINDOW]
        onward[2 * WINDOW:2 * WINDOW + BAND] = jnp.zeros((BAND, width), BF16)
        back[2 * WINDOW:2 * WINDOW + BAND] = jnp.zeros((BAND, width), BF16)
        for step in range(WINDOW // BAND):
            band = info[step * BAND:(step + 1) * BAND]
            back[2 * WINDOW:2 * WINDOW + BAND, step * LANES:(step + 1) * LANES] = band

    odd = is_odd(me_ref)
    pl.when(odd)(lambda: pack(far_ref, near_ref))
    pl.when(jnp.logical_not(odd))(lambda: pack(near_ref, far_ref))
    near_ref[2 * WINDOW + BAND:] = jnp.where(everywhere(odd, memory.shape), adjoint, memory).astype(BF16)

    @pl.when((me_ref[0] == 0) | (me_ref[0] == count - 1))
    def _():
        far_ref[...] = jnp.zeros_like(far_ref)


def received(me_ref, near_ref, far_ref, fwd_ref, bwd_ref):
    odd = is_odd(me_ref)

    def keep(before, after):
        fwd_ref[...] = before[:2 * WINDOW + BAND]
        bwd_ref[...] = after[:2 * WINDOW + BAND]

    pl.when(odd)(lambda: keep(near_ref, far_ref))
    pl.when(jnp.logical_not(odd))(lambda: keep(far_ref, near_ref))


def next_decay(rim_ref, heads):
    info = jnp.concatenate(
        [
            rim_ref[2 * WINDOW:2 * WINDOW + BAND, step * LANES:(step + 1) * LANES]
            for step in range(WINDOW // BAND)
        ],
        axis=0,
    ).astype(F32)
    return info[:, :heads] + info[:, heads:2 * heads] + info[:, 2 * heads:3 * heads]


def join_kernel(heads, count, before_if_odd, me_ref, own_ref, edge_ref, small_ref, memory_ref, adjoint_ref, rim_ref,
                *rest):
    state_ref, part_ref, out_ref = rest if len(rest) == 3 else (None, *rest)
    width = rim_ref.shape[1]
    length = small_ref.shape[0]
    table = head_table(heads, width)
    total = small_ref[:, :heads]
    last = total[length - 1:]
    middle = total[length - WINDOW - 1:length - WINDOW]
    next_total = next_decay(rim_ref, heads)
    before = is_odd(me_ref) if before_if_odd else jnp.logical_not(is_odd(me_ref))
    kept = mask_dot(window_rim_t(), jnp.exp(middle - total[:WINDOW]), 2)
    scale = jnp.where(everywhere(before, kept.shape), kept, jnp.exp(next_total))
    fade = jnp.exp(last - middle)
    weight = jnp.where(
        everywhere(before, fade.shape), jnp.exp(last), fade * jnp.exp(next_total[WINDOW - 1:])
    )
    scale = expand(jnp.concatenate([scale, fade, weight], axis=0), table)
    scaled = (rim_ref[WINDOW:2 * WINDOW].astype(F32) * scale[:WINDOW]).astype(BF16)
    fade, weight = scale[WINDOW:WINDOW + 1], scale[WINDOW + 1:]
    if state_ref is None:
        state = rim_ref[2 * WINDOW + BAND:].astype(F32)
    else:
        edge = (me_ref[0] == 0) | (me_ref[0] == count - 1)
        state = jnp.where(everywhere(edge, state_ref.shape), 0.0, state_ref[...].astype(F32))
    base = jnp.where(everywhere(before, memory_ref.shape), memory_ref[...], adjoint_ref[...])
    base = base + weight * state
    for pair in range(width // LANES):
        at = slice(pair * LANES, (pair + 1) * LANES)
        part = folded(dot_tn(rim_ref[:WINDOW, at], scaled[:, at]))
        part_ref[:, at] = part
        out_ref[:, at] = (base[:, at] + fade[:, at] * part).astype(BF16)


def decays(column_pair, row_pair, keep):
    gap = jnp.where(keep, column_pair - row_pair, -1e30)
    return jnp.exp(gap)


def own_kernel(heads, me_ref, small_ref, wk_ref, qf_ref, v_ref, g_ref, dq_ref, dwk_ref, dv_ref, dl_ref):
    length, width = wk_ref.shape
    table = head_table(heads, width)
    masks = half_masks()
    small = small_ref[...]
    total = small[:, :heads]
    total_t = jnp.transpose(small)[:heads]
    keep = iota((length, length), 1) <= iota((length, length), 0)
    own = window_own(length).astype(F32)
    empty = jnp.zeros_like(own)
    windows = jnp.concatenate(
        [jnp.concatenate([own, empty], axis=1), jnp.concatenate([empty, own], axis=1)], axis=0
    ).astype(BF16)
    pairs = [slice(pair * LANES, (pair + 1) * LANES) for pair in range(width // LANES)]
    held = []
    for pair, at in enumerate(pairs):
        decay = jnp.concatenate(
            [decays(total[:, i:i + 1], total_t[i:i + 1], keep) for i in (2 * pair, 2 * pair + 1)], axis=1
        )
        kernel = dot(decay.astype(BF16), windows)
        scores = dot_nt(qf_ref[:, at], stacked(wk_ref[:, at], masks))
        lifted = dot_nt(g_ref[:, at], stacked(v_ref[:, at], masks))
        held.append(
            (
                decay,
                (scores * kernel).astype(BF16),
                (lifted * kernel).astype(BF16),
                (lifted * scores).astype(BF16),
            )
        )
    columns = []
    products = []
    for (decay, weights, d_scores, d_kernel), at in zip(held, pairs):
        q, g = qf_ref[:, at], g_ref[:, at]
        products.append(dot(weights, stacked(v_ref[:, at], masks)) * g.astype(F32))
        dq_ref[:, at] = dot(d_scores, stacked(wk_ref[:, at], masks))
        dwk_ref[:, at] = dot_tn(one_above(d_scores), stacked(q, masks))
        dv_ref[:, at] = dot_tn(one_above(weights), stacked(g, masks))
        column = jnp.sum(dot_nt(d_kernel, windows) * decay, axis=0, keepdims=True)
        columns += [column[:, :length], column[:, length:]]
    column = jnp.concatenate(columns + [jnp.zeros((LANES - heads, length), F32)], axis=0)
    rows = head_sum(jnp.concatenate(products, axis=1), table)
    dl_ref[...] = rows - jnp.transpose(column)[:, :heads]


def edge_decay(total, heads):
    lane = iota((WINDOW, LANES), 1)
    first = lane < LANES // 2
    keep = jnp.where(first, lane, lane - LANES // 2) <= iota((WINDOW, LANES), 0)
    doubled = jnp.concatenate([total, total], axis=0)
    doubled = jnp.concatenate([doubled, jnp.zeros((2 * WINDOW, LANES - heads), F32)], axis=1)
    rows = jnp.transpose(doubled)[:heads]
    return lambda h: decays(
        jnp.where(first, total[:, h:h + 1], total[:, h + 1:h + 2]),
        jnp.where(first, rows[h:h + 1], rows[h + 1:h + 2]),
        keep,
    )


def scales_of(heads, small_ref, scales_ref):
    length = small_ref.shape[0]
    late = length - WINDOW
    total, gamma = small_ref[:, :heads], small_ref[:, heads:2 * heads]
    last, middle = total[length - 1:], total[late - 1:late]
    own = mask_dot(window_own_t(length), jnp.exp(last - total), 2)
    grown = jnp.exp(jnp.concatenate([total[:late], total[late:] - middle], axis=0))
    rest = [jnp.exp(middle), jnp.exp(last - middle), jnp.zeros((BAND - 2, heads), F32)]
    scales = jnp.concatenate([own, grown, gamma] + rest, axis=0)
    scales_ref[...] = expand(scales, head_table(heads, scales_ref.shape[1]))


def edge_kernel(heads, before_if_odd, me_ref, small_ref, wk_ref, qf_ref, v_ref, g_ref, rim_ref,
                first_ref, second_ref, dl_ref, *rest):
    length, width = wk_ref.shape
    late = length - WINDOW
    table = head_table(heads, width)
    masks = half_masks()
    pairs = [slice(pair * LANES, (pair + 1) * LANES) for pair in range(width // LANES)]
    cell = (iota((LANES, LANES), 0), iota((LANES, LANES), 1))
    same = (cell[0] < WINDOW) == (cell[1] < WINDOW)
    windows = (same & (cell[0] < cell[1])).astype(BF16)
    before = is_odd(me_ref) if before_if_odd else jnp.logical_not(is_odd(me_ref))
    if rest:
        scales_of(heads, small_ref, rest[0])

    @pl.when(before)
    def _():
        decay_at = edge_decay(small_ref[:WINDOW, :heads], heads)
        held = []
        for pair, at in enumerate(pairs):
            keys, values = stacked(rim_ref[:WINDOW, at], masks), stacked(rim_ref[WINDOW:2 * WINDOW, at], masks)
            decay = decay_at(2 * pair)
            kernel = dot(decay.astype(BF16), windows)
            scores = dot_nt(qf_ref[:WINDOW, at], keys)
            lifted = dot_nt(g_ref[:WINDOW, at], values)
            held.append(
                (
                    keys,
                    values,
                    decay,
                    (scores * kernel).astype(BF16),
                    (lifted * kernel).astype(BF16),
                    (lifted * scores).astype(BF16),
                )
            )
        columns, products = [], []
        for (keys, values, decay, weights, d_scores, d_kernel), at in zip(held, pairs):
            products.append(dot(weights, values) * g_ref[:WINDOW, at].astype(F32))
            first_ref[:, at] = dot(d_scores, keys)
            column = jnp.sum(dot_nt(d_kernel, windows) * decay, axis=0, keepdims=True)
            columns += [column[:, :WINDOW], column[:, WINDOW:]]
        column = jnp.concatenate(columns + [jnp.zeros((LANES - heads, WINDOW), F32)], axis=0)
        column = jnp.concatenate([column, jnp.zeros((LANES, LANES - WINDOW), F32)], axis=1)
        rows = head_sum(jnp.concatenate(products, axis=1), table)
        dl_ref[...] = rows - jnp.transpose(column)[:WINDOW, :heads]

    @pl.when(jnp.logical_not(before))
    def _():
        decay_at = edge_decay(next_decay(rim_ref, heads), heads)
        held = []
        for pair, at in enumerate(pairs):
            q, g = rim_ref[:WINDOW, at], rim_ref[WINDOW:2 * WINDOW, at]
            keys, values = stacked(wk_ref[late:, at], masks), stacked(v_ref[late:, at], masks)
            kernel = dot(decay_at(2 * pair).astype(BF16), windows)
            held.append(
                (q, g, (dot_nt(q, keys) * kernel).astype(BF16), (dot_nt(g, values) * kernel).astype(BF16))
            )
        for (q, g, weights, d_scores), at in zip(held, pairs):
            first_ref[:, at] = dot_tn(one_above(d_scores), stacked(q, masks))
            second_ref[:, at] = dot_tn(one_above(weights), stacked(g, masks))


def finish_kernel(heads, count, me_ref, q_ref, k_ref, x_ref, v_ref, g_ref, coef_ref, rate_ref,
                  small_ref, wk_ref, qf_ref, near_ref, far_ref, adjoint_ref,
                  dqf_ref, dwk_ref, dvl_ref, dl_ref, scales_ref,
                  near_first_ref, near_second_ref, near_dl_ref, far_first_ref, far_second_ref, far_dl_ref,
                  near_part_ref, far_part_ref, cross_ref, passed_ref,
                  dq_out, dk_out, dv_out, logits_ref, sums_ref,
                  fwd_ref, bwd_ref, rim_dq_ref, rim_dwk_ref, rim_dv_ref, rim_dl_ref,
                  dq_ref, dk_ref, dv_ref, sems):
    length, width = wk_ref.shape
    late = length - WINDOW
    pairs = width // LANES
    received(me_ref, near_ref, far_ref, fwd_ref, bwd_ref)

    def edges(dq, dl, dwk, dv):
        rim_dq_ref[...], rim_dl_ref[...] = dq[...], dl[...]
        rim_dwk_ref[...], rim_dv_ref[...] = dwk[...], dv[...]

    far_edge = (far_first_ref, far_dl_ref, near_first_ref, near_second_ref)
    near_edge = (near_first_ref, near_dl_ref, far_first_ref, far_second_ref)
    pl.when(is_odd(me_ref))(lambda: edges(*near_edge))
    pl.when(jnp.logical_not(is_odd(me_ref)))(lambda: edges(*far_edge))
    table = head_table(heads, width)
    small = small_ref[...]
    total, gamma, soft, slope = (small[:, i * heads:(i + 1) * heads] for i in range(4))
    last, middle = total[length - 1:], total[late - 1:late]
    tail = jnp.exp(last - total)
    own = mask_dot(window_own_t(length), tail, 2)
    next_total = next_decay(bwd_ref, heads)
    next_middle = next_total[WINDOW - 1:]
    onward = mask_dot(window_rim_t(), jnp.exp(next_middle - next_total), 2)
    grown = jnp.exp(jnp.concatenate([total[:late], total[late:] - middle], axis=0))
    fade = jnp.exp(last - middle)
    onward_x = expand(jnp.concatenate([onward, jnp.exp(next_middle)], axis=0), table)
    onward_x, next_x = onward_x[:WINDOW], onward_x[WINDOW:]
    own_x, grown_x, gamma_x = (scales_ref.at[i * length:(i + 1) * length] for i in range(3))
    middle_x, fade_x = (scales_ref[i:i + 1] for i in range(3 * length, 3 * length + 2))

    me = me_ref[0]
    shape = (WINDOW, width)
    odd = everywhere(is_odd(me_ref), shape)
    edge = everywhere((me == 0) | (me == count - 1), shape)
    cross = jnp.where(edge, 0.0, cross_ref[...].astype(F32))
    passed = passed_ref[...].astype(F32)
    near_part, far_part = near_part_ref[...], far_part_ref[...]
    start = jnp.where(odd, passed, cross)
    later = jnp.where(odd, cross, passed)
    after = jnp.where(odd, far_part, near_part) + next_x * later
    halfway = middle_x * start + jnp.where(odd, near_part, far_part)
    half_after = adjoint_ref[...] + fade_x * after
    d_state = jnp.sum(head_sum(after * halfway, table, 2), axis=0, keepdims=True)
    start, later, after, halfway, half_after = (
        z.astype(BF16) for z in (start, later, after, halfway, half_after)
    )

    own_products, rim_products, out_products, key_products, d_coef = [], [], [], [], []
    coef = coef_ref[...]
    for group in range(pairs // 2):
        at = slice(2 * group * LANES, 2 * (group + 1) * LANES)
        m0, m1, a1, a0, b0 = (stacked_group(z[:, at]) for z in (start, halfway, after, half_after, later))
        qf, g, wk, v = qf_ref[:, at], g_ref[:, at], wk_ref[:, at], v_ref[:, at]
        from_q = jnp.concatenate([dot(qf[:late], m0), dot(qf[late:], m1)], axis=0)
        out_products.append(from_q * g.astype(F32))
        from_g = jnp.concatenate([dot_nt(g[:late], m0), dot_nt(g[late:], m1)], axis=0)
        dqf = dqf_ref[:, at] + grown_x[:, at] * from_g
        dqf = jnp.concatenate([dqf[:late] + rim_dq_ref[:, at], dqf[late:]], axis=0)
        from_keys = dot(wk, a1)
        own_products.append(from_keys * v.astype(F32))
        rim_products.append(dot(fwd_ref[:WINDOW, at], a0) * fwd_ref[WINDOW:2 * WINDOW, at].astype(F32))
        dwk = dwk_ref[:, at] + own_x[:, at] * dot_nt(v, a1)
        dv = dvl_ref[:, at] + own_x[:, at] * from_keys
        dwk = jnp.concatenate(
            [dwk[:late], dwk[late:] + rim_dwk_ref[:, at] + onward_x[:, at] * dot_nt(v[late:], b0)], axis=0
        )
        dv_ref[:late, at] = dv[:late].astype(BF16)
        dv_ref[late:, at] = (
            dv[late:] + rim_dv_ref[:, at] + onward_x[:, at] * dot(wk[late:], b0)
        ).astype(BF16)
        q, k = q_ref[:, at].astype(F32), k_ref[:, at].astype(F32)
        c = coef[:, at]
        key_products.append(dwk * phi(k, c))
        d_phi = dwk * gamma_x[:, at]
        dq_ref[:, at] = (dqf * (0.125 + 0.25 * c * q)).astype(BF16)
        dk_ref[:, at] = (d_phi * (0.125 + 0.25 * c * k)).astype(BF16)
        row = jnp.sum(dqf * (0.125 * q * q) + d_phi * (0.125 * k * k), axis=0, keepdims=True)
        d_coef += [row[:, :LANES], row[:, LANES:]]

    copies = [
        pltpu.make_async_copy(source, target, sems.at[i])
        for i, (source, target) in enumerate([(dq_ref, dq_out), (dk_ref, dk_out), (dv_ref, dv_out)])
    ]
    for copy in copies:
        copy.start()
    sums = jnp.concatenate(
        [
            jnp.concatenate(z, axis=1).astype(BF16)
            for z in (own_products, out_products, key_products, rim_products)
        ],
        axis=0,
    )
    sums = dot_nt(sums, table)
    d_own, d_out, d_gamma = (sums[i * length:(i + 1) * length] for i in range(3))
    d_rim = sums[3 * length:]
    d_tail = tail * mask_dot(window_own(length), d_own, 2)
    rim_tail = jnp.exp(middle - total[:late]) * mask_dot(window_rim(), d_rim, 2)
    at_end = jnp.sum(own * d_own, axis=0, keepdims=True) + fade * d_state
    d_total = dl_ref[...] + grown * d_out - d_tail
    d_total = jnp.concatenate([d_total[:late] + rim_dl_ref[...] - rim_tail, d_total[late:]], axis=0)
    d_total = d_total + jnp.where(iota((length, heads), 0) == length - 1, at_end, 0.0)
    upper = (iota((length, length), 1) >= iota((length, length), 0)).astype(BF16)
    d_decay = mask_dot(upper, d_total, 3)
    d_rate = -jnp.sum(d_decay * soft, axis=0, keepdims=True)
    d_logits = jnp.concatenate(
        [-rate_ref[...] * d_decay * slope, d_gamma * gamma * (1.0 - WINDOW * gamma)], axis=1
    )
    logits_ref[...] = d_logits
    gate = dot_tn(d_logits.astype(BF16), x_ref[...])
    d_rate = jnp.concatenate([d_rate, jnp.zeros((1, LANES - heads), F32)], axis=1)
    for i in range(pairs):
        sums_ref[i * 2 * heads:(i + 1) * 2 * heads] = gate[:, i * LANES:(i + 1) * LANES].astype(BF16)
    rest = d_coef + [d_rate, jnp.zeros((BAND - 1 - pairs, LANES), F32)]
    sums_ref[pairs * 2 * heads:] = jnp.concatenate(rest, axis=0).astype(BF16)
    for copy in copies:
        copy.wait()


def inputs_kernel(me_ref, logits_ref, w_ref, dx_ref):
    high, low = (part.astype(F32) for part in split(logits_ref[...], 2))
    w_high, w_low = split(w_ref[...], 2)
    dx_ref[...] = dot(
        jnp.concatenate([high, low, high], axis=1).astype(BF16),
        jnp.concatenate([w_high, w_high, w_low], axis=0),
    ).astype(BF16)


def last_kernel(heads, me_ref, mine_ref, theirs_ref, gate_ref, coef_ref, rate_ref):
    blocks = gate_ref.shape[1] // LANES

    def write(sums_ref):
        for i in range(blocks):
            at = slice(i * LANES, (i + 1) * LANES)
            gate_ref[:, at] = sums_ref[i * 2 * heads:(i + 1) * 2 * heads]
            coef_ref[:, at] = sums_ref[blocks * 2 * heads + i:blocks * 2 * heads + i + 1]
        at = blocks * (2 * heads + 1)
        rate_ref[...] = sums_ref[at:at + 1, :heads]

    pl.when(is_odd(me_ref))(lambda: write(mine_ref))
    pl.when(jnp.logical_not(is_odd(me_ref)))(lambda: write(theirs_ref))


def call(kernel, outs, operands, name, scratch=(), in_place=(), outside=(), flops=10**8, moved=3 * 10**6):
    specs = [pl.BlockSpec(memory_space=pltpu.SMEM)]
    specs += [
        pl.BlockSpec(memory_space=pltpu.HBM if i in in_place else pltpu.VMEM)
        for i in range(1, len(operands))
    ]
    operands = [
        pltpu.with_memory_space_constraint(z, pltpu.HBM) if i in in_place else z
        for i, z in enumerate(operands)
    ]
    return pl.pallas_call(
        kernel,
        out_shape=tuple(jax.ShapeDtypeStruct(*out) for out in outs),
        in_specs=specs,
        out_specs=tuple(
            pl.BlockSpec(memory_space=pltpu.HBM if i in outside else pltpu.VMEM) for i in range(len(outs))
        ),
        scratch_shapes=list(scratch),
        compiler_params=pltpu.CompilerParams(vmem_limit_bytes=32 * 2**20),
        cost_estimate=pl.CostEstimate(flops=flops, bytes_accessed=moved, transcendentals=10**6),
        name=name,
    )(*operands)


EVERYONE = ("dp", "seq")


def swapped(value, axis, distance):
    return lax.ppermute(value, axis, [(i, i ^ distance) for i in range(lax.axis_size(axis))])


def odd_swapped(value, distance, stage):
    count = lax.axis_size(EVERYONE)
    idle = 8 if stage == 2 and count > 8 else 4
    return lax.ppermute(value, EVERYONE, [(i, i ^ (distance if i % 2 else idle)) for i in range(count)])


def inner_swapped(value):
    dp, seq = (lax.axis_size(axis) for axis in EVERYONE)
    pairs = []
    for i in range(dp):
        for j in range(seq):
            inner = 0 < j < seq - 1
            pairs.append((i * seq + j, i * seq + seq - 1 - j if inner else (i ^ 1) * seq + j))
    return lax.ppermute(value, EVERYONE, pairs)


def on_device(queries, key_rows, value_rows, inputs, w_gate, poly_coef, decay_rate, cotangent):
    q, k, v, x, g = (z[0] for z in (queries, key_rows, value_rows, inputs, cotangent))
    length, width = x.shape
    heads = decay_rate.shape[0]
    count = lax.axis_size("seq")
    assert count == 4 and length == 2 * WINDOW
    me = lax.axis_index("seq").astype(jnp.int32).reshape(1)
    wide, small = ((length, width), BF16), ((length, LANES), F32)
    full, half, gain = ((length, width), F32), ((WINDOW, width), F32), ((length, heads), F32)
    rim, sent = ((2 * WINDOW + BAND, width), BF16), ((WINDOW, width), BF16)
    wk, qf, gates, near, far, memory, adjoint, q, k, v, x, g, wt, coef, rate = call(
        functools.partial(prep_kernel, heads, count),
        [wide, wide, small, ((3 * WINDOW + BAND, width), BF16), rim, half, half]
        + [wide] * 5
        + [((2 * heads, width), F32), ((1, width), F32), ((1, heads), F32)],
        (me, q, k, v, x, g, w_gate.T, poly_coef.reshape(1, width), decay_rate.reshape(1, heads)),
        "prep",
        scratch=[pltpu.SemaphoreType.DMA((8,))],
        in_place=range(1, 9),
    )
    near = swapped(near, "seq", 1)
    far = inner_swapped(far)
    near_part, cross = call(
        functools.partial(join_kernel, heads, count, True),
        [half, sent],
        (me, gates, gates, gates, memory, adjoint, near),
        "join_near",
    )
    cross = inner_swapped(cross)
    own = call(
        functools.partial(own_kernel, heads),
        [full, full, full, gain],
        (me, gates, wk, qf, v, g),
        "own",
        flops=7 * 10**8,
        moved=7 * 10**6,
    )
    edge = [half, half, ((WINDOW, heads), F32)]
    *near_edge, scales = call(
        functools.partial(edge_kernel, heads, True),
        edge + [((3 * length + BAND, width), F32)],
        (me, gates, wk, qf, v, g, near),
        "edge_near",
        flops=2 * 10**8,
        moved=5 * 10**6,
    )
    far_part, passed = call(
        functools.partial(join_kernel, heads, count, False),
        [half, sent],
        (me, own[3], near_edge[2], gates, memory, adjoint, far, cross),
        "join_far",
    )
    passed = swapped(passed, "seq", 1)
    far_edge = call(
        functools.partial(edge_kernel, heads, False),
        edge,
        (me, gates, wk, qf, v, g, far),
        "edge_far",
        flops=2 * 10**8,
        moved=3 * 10**6,
    )
    all_sums = ((width // LANES * 2 * heads + BAND, LANES), BF16)
    dq, dk, dv, d_logits, sums = call(
        functools.partial(finish_kernel, heads, count),
        [wide, wide, wide, ((length, 2 * heads), F32), all_sums],
        (me, q, k, x, v, g, coef, rate, gates, wk, qf, near, far, adjoint, *own, scales, *near_edge, *far_edge,
         near_part, far_part, cross, passed),
        "finish",
        scratch=[pltpu.VMEM(*z) for z in (rim, rim, half, half, half, edge[2], wide, wide, wide)]
        + [pltpu.SemaphoreType.DMA((3,))],
        outside=range(3),
    )
    dx = call(inputs_kernel, [wide], (me, d_logits, wt), "inputs")[0]
    sums = sums.astype(F32) + swapped(sums, EVERYONE, 1).astype(F32)
    distance = 2
    while distance < lax.axis_size(EVERYONE):
        sums = sums.astype(BF16)
        if 2 * distance < lax.axis_size(EVERYONE):
            far, mid, one = (odd_swapped(sums, i * distance, distance).astype(F32) for i in (3, 2, 1))
            sums = (sums.astype(F32) + one) + (mid + far)
        else:
            sums = sums.astype(F32) + odd_swapped(sums, distance, distance).astype(F32)
        if distance == 2:
            sums, dx = lax.optimization_barrier((sums, dx))
        distance *= 4
    gate, d_coef, d_rate = call(
        functools.partial(last_kernel, heads),
        [((2 * heads, width), F32), ((1, width), F32), ((1, heads), F32)],
        (me, sums, swapped(sums, "seq", 1)),
        "last",
    )
    return (dq[None], dk[None], dv[None], dx[None], gate.T, d_coef.reshape(width), d_rate.reshape(heads))


def solution(mesh):
    rows = P("dp", "seq", None)
    return jax.shard_map(
        on_device,
        mesh=mesh,
        in_specs=(rows, rows, rows, rows, P(), P(), P(), rows),
        out_specs=(rows, rows, rows, rows, P(), P(), P()),
        check_vma=False,
    )
```

```python
import functools

import jax
import jax.numpy as jnp
from jax import lax
from jax.experimental import pallas as pl
from jax.experimental.pallas import tpu as pltpu
from jax.sharding import PartitionSpec as P

WINDOW = 64
LANES = 128
BAND = 16
F32 = jnp.float32
BF16 = jnp.bfloat16


def iota(shape, dim):
    return lax.broadcasted_iota(jnp.int32, shape, dim)


def split(z, count):
    parts = []
    for _ in range(count):
        high = z.astype(BF16)
        parts.append(high)
        z = z - high.astype(F32)
    return parts


def dot(a, b):
    return lax.dot_general(a, b, (((1,), (0,)), ((), ())), preferred_element_type=F32)


def dot_nt(a, b):
    return lax.dot_general(a, b, (((1,), (1,)), ((), ())), preferred_element_type=F32)


def dot_tn(a, b):
    return lax.dot_general(a, b, (((0,), (0,)), ((), ())), preferred_element_type=F32)


def mask_dot(mask, z, count):
    return sum(dot(mask, part) for part in split(z, count))


def head_table(heads, width):
    per_head = width // heads
    return (iota((heads, width), 1) // per_head == iota((heads, width), 0)).astype(BF16)


def expand(z, table, count=1):
    return sum(dot(part, table) for part in split(z, count))


def head_sum(z, table, count=1):
    return sum(dot_nt(part, table) for part in split(z, count))


def half_masks():
    lane = iota((1, LANES), 1)
    return (lane < LANES // 2).astype(BF16), (lane >= LANES // 2).astype(BF16)


def stacked(z, masks):
    return jnp.concatenate([z * masks[0], z * masks[1]], axis=0)


def one_above(z):
    columns = z.shape[1] // 2
    return jnp.concatenate([z[:, :columns], z[:, columns:]], axis=0)


def folded(z):
    rows = z.shape[0] // 2
    return jnp.where(iota((rows, LANES), 1) < LANES // 2, z[:rows], z[rows:])


def window_own(length):
    gap = iota((length, length), 0) - iota((length, length), 1)
    return ((gap >= 0) & (gap < WINDOW)).astype(BF16)


def window_own_t(length):
    gap = iota((length, length), 1) - iota((length, length), 0)
    return ((gap >= 0) & (gap < WINDOW)).astype(BF16)


def window_rim():
    return (iota((WINDOW, WINDOW), 0) < iota((WINDOW, WINDOW), 1)).astype(BF16)


def window_rim_t():
    return (iota((WINDOW, WINDOW), 1) < iota((WINDOW, WINDOW), 0)).astype(BF16)


def phi(raw, coef):
    return 0.125 * (raw + coef * raw * raw)


def is_odd(me_ref):
    return jax.lax.rem(me_ref[0], 2) == 1


def everywhere(flag, shape):
    return jnp.full(shape, flag.astype(jnp.int32)) == 1


def prep_kernel(heads, count, me_ref, q_ref, k_ref, v_ref, x_ref, g_ref, w_ref, coef_ref, rate_ref,
                wk_ref, qf_ref, small_ref, near_ref, far_ref, memory_ref, adjoint_ref,
                q_buf, k_buf, v_buf, x_buf, g_buf, w_buf, coef_buf, rate_buf, sems):
    length, width = x_ref.shape
    late = length - WINDOW
    copies = [
        pltpu.make_async_copy(source, target, sems.at[i])
        for i, (source, target) in enumerate(
            [
                (x_ref, x_buf), (w_ref, w_buf), (rate_ref, rate_buf), (k_ref, k_buf),
                (coef_ref, coef_buf), (q_ref, q_buf), (v_ref, v_buf), (g_ref, g_buf),
            ]
        )
    ]
    for copy in copies:
        copy.start()
    table = head_table(heads, width)
    lower = (iota((length, length), 1) <= iota((length, length), 0)).astype(BF16)
    copies[0].wait()
    copies[1].wait()
    x = x_buf[...]
    logits = sum(dot_nt(x, part) for part in split(w_buf[...], 2))
    decay_logit = logits[:, :heads]
    soft = jnp.maximum(decay_logit, 0.0) + jnp.log1p(jnp.exp(-jnp.abs(decay_logit)))
    slope = jax.nn.sigmoid(decay_logit)
    gamma = jax.nn.sigmoid(logits[:, heads:]) * (1.0 / WINDOW)
    copies[2].wait()
    total = mask_dot(lower, -rate_buf[...] * soft, 3)
    small_ref[...] = jnp.concatenate(
        [total, gamma, soft, slope, jnp.zeros((length, LANES - 4 * heads), F32)], axis=1
    )
    info = jnp.concatenate(
        [part.astype(F32) for part in split(total[:WINDOW], 3)]
        + [jnp.zeros((WINDOW, LANES - 3 * heads), F32)],
        axis=1,
    ).astype(BF16)
    copies[3].wait()
    copies[4].wait()
    coef = coef_buf[...]
    wk = (phi(k_buf[...].astype(F32), coef) * expand(gamma, table)).astype(BF16)
    wk_ref[...] = wk
    copies[5].wait()
    qf = phi(q_buf[...].astype(F32), coef).astype(BF16)
    qf_ref[...] = qf
    copies[6].wait()
    copies[7].wait()
    kept = mask_dot(window_own_t(length), jnp.exp(total[length - 1:] - total), 2)
    faded = jnp.exp(total[late:] - total[late - 1:late])
    scale = expand(jnp.concatenate([kept, faded], axis=0), table)
    carried = (wk.astype(F32) * scale[:length]).astype(BF16)
    faded = (g_buf[late:].astype(F32) * scale[length:]).astype(BF16)
    memory, adjoint = [], []
    for pair in range(width // LANES):
        at = slice(pair * LANES, (pair + 1) * LANES)
        memory.append(folded(dot_tn(carried[:, at], v_buf[:, at])))
        adjoint.append(folded(dot_tn(qf[late:, at], faded[:, at])))
    memory, adjoint = jnp.concatenate(memory, axis=1), jnp.concatenate(adjoint, axis=1)
    memory_ref[...] = memory
    adjoint_ref[...] = adjoint

    def pack(onward, back):
        onward[:WINDOW] = wk[late:]
        onward[WINDOW:2 * WINDOW] = v_buf[late:]
        back[:WINDOW] = qf[:WINDOW]
        back[WINDOW:2 * WINDOW] = g_buf[:WINDOW]
        onward[2 * WINDOW:2 * WINDOW + BAND] = jnp.zeros((BAND, width), BF16)
        back[2 * WINDOW:2 * WINDOW + BAND] = jnp.zeros((BAND, width), BF16)
        for step in range(WINDOW // BAND):
            band = info[step * BAND:(step + 1) * BAND]
            back[2 * WINDOW:2 * WINDOW + BAND, step * LANES:(step + 1) * LANES] = band

    odd = is_odd(me_ref)
    pl.when(odd)(lambda: pack(far_ref, near_ref))
    pl.when(jnp.logical_not(odd))(lambda: pack(near_ref, far_ref))
    near_ref[2 * WINDOW + BAND:] = jnp.where(everywhere(odd, memory.shape), adjoint, memory).astype(BF16)

    @pl.when((me_ref[0] == 0) | (me_ref[0] == count - 1))
    def _():
        far_ref[...] = jnp.zeros_like(far_ref)


def received(me_ref, near_ref, far_ref, fwd_ref, bwd_ref):
    odd = is_odd(me_ref)

    def keep(before, after):
        fwd_ref[...] = before[:2 * WINDOW + BAND]
        bwd_ref[...] = after[:2 * WINDOW + BAND]

    pl.when(odd)(lambda: keep(near_ref, far_ref))
    pl.when(jnp.logical_not(odd))(lambda: keep(far_ref, near_ref))


def next_decay(rim_ref, heads):
    info = jnp.concatenate(
        [
            rim_ref[2 * WINDOW:2 * WINDOW + BAND, step * LANES:(step + 1) * LANES]
            for step in range(WINDOW // BAND)
        ],
        axis=0,
    ).astype(F32)
    return info[:, :heads] + info[:, heads:2 * heads] + info[:, 2 * heads:3 * heads]


def join_kernel(heads, count, before_if_odd, me_ref, own_ref, edge_ref, small_ref, memory_ref, adjoint_ref, rim_ref,
                *rest):
    part_ref, out_ref, weight_ref = rest if len(rest) == 3 else (*rest, None)
    width = rim_ref.shape[1]
    length = small_ref.shape[0]
    table = head_table(heads, width)
    total = small_ref[:, :heads]
    last = total[length - 1:]
    middle = total[length - WINDOW - 1:length - WINDOW]
    next_total = next_decay(rim_ref, heads)
    before = is_odd(me_ref) if before_if_odd else jnp.logical_not(is_odd(me_ref))
    kept = mask_dot(window_rim_t(), jnp.exp(middle - total[:WINDOW]), 2)
    scale = jnp.where(everywhere(before, kept.shape), kept, jnp.exp(next_total))
    fade = jnp.exp(last - middle)
    weight = jnp.where(
        everywhere(before, fade.shape), jnp.exp(last), fade * jnp.exp(next_total[WINDOW - 1:])
    )
    scale = expand(jnp.concatenate([scale, fade, weight], axis=0), table)
    scaled = (rim_ref[WINDOW:2 * WINDOW].astype(F32) * scale[:WINDOW]).astype(BF16)
    fade, weight = scale[WINDOW:WINDOW + 1], scale[WINDOW + 1:]
    base = jnp.where(everywhere(before, memory_ref.shape), memory_ref[...], adjoint_ref[...])
    if weight_ref is None:
        base = base + weight * rim_ref[2 * WINDOW + BAND:].astype(F32)
    else:
        edge = (me_ref[0] == 0) | (me_ref[0] == count - 1)
        weight_ref[...] = jnp.where(everywhere(edge, weight.shape), 0.0, weight)
    for pair in range(width // LANES):
        at = slice(pair * LANES, (pair + 1) * LANES)
        part = folded(dot_tn(rim_ref[:WINDOW, at], scaled[:, at]))
        part_ref[:, at] = part
        out_ref[:, at] = (base[:, at] + fade[:, at] * part).astype(out_ref.dtype)


def pass_kernel(me_ref, base_ref, weight_ref, state_ref, out_ref):
    out_ref[...] = (base_ref[...] + weight_ref[...] * state_ref[...].astype(F32)).astype(BF16)


def decays(column_pair, row_pair, keep):
    gap = jnp.where(keep, column_pair - row_pair, -1e30)
    return jnp.exp(gap)


def own_kernel(heads, me_ref, small_ref, wk_ref, qf_ref, v_ref, g_ref, dq_ref, dwk_ref, dv_ref, dl_ref):
    length, width = wk_ref.shape
    table = head_table(heads, width)
    masks = half_masks()
    small = small_ref[...]
    total = small[:, :heads]
    total_t = jnp.transpose(small)[:heads]
    keep = iota((length, length), 1) <= iota((length, length), 0)
    own = window_own(length).astype(F32)
    empty = jnp.zeros_like(own)
    windows = jnp.concatenate(
        [jnp.concatenate([own, empty], axis=1), jnp.concatenate([empty, own], axis=1)], axis=0
    ).astype(BF16)
    pairs = [slice(pair * LANES, (pair + 1) * LANES) for pair in range(width // LANES)]
    held = []
    for pair, at in enumerate(pairs):
        decay = jnp.concatenate(
            [decays(total[:, i:i + 1], total_t[i:i + 1], keep) for i in (2 * pair, 2 * pair + 1)], axis=1
        )
        kernel = dot(decay.astype(BF16), windows)
        scores = dot_nt(qf_ref[:, at], stacked(wk_ref[:, at], masks))
        lifted = dot_nt(g_ref[:, at], stacked(v_ref[:, at], masks))
        held.append(
            (
                decay,
                (scores * kernel).astype(BF16),
                (lifted * kernel).astype(BF16),
                (lifted * scores).astype(BF16),
            )
        )
    columns = []
    products = []
    for (decay, weights, d_scores, d_kernel), at in zip(held, pairs):
        q, g = qf_ref[:, at], g_ref[:, at]
        products.append(dot(weights, stacked(v_ref[:, at], masks)) * g.astype(F32))
        dq_ref[:, at] = dot(d_scores, stacked(wk_ref[:, at], masks))
        dwk_ref[:, at] = dot_tn(one_above(d_scores), stacked(q, masks))
        dv_ref[:, at] = dot_tn(one_above(weights), stacked(g, masks))
        column = jnp.sum(dot_nt(d_kernel, windows) * decay, axis=0, keepdims=True)
        columns += [column[:, :length], column[:, length:]]
    column = jnp.concatenate(columns + [jnp.zeros((LANES - heads, length), F32)], axis=0)
    rows = head_sum(jnp.concatenate(products, axis=1), table)
    dl_ref[...] = rows - jnp.transpose(column)[:, :heads]


def edge_decay(total, heads):
    lane = iota((WINDOW, LANES), 1)
    first = lane < LANES // 2
    keep = jnp.where(first, lane, lane - LANES // 2) <= iota((WINDOW, LANES), 0)
    doubled = jnp.concatenate([total, total], axis=0)
    doubled = jnp.concatenate([doubled, jnp.zeros((2 * WINDOW, LANES - heads), F32)], axis=1)
    rows = jnp.transpose(doubled)[:heads]
    return lambda h: decays(
        jnp.where(first, total[:, h:h + 1], total[:, h + 1:h + 2]),
        jnp.where(first, rows[h:h + 1], rows[h + 1:h + 2]),
        keep,
    )


def scales_of(heads, small_ref, scales_ref):
    length = small_ref.shape[0]
    late = length - WINDOW
    total, gamma = small_ref[:, :heads], small_ref[:, heads:2 * heads]
    last, middle = total[length - 1:], total[late - 1:late]
    own = mask_dot(window_own_t(length), jnp.exp(last - total), 2)
    grown = jnp.exp(jnp.concatenate([total[:late], total[late:] - middle], axis=0))
    rest = [jnp.exp(middle), jnp.exp(last - middle), jnp.zeros((BAND - 2, heads), F32)]
    scales = jnp.concatenate([own, grown, gamma] + rest, axis=0)
    scales_ref[...] = expand(scales, head_table(heads, scales_ref.shape[1]))


def edge_kernel(heads, before_if_odd, me_ref, small_ref, wk_ref, qf_ref, v_ref, g_ref, rim_ref,
                first_ref, second_ref, dl_ref, *rest):
    length, width = wk_ref.shape
    late = length - WINDOW
    table = head_table(heads, width)
    masks = half_masks()
    pairs = [slice(pair * LANES, (pair + 1) * LANES) for pair in range(width // LANES)]
    cell = (iota((LANES, LANES), 0), iota((LANES, LANES), 1))
    same = (cell[0] < WINDOW) == (cell[1] < WINDOW)
    windows = (same & (cell[0] < cell[1])).astype(BF16)
    before = is_odd(me_ref) if before_if_odd else jnp.logical_not(is_odd(me_ref))
    if rest:
        scales_of(heads, small_ref, rest[0])

    @pl.when(before)
    def _():
        decay_at = edge_decay(small_ref[:WINDOW, :heads], heads)
        held = []
        for pair, at in enumerate(pairs):
            keys, values = stacked(rim_ref[:WINDOW, at], masks), stacked(rim_ref[WINDOW:2 * WINDOW, at], masks)
            decay = decay_at(2 * pair)
            kernel = dot(decay.astype(BF16), windows)
            scores = dot_nt(qf_ref[:WINDOW, at], keys)
            lifted = dot_nt(g_ref[:WINDOW, at], values)
            held.append(
                (
                    keys,
                    values,
                    decay,
                    (scores * kernel).astype(BF16),
                    (lifted * kernel).astype(BF16),
                    (lifted * scores).astype(BF16),
                )
            )
        columns, products = [], []
        for (keys, values, decay, weights, d_scores, d_kernel), at in zip(held, pairs):
            products.append(dot(weights, values) * g_ref[:WINDOW, at].astype(F32))
            first_ref[:, at] = dot(d_scores, keys)
            column = jnp.sum(dot_nt(d_kernel, windows) * decay, axis=0, keepdims=True)
            columns += [column[:, :WINDOW], column[:, WINDOW:]]
        column = jnp.concatenate(columns + [jnp.zeros((LANES - heads, WINDOW), F32)], axis=0)
        column = jnp.concatenate([column, jnp.zeros((LANES, LANES - WINDOW), F32)], axis=1)
        rows = head_sum(jnp.concatenate(products, axis=1), table)
        dl_ref[...] = rows - jnp.transpose(column)[:WINDOW, :heads]

    @pl.when(jnp.logical_not(before))
    def _():
        decay_at = edge_decay(next_decay(rim_ref, heads), heads)
        held = []
        for pair, at in enumerate(pairs):
            q, g = rim_ref[:WINDOW, at], rim_ref[WINDOW:2 * WINDOW, at]
            keys, values = stacked(wk_ref[late:, at], masks), stacked(v_ref[late:, at], masks)
            kernel = dot(decay_at(2 * pair).astype(BF16), windows)
            held.append(
                (q, g, (dot_nt(q, keys) * kernel).astype(BF16), (dot_nt(g, values) * kernel).astype(BF16))
            )
        for (q, g, weights, d_scores), at in zip(held, pairs):
            first_ref[:, at] = dot_tn(one_above(d_scores), stacked(q, masks))
            second_ref[:, at] = dot_tn(one_above(weights), stacked(g, masks))


def finish_kernel(heads, count, me_ref, q_ref, k_ref, x_ref, v_ref, g_ref, coef_ref, rate_ref,
                  small_ref, wk_ref, qf_ref, near_ref, far_ref, adjoint_ref,
                  dqf_ref, dwk_ref, dvl_ref, dl_ref, scales_ref,
                  near_first_ref, near_second_ref, near_dl_ref, far_first_ref, far_second_ref, far_dl_ref,
                  near_part_ref, far_part_ref, cross_ref, passed_ref,
                  dq_ref, dk_ref, dv_ref, logits_ref, sums_ref,
                  fwd_ref, bwd_ref, rim_dq_ref, rim_dwk_ref, rim_dv_ref, rim_dl_ref):
    length, width = wk_ref.shape
    late = length - WINDOW
    pairs = width // LANES
    received(me_ref, near_ref, far_ref, fwd_ref, bwd_ref)

    def edges(dq, dl, dwk, dv):
        rim_dq_ref[...], rim_dl_ref[...] = dq[...], dl[...]
        rim_dwk_ref[...], rim_dv_ref[...] = dwk[...], dv[...]

    far_edge = (far_first_ref, far_dl_ref, near_first_ref, near_second_ref)
    near_edge = (near_first_ref, near_dl_ref, far_first_ref, far_second_ref)
    pl.when(is_odd(me_ref))(lambda: edges(*near_edge))
    pl.when(jnp.logical_not(is_odd(me_ref)))(lambda: edges(*far_edge))
    table = head_table(heads, width)
    masks = half_masks()
    small = small_ref[...]
    total, gamma, soft, slope = (small[:, i * heads:(i + 1) * heads] for i in range(4))
    last, middle = total[length - 1:], total[late - 1:late]
    tail = jnp.exp(last - total)
    own = mask_dot(window_own_t(length), tail, 2)
    next_total = next_decay(bwd_ref, heads)
    next_middle = next_total[WINDOW - 1:]
    onward = mask_dot(window_rim_t(), jnp.exp(next_middle - next_total), 2)
    grown = jnp.exp(jnp.concatenate([total[:late], total[late:] - middle], axis=0))
    fade = jnp.exp(last - middle)
    onward_x = expand(jnp.concatenate([onward, jnp.exp(next_middle)], axis=0), table)
    onward_x, next_x = onward_x[:WINDOW], onward_x[WINDOW:]
    own_x, grown_x, gamma_x = (scales_ref.at[i * length:(i + 1) * length] for i in range(3))
    middle_x, fade_x = (scales_ref[i:i + 1] for i in range(3 * length, 3 * length + 2))

    me = me_ref[0]
    shape = (WINDOW, width)
    odd = everywhere(is_odd(me_ref), shape)
    edge = everywhere((me == 0) | (me == count - 1), shape)
    cross = jnp.where(edge, 0.0, cross_ref[...].astype(F32))
    passed = passed_ref[...].astype(F32)
    near_part, far_part = near_part_ref[...], far_part_ref[...]
    start = jnp.where(odd, passed, cross)
    later = jnp.where(odd, cross, passed)
    after = jnp.where(odd, far_part, near_part) + next_x * later
    halfway = middle_x * start + jnp.where(odd, near_part, far_part)
    half_after = adjoint_ref[...] + fade_x * after
    d_state = jnp.sum(head_sum(after * halfway, table, 2), axis=0, keepdims=True)
    start, later, after, halfway, half_after = (
        z.astype(BF16) for z in (start, later, after, halfway, half_after)
    )

    own_products, rim_products, out_products, key_products, d_coef = [], [], [], [], []
    coef = coef_ref[...]
    for pair in range(pairs):
        at = slice(pair * LANES, (pair + 1) * LANES)
        m0, m1, a1, a0, b0 = (stacked(z[:, at], masks) for z in (start, halfway, after, half_after, later))
        qf, g, wk, v = qf_ref[:, at], g_ref[:, at], wk_ref[:, at], v_ref[:, at]
        from_q = jnp.concatenate([dot(qf[:late], m0), dot(qf[late:], m1)], axis=0)
        out_products.append(from_q * g.astype(F32))
        from_g = jnp.concatenate([dot_nt(g[:late], m0), dot_nt(g[late:], m1)], axis=0)
        dqf = dqf_ref[:, at] + grown_x[:, at] * from_g
        dqf = jnp.concatenate([dqf[:late] + rim_dq_ref[:, at], dqf[late:]], axis=0)
        from_keys = dot(wk, a1)
        own_products.append(from_keys * v.astype(F32))
        rim_products.append(dot(fwd_ref[:WINDOW, at], a0) * fwd_ref[WINDOW:2 * WINDOW, at].astype(F32))
        dwk = dwk_ref[:, at] + own_x[:, at] * dot_nt(v, a1)
        dv = dvl_ref[:, at] + own_x[:, at] * from_keys
        dwk = jnp.concatenate(
            [dwk[:late], dwk[late:] + rim_dwk_ref[:, at] + onward_x[:, at] * dot_nt(v[late:], b0)], axis=0
        )
        dv_ref[:late, at] = dv[:late].astype(BF16)
        dv_ref[late:, at] = (
            dv[late:] + rim_dv_ref[:, at] + onward_x[:, at] * dot(wk[late:], b0)
        ).astype(BF16)
        q, k = q_ref[:, at].astype(F32), k_ref[:, at].astype(F32)
        c = coef[:, at]
        key_products.append(dwk * phi(k, c))
        d_phi = dwk * gamma_x[:, at]
        dq_ref[:, at] = dqf
        dk_ref[:, at] = d_phi
        d_coef.append(jnp.sum(dqf * (0.125 * q * q) + d_phi * (0.125 * k * k), axis=0, keepdims=True))

    sums = jnp.concatenate(
        [
            jnp.concatenate(z, axis=1).astype(BF16)
            for z in (own_products, out_products, key_products, rim_products)
        ],
        axis=0,
    )
    sums = dot_nt(sums, table)
    d_own, d_out, d_gamma = (sums[i * length:(i + 1) * length] for i in range(3))
    d_rim = sums[3 * length:]
    d_tail = tail * mask_dot(window_own(length), d_own, 2)
    rim_tail = jnp.exp(middle - total[:late]) * mask_dot(window_rim(), d_rim, 2)
    at_end = jnp.sum(own * d_own, axis=0, keepdims=True) + fade * d_state
    d_total = dl_ref[...] + grown * d_out - d_tail
    d_total = jnp.concatenate([d_total[:late] + rim_dl_ref[...] - rim_tail, d_total[late:]], axis=0)
    d_total = d_total + jnp.where(iota((length, heads), 0) == length - 1, at_end, 0.0)
    upper = (iota((length, length), 1) >= iota((length, length), 0)).astype(BF16)
    d_decay = mask_dot(upper, d_total, 3)
    d_rate = -jnp.sum(d_decay * soft, axis=0, keepdims=True)
    d_logits = jnp.concatenate(
        [-rate_ref[...] * d_decay * slope, d_gamma * gamma * (1.0 - WINDOW * gamma)], axis=1
    )
    logits_ref[...] = d_logits
    gate = dot_tn(d_logits.astype(BF16), x_ref[...])
    d_rate = jnp.concatenate([d_rate, jnp.zeros((1, LANES - heads), F32)], axis=1)
    for i in range(pairs):
        sums_ref[i * 2 * heads:(i + 1) * 2 * heads] = gate[:, i * LANES:(i + 1) * LANES].astype(BF16)
    rest = d_coef + [d_rate, jnp.zeros((BAND - 1 - pairs, LANES), F32)]
    sums_ref[pairs * 2 * heads:] = jnp.concatenate(rest, axis=0).astype(BF16)


def outputs_kernel(me_ref, logits_ref, w_ref, q_ref, k_ref, coef_ref, dqf_ref, d_phi_ref, dv_ref,
                   dx_ref, dq_ref, dk_ref, dv_out, sem):
    copy = pltpu.make_async_copy(dv_ref, dv_out, sem)
    copy.start()
    coef = 0.25 * coef_ref[...]
    dq_ref[...] = (dqf_ref[...] * (0.125 + coef * q_ref[...].astype(F32))).astype(BF16)
    dk_ref[...] = (d_phi_ref[...] * (0.125 + coef * k_ref[...].astype(F32))).astype(BF16)
    high, low = (part.astype(F32) for part in split(logits_ref[...], 2))
    w_high, w_low = split(w_ref[...], 2)
    dx_ref[...] = dot(
        jnp.concatenate([high, low, high], axis=1).astype(BF16),
        jnp.concatenate([w_high, w_high, w_low], axis=0),
    ).astype(BF16)
    copy.wait()


def last_kernel(heads, me_ref, mine_ref, theirs_ref, gate_ref, coef_ref, rate_ref):
    blocks = gate_ref.shape[1] // LANES

    def write(sums_ref):
        for i in range(blocks):
            at = slice(i * LANES, (i + 1) * LANES)
            gate_ref[:, at] = sums_ref[i * 2 * heads:(i + 1) * 2 * heads]
            coef_ref[:, at] = sums_ref[blocks * 2 * heads + i:blocks * 2 * heads + i + 1]
        at = blocks * (2 * heads + 1)
        rate_ref[...] = sums_ref[at:at + 1, :heads]

    pl.when(is_odd(me_ref))(lambda: write(mine_ref))
    pl.when(jnp.logical_not(is_odd(me_ref)))(lambda: write(theirs_ref))


def call(kernel, outs, operands, name, scratch=(), in_place=(), outside=(), flops=10**8, moved=3 * 10**6):
    specs = [pl.BlockSpec(memory_space=pltpu.SMEM)]
    specs += [
        pl.BlockSpec(memory_space=pltpu.HBM if i in in_place else pltpu.VMEM)
        for i in range(1, len(operands))
    ]
    operands = [
        pltpu.with_memory_space_constraint(z, pltpu.HBM) if i in in_place else z
        for i, z in enumerate(operands)
    ]
    return pl.pallas_call(
        kernel,
        out_shape=tuple(jax.ShapeDtypeStruct(*out) for out in outs),
        in_specs=specs,
        out_specs=tuple(
            pl.BlockSpec(memory_space=pltpu.HBM if i in outside else pltpu.VMEM) for i in range(len(outs))
        ),
        scratch_shapes=list(scratch),
        compiler_params=pltpu.CompilerParams(vmem_limit_bytes=32 * 2**20),
        cost_estimate=pl.CostEstimate(flops=flops, bytes_accessed=moved, transcendentals=10**6),
        name=name,
    )(*operands)


EVERYONE = ("dp", "seq")


def swapped(value, axis, distance):
    return lax.ppermute(value, axis, [(i, i ^ distance) for i in range(lax.axis_size(axis))])


def odd_swapped(value, distance, stage):
    count = lax.axis_size(EVERYONE)
    idle = 8 if stage == 2 and count > 8 else 4
    return lax.ppermute(value, EVERYONE, [(i, i ^ (distance if i % 2 else idle)) for i in range(count)])


def inner_swapped(value):
    dp, seq = (lax.axis_size(axis) for axis in EVERYONE)
    pairs = []
    for i in range(dp):
        for j in range(seq):
            inner = 0 < j < seq - 1
            pairs.append((i * seq + j, i * seq + seq - 1 - j if inner else (i ^ 1) * seq + j))
    return lax.ppermute(value, EVERYONE, pairs)


def on_device(queries, key_rows, value_rows, inputs, w_gate, poly_coef, decay_rate, cotangent):
    q, k, v, x, g = (z[0] for z in (queries, key_rows, value_rows, inputs, cotangent))
    length, width = x.shape
    heads = decay_rate.shape[0]
    count = lax.axis_size("seq")
    assert count == 4 and length == 2 * WINDOW
    me = lax.axis_index("seq").astype(jnp.int32).reshape(1)
    wide, small = ((length, width), BF16), ((length, LANES), F32)
    full, half, gain = ((length, width), F32), ((WINDOW, width), F32), ((length, heads), F32)
    rim, sent = ((2 * WINDOW + BAND, width), BF16), ((WINDOW, width), BF16)
    wk, qf, gates, near, far, memory, adjoint, q, k, v, x, g, wt, coef, rate = call(
        functools.partial(prep_kernel, heads, count),
        [wide, wide, small, ((3 * WINDOW + BAND, width), BF16), rim, half, half]
        + [wide] * 5
        + [((2 * heads, width), F32), ((1, width), F32), ((1, heads), F32)],
        (me, q, k, v, x, g, w_gate.T, poly_coef.reshape(1, width), decay_rate.reshape(1, heads)),
        "prep",
        scratch=[pltpu.SemaphoreType.DMA((8,))],
        in_place=range(1, 9),
    )
    near = swapped(near, "seq", 1)
    far = inner_swapped(far)
    near_part, cross = call(
        functools.partial(join_kernel, heads, count, True),
        [half, sent],
        (me, gates, gates, gates, memory, adjoint, near),
        "join_near",
    )
    cross = inner_swapped(cross)
    own = call(
        functools.partial(own_kernel, heads),
        [full, full, full, gain],
        (me, gates, wk, qf, v, g),
        "own",
        flops=7 * 10**8,
        moved=7 * 10**6,
    )
    edge = [half, half, ((WINDOW, heads), F32)]
    *near_edge, scales = call(
        functools.partial(edge_kernel, heads, True),
        edge + [((3 * length + BAND, width), F32)],
        (me, gates, wk, qf, v, g, near),
        "edge_near",
        flops=2 * 10**8,
        moved=5 * 10**6,
    )
    far_part, base, weight = call(
        functools.partial(join_kernel, heads, count, False),
        [half, half, ((1, width), F32)],
        (me, own[3], near_edge[2], gates, memory, adjoint, far),
        "join_far",
    )
    passed = call(pass_kernel, [sent], (me, base, weight, cross), "pass_on")[0]
    passed = swapped(passed, "seq", 1)
    far_edge = call(
        functools.partial(edge_kernel, heads, False),
        edge,
        (me, gates, wk, qf, v, g, far),
        "edge_far",
        flops=2 * 10**8,
        moved=3 * 10**6,
    )
    all_sums = ((width // LANES * 2 * heads + BAND, LANES), BF16)
    dqf, d_phi, dv, d_logits, sums = call(
        functools.partial(finish_kernel, heads, count),
        [full, full, wide, ((length, 2 * heads), F32), all_sums],
        (me, q, k, x, v, g, coef, rate, gates, wk, qf, near, far, adjoint, *own, scales, *near_edge, *far_edge,
         near_part, far_part, cross, passed),
        "finish",
        scratch=[pltpu.VMEM(*z) for z in (rim, rim, half, half, half, edge[2])],
    )
    dx, dq, dk, dv = call(
        outputs_kernel,
        [wide] * 4,
        (me, d_logits, wt, q, k, coef, dqf, d_phi, dv),
        "outputs",
        scratch=[pltpu.SemaphoreType.DMA],
        outside=(3,),
    )
    sums = sums.astype(F32) + swapped(sums, EVERYONE, 1).astype(F32)
    distance = 2
    while distance < lax.axis_size(EVERYONE):
        sums = sums.astype(BF16)
        if 2 * distance < lax.axis_size(EVERYONE):
            far, mid, one = (odd_swapped(sums, i * distance, distance).astype(F32) for i in (3, 2, 1))
            sums = (one + mid) + (far + sums.astype(F32))
        else:
            sums = sums.astype(F32) + odd_swapped(sums, distance, distance).astype(F32)
        if distance == 2:
            sums, dx, dq, dk, dv = lax.optimization_barrier((sums, dx, dq, dk, dv))
        distance *= 4
    gate, d_coef, d_rate = call(
        functools.partial(last_kernel, heads),
        [((2 * heads, width), F32), ((1, width), F32), ((1, heads), F32)],
        (me, sums, swapped(sums, "seq", 1)),
        "last",
    )
    return (dq[None], dk[None], dv[None], dx[None], gate.T, d_coef.reshape(width), d_rate.reshape(heads))


def solution(mesh):
    rows = P("dp", "seq", None)
    return jax.shard_map(
        on_device,
        mesh=mesh,
        in_specs=(rows, rows, rows, rows, P(), P(), P(), rows),
        out_specs=(rows, rows, rows, rows, P(), P(), P()),
        check_vma=False,
    )
```

```python
import functools

import jax
import jax.numpy as jnp
from jax import lax
from jax.experimental import pallas as pl
from jax.experimental.pallas import tpu as pltpu
from jax.sharding import PartitionSpec as P

WINDOW = 64
LANES = 128
BAND = 16
F32 = jnp.float32
BF16 = jnp.bfloat16


def iota(shape, dim):
    return lax.broadcasted_iota(jnp.int32, shape, dim)


def split(z, count):
    parts = []
    for _ in range(count):
        high = z.astype(BF16)
        parts.append(high)
        z = z - high.astype(F32)
    return parts


def dot(a, b):
    return lax.dot_general(a, b, (((1,), (0,)), ((), ())), preferred_element_type=F32)


def dot_nt(a, b):
    return lax.dot_general(a, b, (((1,), (1,)), ((), ())), preferred_element_type=F32)


def dot_tn(a, b):
    return lax.dot_general(a, b, (((0,), (0,)), ((), ())), preferred_element_type=F32)


def mask_dot(mask, z, count):
    return sum(dot(mask, part) for part in split(z, count))


def head_table(heads, width):
    per_head = width // heads
    return (iota((heads, width), 1) // per_head == iota((heads, width), 0)).astype(BF16)


def expand(z, table, count=1):
    return sum(dot(part, table) for part in split(z, count))


def head_sum(z, table, count=1):
    return sum(dot_nt(part, table) for part in split(z, count))


def half_masks():
    lane = iota((1, LANES), 1)
    return (lane < LANES // 2).astype(BF16), (lane >= LANES // 2).astype(BF16)


def stacked(z, masks):
    return jnp.concatenate([z * masks[0], z * masks[1]], axis=0)


def one_above(z):
    columns = z.shape[1] // 2
    return jnp.concatenate([z[:, :columns], z[:, columns:]], axis=0)


def folded(z):
    rows = z.shape[0] // 2
    return jnp.where(iota((rows, LANES), 1) < LANES // 2, z[:rows], z[rows:])


def window_own(length):
    gap = iota((length, length), 0) - iota((length, length), 1)
    return ((gap >= 0) & (gap < WINDOW)).astype(BF16)


def window_own_t(length):
    gap = iota((length, length), 1) - iota((length, length), 0)
    return ((gap >= 0) & (gap < WINDOW)).astype(BF16)


def window_rim():
    return (iota((WINDOW, WINDOW), 0) < iota((WINDOW, WINDOW), 1)).astype(BF16)


def window_rim_t():
    return (iota((WINDOW, WINDOW), 1) < iota((WINDOW, WINDOW), 0)).astype(BF16)


def phi(raw, coef):
    return 0.125 * (raw + coef * raw * raw)


def is_odd(me_ref):
    return jax.lax.rem(me_ref[0], 2) == 1


def everywhere(flag, shape):
    return jnp.full(shape, flag.astype(jnp.int32)) == 1


def prep_kernel(heads, count, me_ref, q_ref, k_ref, v_ref, x_ref, g_ref, w_ref, coef_ref, rate_ref,
                wk_ref, qf_ref, small_ref, near_ref, far_ref, memory_ref, adjoint_ref,
                q_buf, k_buf, v_buf, x_buf, g_buf, w_buf, coef_buf, rate_buf, sems):
    length, width = x_ref.shape
    late = length - WINDOW
    copies = [
        pltpu.make_async_copy(source, target, sems.at[i])
        for i, (source, target) in enumerate(
            [
                (x_ref, x_buf), (w_ref, w_buf), (rate_ref, rate_buf), (k_ref, k_buf),
                (coef_ref, coef_buf), (q_ref, q_buf), (v_ref, v_buf), (g_ref, g_buf),
            ]
        )
    ]
    for copy in copies:
        copy.start()
    table = head_table(heads, width)
    lower = (iota((length, length), 1) <= iota((length, length), 0)).astype(BF16)
    copies[0].wait()
    copies[1].wait()
    x = x_buf[...]
    logits = sum(dot_nt(x, part) for part in split(w_buf[...], 2))
    decay_logit = logits[:, :heads]
    soft = jnp.maximum(decay_logit, 0.0) + jnp.log1p(jnp.exp(-jnp.abs(decay_logit)))
    slope = jax.nn.sigmoid(decay_logit)
    gamma = jax.nn.sigmoid(logits[:, heads:]) * (1.0 / WINDOW)
    copies[2].wait()
    total = mask_dot(lower, -rate_buf[...] * soft, 3)
    small_ref[...] = jnp.concatenate(
        [total, gamma, soft, slope, jnp.zeros((length, LANES - 4 * heads), F32)], axis=1
    )
    info = jnp.concatenate(
        [part.astype(F32) for part in split(total[:WINDOW], 3)]
        + [jnp.zeros((WINDOW, LANES - 3 * heads), F32)],
        axis=1,
    ).astype(BF16)
    copies[3].wait()
    copies[4].wait()
    coef = coef_buf[...]
    wk = (phi(k_buf[...].astype(F32), coef) * expand(gamma, table)).astype(BF16)
    wk_ref[...] = wk
    copies[5].wait()
    qf = phi(q_buf[...].astype(F32), coef).astype(BF16)
    qf_ref[...] = qf
    copies[6].wait()
    copies[7].wait()
    kept = mask_dot(window_own_t(length), jnp.exp(total[length - 1:] - total), 2)
    faded = jnp.exp(total[late:] - total[late - 1:late])
    scale = expand(jnp.concatenate([kept, faded], axis=0), table)
    carried = (wk.astype(F32) * scale[:length]).astype(BF16)
    faded = (g_buf[late:].astype(F32) * scale[length:]).astype(BF16)
    memory, adjoint = [], []
    for pair in range(width // LANES):
        at = slice(pair * LANES, (pair + 1) * LANES)
        memory.append(folded(dot_tn(carried[:, at], v_buf[:, at])))
        adjoint.append(folded(dot_tn(qf[late:, at], faded[:, at])))
    memory, adjoint = jnp.concatenate(memory, axis=1), jnp.concatenate(adjoint, axis=1)
    memory_ref[...] = memory
    adjoint_ref[...] = adjoint

    def pack(onward, back):
        onward[:WINDOW] = wk[late:]
        onward[WINDOW:2 * WINDOW] = v_buf[late:]
        back[:WINDOW] = qf[:WINDOW]
        back[WINDOW:2 * WINDOW] = g_buf[:WINDOW]
        onward[2 * WINDOW:2 * WINDOW + BAND] = jnp.zeros((BAND, width), BF16)
        back[2 * WINDOW:2 * WINDOW + BAND] = jnp.zeros((BAND, width), BF16)
        for step in range(WINDOW // BAND):
            band = info[step * BAND:(step + 1) * BAND]
            back[2 * WINDOW:2 * WINDOW + BAND, step * LANES:(step + 1) * LANES] = band

    odd = is_odd(me_ref)
    pl.when(odd)(lambda: pack(far_ref, near_ref))
    pl.when(jnp.logical_not(odd))(lambda: pack(near_ref, far_ref))
    near_ref[2 * WINDOW + BAND:] = jnp.where(everywhere(odd, memory.shape), adjoint, memory).astype(BF16)

    @pl.when((me_ref[0] == 0) | (me_ref[0] == count - 1))
    def _():
        far_ref[...] = jnp.zeros_like(far_ref)


def received(me_ref, near_ref, far_ref, fwd_ref, bwd_ref):
    odd = is_odd(me_ref)

    def keep(before, after):
        fwd_ref[...] = before[:2 * WINDOW + BAND]
        bwd_ref[...] = after[:2 * WINDOW + BAND]

    pl.when(odd)(lambda: keep(near_ref, far_ref))
    pl.when(jnp.logical_not(odd))(lambda: keep(far_ref, near_ref))


def next_decay(rim_ref, heads):
    info = jnp.concatenate(
        [
            rim_ref[2 * WINDOW:2 * WINDOW + BAND, step * LANES:(step + 1) * LANES]
            for step in range(WINDOW // BAND)
        ],
        axis=0,
    ).astype(F32)
    return info[:, :heads] + info[:, heads:2 * heads] + info[:, 2 * heads:3 * heads]


def join_kernel(heads, count, before_if_odd, me_ref, own_ref, edge_ref, small_ref, memory_ref, adjoint_ref, rim_ref,
                *rest):
    part_ref, out_ref, weight_ref = rest if len(rest) == 3 else (*rest, None)
    width = rim_ref.shape[1]
    length = small_ref.shape[0]
    table = head_table(heads, width)
    total = small_ref[:, :heads]
    last = total[length - 1:]
    middle = total[length - WINDOW - 1:length - WINDOW]
    next_total = next_decay(rim_ref, heads)
    before = is_odd(me_ref) if before_if_odd else jnp.logical_not(is_odd(me_ref))
    kept = mask_dot(window_rim_t(), jnp.exp(middle - total[:WINDOW]), 2)
    scale = jnp.where(everywhere(before, kept.shape), kept, jnp.exp(next_total))
    fade = jnp.exp(last - middle)
    weight = jnp.where(
        everywhere(before, fade.shape), jnp.exp(last), fade * jnp.exp(next_total[WINDOW - 1:])
    )
    scale = expand(jnp.concatenate([scale, fade, weight], axis=0), table)
    scaled = (rim_ref[WINDOW:2 * WINDOW].astype(F32) * scale[:WINDOW]).astype(BF16)
    fade, weight = scale[WINDOW:WINDOW + 1], scale[WINDOW + 1:]
    base = jnp.where(everywhere(before, memory_ref.shape), memory_ref[...], adjoint_ref[...])
    if weight_ref is None:
        base = base + weight * rim_ref[2 * WINDOW + BAND:].astype(F32)
    else:
        edge = (me_ref[0] == 0) | (me_ref[0] == count - 1)
        weight_ref[...] = jnp.where(everywhere(edge, weight.shape), 0.0, weight)
    for pair in range(width // LANES):
        at = slice(pair * LANES, (pair + 1) * LANES)
        part = folded(dot_tn(rim_ref[:WINDOW, at], scaled[:, at]))
        part_ref[:, at] = part
        out_ref[:, at] = (base[:, at] + fade[:, at] * part).astype(out_ref.dtype)


def pass_kernel(me_ref, base_ref, weight_ref, state_ref, out_ref):
    out_ref[...] = (base_ref[...] + weight_ref[...] * state_ref[...].astype(F32)).astype(BF16)


def decays(column_pair, row_pair, keep):
    gap = jnp.where(keep, column_pair - row_pair, -1e30)
    return jnp.exp(gap)


def own_kernel(heads, me_ref, small_ref, wk_ref, qf_ref, v_ref, g_ref, dq_ref, dwk_ref, dv_ref, dl_ref):
    length, width = wk_ref.shape
    table = head_table(heads, width)
    masks = half_masks()
    small = small_ref[...]
    total = small[:, :heads]
    total_t = jnp.transpose(small)[:heads]
    keep = iota((length, length), 1) <= iota((length, length), 0)
    own = window_own(length).astype(F32)
    empty = jnp.zeros_like(own)
    windows = jnp.concatenate(
        [jnp.concatenate([own, empty], axis=1), jnp.concatenate([empty, own], axis=1)], axis=0
    ).astype(BF16)
    pairs = [slice(pair * LANES, (pair + 1) * LANES) for pair in range(width // LANES)]
    held = []
    for pair, at in enumerate(pairs):
        decay = jnp.concatenate(
            [decays(total[:, i:i + 1], total_t[i:i + 1], keep) for i in (2 * pair, 2 * pair + 1)], axis=1
        )
        kernel = dot(decay.astype(BF16), windows)
        scores = dot_nt(qf_ref[:, at], stacked(wk_ref[:, at], masks))
        lifted = dot_nt(g_ref[:, at], stacked(v_ref[:, at], masks))
        held.append(
            (
                decay,
                (scores * kernel).astype(BF16),
                (lifted * kernel).astype(BF16),
                (lifted * scores).astype(BF16),
            )
        )
    columns = []
    products = []
    for (decay, weights, d_scores, d_kernel), at in zip(held, pairs):
        q, g = qf_ref[:, at], g_ref[:, at]
        products.append(dot(weights, stacked(v_ref[:, at], masks)) * g.astype(F32))
        dq_ref[:, at] = dot(d_scores, stacked(wk_ref[:, at], masks))
        dwk_ref[:, at] = dot_tn(one_above(d_scores), stacked(q, masks))
        dv_ref[:, at] = dot_tn(one_above(weights), stacked(g, masks))
        column = jnp.sum(dot_nt(d_kernel, windows) * decay, axis=0, keepdims=True)
        columns += [column[:, :length], column[:, length:]]
    column = jnp.concatenate(columns + [jnp.zeros((LANES - heads, length), F32)], axis=0)
    rows = head_sum(jnp.concatenate(products, axis=1), table)
    dl_ref[...] = rows - jnp.transpose(column)[:, :heads]


def edge_decay(total, heads):
    lane = iota((WINDOW, LANES), 1)
    first = lane < LANES // 2
    keep = jnp.where(first, lane, lane - LANES // 2) <= iota((WINDOW, LANES), 0)
    doubled = jnp.concatenate([total, total], axis=0)
    doubled = jnp.concatenate([doubled, jnp.zeros((2 * WINDOW, LANES - heads), F32)], axis=1)
    rows = jnp.transpose(doubled)[:heads]
    return lambda h: decays(
        jnp.where(first, total[:, h:h + 1], total[:, h + 1:h + 2]),
        jnp.where(first, rows[h:h + 1], rows[h + 1:h + 2]),
        keep,
    )


def scales_of(heads, small_ref, scales_ref):
    length = small_ref.shape[0]
    late = length - WINDOW
    total, gamma = small_ref[:, :heads], small_ref[:, heads:2 * heads]
    last, middle = total[length - 1:], total[late - 1:late]
    own = mask_dot(window_own_t(length), jnp.exp(last - total), 2)
    grown = jnp.exp(jnp.concatenate([total[:late], total[late:] - middle], axis=0))
    rest = [jnp.exp(middle), jnp.exp(last - middle), jnp.zeros((BAND - 2, heads), F32)]
    scales = jnp.concatenate([own, grown, gamma] + rest, axis=0)
    scales_ref[...] = expand(scales, head_table(heads, scales_ref.shape[1]))


def edge_kernel(heads, before_if_odd, me_ref, small_ref, wk_ref, qf_ref, v_ref, g_ref, rim_ref,
                first_ref, second_ref, dl_ref, *rest):
    length, width = wk_ref.shape
    late = length - WINDOW
    table = head_table(heads, width)
    masks = half_masks()
    pairs = [slice(pair * LANES, (pair + 1) * LANES) for pair in range(width // LANES)]
    cell = (iota((LANES, LANES), 0), iota((LANES, LANES), 1))
    same = (cell[0] < WINDOW) == (cell[1] < WINDOW)
    windows = (same & (cell[0] < cell[1])).astype(BF16)
    before = is_odd(me_ref) if before_if_odd else jnp.logical_not(is_odd(me_ref))
    if rest:
        scales_of(heads, small_ref, rest[0])

    @pl.when(before)
    def _():
        decay_at = edge_decay(small_ref[:WINDOW, :heads], heads)
        held = []
        for pair, at in enumerate(pairs):
            keys, values = stacked(rim_ref[:WINDOW, at], masks), stacked(rim_ref[WINDOW:2 * WINDOW, at], masks)
            decay = decay_at(2 * pair)
            kernel = dot(decay.astype(BF16), windows)
            scores = dot_nt(qf_ref[:WINDOW, at], keys)
            lifted = dot_nt(g_ref[:WINDOW, at], values)
            held.append(
                (
                    keys,
                    values,
                    decay,
                    (scores * kernel).astype(BF16),
                    (lifted * kernel).astype(BF16),
                    (lifted * scores).astype(BF16),
                )
            )
        columns, products = [], []
        for (keys, values, decay, weights, d_scores, d_kernel), at in zip(held, pairs):
            products.append(dot(weights, values) * g_ref[:WINDOW, at].astype(F32))
            first_ref[:, at] = dot(d_scores, keys)
            column = jnp.sum(dot_nt(d_kernel, windows) * decay, axis=0, keepdims=True)
            columns += [column[:, :WINDOW], column[:, WINDOW:]]
        column = jnp.concatenate(columns + [jnp.zeros((LANES - heads, WINDOW), F32)], axis=0)
        column = jnp.concatenate([column, jnp.zeros((LANES, LANES - WINDOW), F32)], axis=1)
        rows = head_sum(jnp.concatenate(products, axis=1), table)
        dl_ref[...] = rows - jnp.transpose(column)[:WINDOW, :heads]

    @pl.when(jnp.logical_not(before))
    def _():
        decay_at = edge_decay(next_decay(rim_ref, heads), heads)
        held = []
        for pair, at in enumerate(pairs):
            q, g = rim_ref[:WINDOW, at], rim_ref[WINDOW:2 * WINDOW, at]
            keys, values = stacked(wk_ref[late:, at], masks), stacked(v_ref[late:, at], masks)
            kernel = dot(decay_at(2 * pair).astype(BF16), windows)
            held.append(
                (q, g, (dot_nt(q, keys) * kernel).astype(BF16), (dot_nt(g, values) * kernel).astype(BF16))
            )
        for (q, g, weights, d_scores), at in zip(held, pairs):
            first_ref[:, at] = dot_tn(one_above(d_scores), stacked(q, masks))
            second_ref[:, at] = dot_tn(one_above(weights), stacked(g, masks))


def finish_kernel(heads, count, me_ref, q_ref, k_ref, x_ref, v_ref, g_ref, coef_ref, rate_ref,
                  small_ref, wk_ref, qf_ref, near_ref, far_ref, adjoint_ref,
                  dqf_ref, dwk_ref, dvl_ref, dl_ref, scales_ref,
                  near_first_ref, near_second_ref, near_dl_ref, far_first_ref, far_second_ref, far_dl_ref,
                  near_part_ref, far_part_ref, cross_ref, passed_ref,
                  dq_ref, dk_ref, dv_ref, logits_ref, sums_ref,
                  fwd_ref, bwd_ref, rim_dq_ref, rim_dwk_ref, rim_dv_ref, rim_dl_ref):
    length, width = wk_ref.shape
    late = length - WINDOW
    pairs = width // LANES
    received(me_ref, near_ref, far_ref, fwd_ref, bwd_ref)

    def edges(dq, dl, dwk, dv):
        rim_dq_ref[...], rim_dl_ref[...] = dq[...], dl[...]
        rim_dwk_ref[...], rim_dv_ref[...] = dwk[...], dv[...]

    far_edge = (far_first_ref, far_dl_ref, near_first_ref, near_second_ref)
    near_edge = (near_first_ref, near_dl_ref, far_first_ref, far_second_ref)
    pl.when(is_odd(me_ref))(lambda: edges(*near_edge))
    pl.when(jnp.logical_not(is_odd(me_ref)))(lambda: edges(*far_edge))
    table = head_table(heads, width)
    masks = half_masks()
    small = small_ref[...]
    total, gamma, soft, slope = (small[:, i * heads:(i + 1) * heads] for i in range(4))
    last, middle = total[length - 1:], total[late - 1:late]
    tail = jnp.exp(last - total)
    own = mask_dot(window_own_t(length), tail, 2)
    next_total = next_decay(bwd_ref, heads)
    next_middle = next_total[WINDOW - 1:]
    onward = mask_dot(window_rim_t(), jnp.exp(next_middle - next_total), 2)
    grown = jnp.exp(jnp.concatenate([total[:late], total[late:] - middle], axis=0))
    fade = jnp.exp(last - middle)
    onward_x = expand(jnp.concatenate([onward, jnp.exp(next_middle)], axis=0), table)
    onward_x, next_x = onward_x[:WINDOW], onward_x[WINDOW:]
    own_x, grown_x, gamma_x = (scales_ref.at[i * length:(i + 1) * length] for i in range(3))
    middle_x, fade_x = (scales_ref[i:i + 1] for i in range(3 * length, 3 * length + 2))

    me = me_ref[0]
    shape = (WINDOW, width)
    odd = everywhere(is_odd(me_ref), shape)
    edge = everywhere((me == 0) | (me == count - 1), shape)
    cross = jnp.where(edge, 0.0, cross_ref[...].astype(F32))
    passed = passed_ref[...].astype(F32)
    near_part, far_part = near_part_ref[...], far_part_ref[...]
    start = jnp.where(odd, passed, cross)
    later = jnp.where(odd, cross, passed)
    after = jnp.where(odd, far_part, near_part) + next_x * later
    halfway = middle_x * start + jnp.where(odd, near_part, far_part)
    half_after = adjoint_ref[...] + fade_x * after
    d_state = jnp.sum(head_sum(after * halfway, table, 2), axis=0, keepdims=True)
    start, later, after, halfway, half_after = (
        z.astype(BF16) for z in (start, later, after, halfway, half_after)
    )

    own_products, rim_products, out_products, key_products, d_coef = [], [], [], [], []
    coef = coef_ref[...]
    for pair in range(pairs):
        at = slice(pair * LANES, (pair + 1) * LANES)
        m0, m1, a1, a0, b0 = (stacked(z[:, at], masks) for z in (start, halfway, after, half_after, later))
        qf, g, wk, v = qf_ref[:, at], g_ref[:, at], wk_ref[:, at], v_ref[:, at]
        from_q = jnp.concatenate([dot(qf[:late], m0), dot(qf[late:], m1)], axis=0)
        out_products.append(from_q * g.astype(F32))
        from_g = jnp.concatenate([dot_nt(g[:late], m0), dot_nt(g[late:], m1)], axis=0)
        dqf = dqf_ref[:, at] + grown_x[:, at] * from_g
        dqf = jnp.concatenate([dqf[:late] + rim_dq_ref[:, at], dqf[late:]], axis=0)
        from_keys = dot(wk, a1)
        own_products.append(from_keys * v.astype(F32))
        rim_products.append(dot(fwd_ref[:WINDOW, at], a0) * fwd_ref[WINDOW:2 * WINDOW, at].astype(F32))
        dwk = dwk_ref[:, at] + own_x[:, at] * dot_nt(v, a1)
        dv = dvl_ref[:, at] + own_x[:, at] * from_keys
        dwk = jnp.concatenate(
            [dwk[:late], dwk[late:] + rim_dwk_ref[:, at] + onward_x[:, at] * dot_nt(v[late:], b0)], axis=0
        )
        dv_ref[:late, at] = dv[:late].astype(BF16)
        dv_ref[late:, at] = (
            dv[late:] + rim_dv_ref[:, at] + onward_x[:, at] * dot(wk[late:], b0)
        ).astype(BF16)
        q, k = q_ref[:, at].astype(F32), k_ref[:, at].astype(F32)
        c = coef[:, at]
        key_products.append(dwk * phi(k, c))
        d_phi = dwk * gamma_x[:, at]
        dq_ref[:, at] = dqf
        dk_ref[:, at] = d_phi
        d_coef.append(jnp.sum(dqf * (0.125 * q * q) + d_phi * (0.125 * k * k), axis=0, keepdims=True))

    sums = jnp.concatenate(
        [
            jnp.concatenate(z, axis=1).astype(BF16)
            for z in (own_products, out_products, key_products, rim_products)
        ],
        axis=0,
    )
    sums = dot_nt(sums, table)
    d_own, d_out, d_gamma = (sums[i * length:(i + 1) * length] for i in range(3))
    d_rim = sums[3 * length:]
    d_tail = tail * mask_dot(window_own(length), d_own, 2)
    rim_tail = jnp.exp(middle - total[:late]) * mask_dot(window_rim(), d_rim, 2)
    at_end = jnp.sum(own * d_own, axis=0, keepdims=True) + fade * d_state
    d_total = dl_ref[...] + grown * d_out - d_tail
    d_total = jnp.concatenate([d_total[:late] + rim_dl_ref[...] - rim_tail, d_total[late:]], axis=0)
    d_total = d_total + jnp.where(iota((length, heads), 0) == length - 1, at_end, 0.0)
    upper = (iota((length, length), 1) >= iota((length, length), 0)).astype(BF16)
    d_decay = mask_dot(upper, d_total, 3)
    d_rate = -jnp.sum(d_decay * soft, axis=0, keepdims=True)
    d_logits = jnp.concatenate(
        [-rate_ref[...] * d_decay * slope, d_gamma * gamma * (1.0 - WINDOW * gamma)], axis=1
    )
    logits_ref[...] = d_logits
    gate = dot_tn(d_logits.astype(BF16), x_ref[...])
    d_rate = jnp.concatenate([d_rate, jnp.zeros((1, LANES - heads), F32)], axis=1)
    for i in range(pairs):
        sums_ref[i * 2 * heads:(i + 1) * 2 * heads] = gate[:, i * LANES:(i + 1) * LANES].astype(BF16)
    rest = d_coef + [d_rate, jnp.zeros((BAND - 1 - pairs, LANES), F32)]
    sums_ref[pairs * 2 * heads:] = jnp.concatenate(rest, axis=0).astype(BF16)


def outputs_kernel(me_ref, logits_ref, w_ref, q_ref, k_ref, coef_ref, dqf_ref, d_phi_ref, dv_ref,
                   dx_ref, dq_ref, dk_ref, dv_out, sem):
    copy = pltpu.make_async_copy(dv_ref, dv_out, sem)
    copy.start()
    coef = 0.25 * coef_ref[...]
    dq_ref[...] = (dqf_ref[...] * (0.125 + coef * q_ref[...].astype(F32))).astype(BF16)
    dk_ref[...] = (d_phi_ref[...] * (0.125 + coef * k_ref[...].astype(F32))).astype(BF16)
    high, low = (part.astype(F32) for part in split(logits_ref[...], 2))
    w_high, w_low = split(w_ref[...], 2)
    dx_ref[...] = dot(
        jnp.concatenate([high, low, high], axis=1).astype(BF16),
        jnp.concatenate([w_high, w_high, w_low], axis=0),
    ).astype(BF16)
    copy.wait()


def last_kernel(heads, me_ref, mine_ref, theirs_ref, gate_ref, coef_ref, rate_ref):
    blocks = gate_ref.shape[1] // LANES

    def write(sums_ref):
        rest = sums_ref[blocks * 2 * heads:].astype(F32)
        for i in range(blocks):
            at = slice(i * LANES, (i + 1) * LANES)
            gate_ref[:, at] = sums_ref[i * 2 * heads:(i + 1) * 2 * heads].astype(F32)
            coef_ref[:, at] = rest[i:i + 1]
        rate_ref[...] = rest[blocks:blocks + 1, :heads]

    pl.when(is_odd(me_ref))(lambda: write(mine_ref))
    pl.when(jnp.logical_not(is_odd(me_ref)))(lambda: write(theirs_ref))


def call(kernel, outs, operands, name, scratch=(), in_place=(), outside=(), flops=10**8, moved=3 * 10**6):
    specs = [pl.BlockSpec(memory_space=pltpu.SMEM)]
    specs += [
        pl.BlockSpec(memory_space=pltpu.HBM if i in in_place else pltpu.VMEM)
        for i in range(1, len(operands))
    ]
    operands = [
        pltpu.with_memory_space_constraint(z, pltpu.HBM) if i in in_place else z
        for i, z in enumerate(operands)
    ]
    return pl.pallas_call(
        kernel,
        out_shape=tuple(jax.ShapeDtypeStruct(*out) for out in outs),
        in_specs=specs,
        out_specs=tuple(
            pl.BlockSpec(memory_space=pltpu.HBM if i in outside else pltpu.VMEM) for i in range(len(outs))
        ),
        scratch_shapes=list(scratch),
        compiler_params=pltpu.CompilerParams(vmem_limit_bytes=32 * 2**20),
        cost_estimate=pl.CostEstimate(flops=flops, bytes_accessed=moved, transcendentals=10**6),
        name=name,
    )(*operands)


EVERYONE = ("dp", "seq")


def swapped(value, axis, distance):
    return lax.ppermute(value, axis, [(i, i ^ distance) for i in range(lax.axis_size(axis))])


def odd_swapped(value, distance, stage):
    count = lax.axis_size(EVERYONE)
    idle = 8 if stage == 2 and count > 8 else 2 if distance == 2 * stage else 4
    return lax.ppermute(value, EVERYONE, [(i, i ^ (distance if i % 2 else idle)) for i in range(count)])


def inner_swapped(value):
    dp, seq = (lax.axis_size(axis) for axis in EVERYONE)
    pairs = []
    for i in range(dp):
        for j in range(seq):
            inner = 0 < j < seq - 1
            pairs.append((i * seq + j, i * seq + seq - 1 - j if inner else (i ^ 1) * seq + j))
    return lax.ppermute(value, EVERYONE, pairs)


def on_device(queries, key_rows, value_rows, inputs, w_gate, poly_coef, decay_rate, cotangent):
    q, k, v, x, g = (z[0] for z in (queries, key_rows, value_rows, inputs, cotangent))
    length, width = x.shape
    heads = decay_rate.shape[0]
    count = lax.axis_size("seq")
    assert count == 4 and length == 2 * WINDOW
    me = lax.axis_index("seq").astype(jnp.int32).reshape(1)
    wide, small = ((length, width), BF16), ((length, LANES), F32)
    full, half, gain = ((length, width), F32), ((WINDOW, width), F32), ((length, heads), F32)
    rim, sent = ((2 * WINDOW + BAND, width), BF16), ((WINDOW, width), BF16)
    wk, qf, gates, near, far, memory, adjoint, q, k, v, x, g, wt, coef, rate = call(
        functools.partial(prep_kernel, heads, count),
        [wide, wide, small, ((3 * WINDOW + BAND, width), BF16), rim, half, half]
        + [wide] * 5
        + [((2 * heads, width), F32), ((1, width), F32), ((1, heads), F32)],
        (me, q, k, v, x, g, w_gate.T, poly_coef.reshape(1, width), decay_rate.reshape(1, heads)),
        "prep",
        scratch=[pltpu.SemaphoreType.DMA((8,))],
        in_place=range(1, 9),
    )
    near = swapped(near, "seq", 1)
    far = inner_swapped(far)
    near_part, cross = call(
        functools.partial(join_kernel, heads, count, True),
        [half, sent],
        (me, gates, gates, gates, memory, adjoint, near),
        "join_near",
    )
    cross = inner_swapped(cross)
    own = call(
        functools.partial(own_kernel, heads),
        [full, full, full, gain],
        (me, gates, wk, qf, v, g),
        "own",
        flops=7 * 10**8,
        moved=7 * 10**6,
    )
    edge = [half, half, ((WINDOW, heads), F32)]
    *near_edge, scales = call(
        functools.partial(edge_kernel, heads, True),
        edge + [((3 * length + BAND, width), F32)],
        (me, gates, wk, qf, v, g, near),
        "edge_near",
        flops=2 * 10**8,
        moved=5 * 10**6,
    )
    far_part, base, weight = call(
        functools.partial(join_kernel, heads, count, False),
        [half, half, ((1, width), F32)],
        (me, own[3], near_edge[2], gates, memory, adjoint, far),
        "join_far",
    )
    passed = call(pass_kernel, [sent], (me, base, weight, cross), "pass_on")[0]
    passed = swapped(passed, "seq", 1)
    far_edge = call(
        functools.partial(edge_kernel, heads, False),
        edge,
        (me, gates, wk, qf, v, g, far),
        "edge_far",
        flops=2 * 10**8,
        moved=3 * 10**6,
    )
    all_sums = ((width // LANES * 2 * heads + BAND, LANES), BF16)
    dqf, d_phi, dv, d_logits, sums = call(
        functools.partial(finish_kernel, heads, count),
        [full, full, wide, ((length, 2 * heads), F32), all_sums],
        (me, q, k, x, v, g, coef, rate, gates, wk, qf, near, far, adjoint, *own, scales, *near_edge, *far_edge,
         near_part, far_part, cross, passed),
        "finish",
        scratch=[pltpu.VMEM(*z) for z in (rim, rim, half, half, half, edge[2])],
    )
    dx, dq, dk, dv = call(
        outputs_kernel,
        [wide] * 4,
        (me, d_logits, wt, q, k, coef, dqf, d_phi, dv),
        "outputs",
        scratch=[pltpu.SemaphoreType.DMA],
        outside=(3,),
    )
    sums = sums.astype(F32) + swapped(sums, EVERYONE, 1).astype(F32)
    distance = 2
    while distance < lax.axis_size(EVERYONE):
        sums = sums.astype(BF16)
        if 2 * distance < lax.axis_size(EVERYONE):
            far, mid, one = (odd_swapped(sums, i * distance, distance).astype(F32) for i in (3, 2, 1))
            sums = (one + mid) + (far + sums.astype(F32))
        else:
            sums = sums.astype(F32) + odd_swapped(sums, distance, distance).astype(F32)
        if distance == 2:
            sums, dx, dq, dk, dv = lax.optimization_barrier((sums, dx, dq, dk, dv))
        distance *= 4
    sums = sums.astype(BF16)
    gate, d_coef, d_rate = call(
        functools.partial(last_kernel, heads),
        [((2 * heads, width), F32), ((1, width), F32), ((1, heads), F32)],
        (me, sums, swapped(sums, EVERYONE, 1)),
        "last",
    )
    return (dq[None], dk[None], dv[None], dx[None], gate.T, d_coef.reshape(width), d_rate.reshape(heads))


def solution(mesh):
    rows = P("dp", "seq", None)
    return jax.shard_map(
        on_device,
        mesh=mesh,
        in_specs=(rows, rows, rows, rows, P(), P(), P(), rows),
        out_specs=(rows, rows, rows, rows, P(), P(), P()),
        check_vma=False,
    )
```

```python
import functools

import jax
import jax.numpy as jnp
from jax import lax
from jax.experimental import pallas as pl
from jax.experimental.pallas import tpu as pltpu
from jax.sharding import PartitionSpec as P

WINDOW = 64
LANES = 128
BAND = 16
F32 = jnp.float32
BF16 = jnp.bfloat16


def iota(shape, dim):
    return lax.broadcasted_iota(jnp.int32, shape, dim)


def split(z, count):
    parts = []
    for _ in range(count):
        high = z.astype(BF16)
        parts.append(high)
        z = z - high.astype(F32)
    return parts


def dot(a, b):
    return lax.dot_general(a, b, (((1,), (0,)), ((), ())), preferred_element_type=F32)


def dot_nt(a, b):
    return lax.dot_general(a, b, (((1,), (1,)), ((), ())), preferred_element_type=F32)


def dot_tn(a, b):
    return lax.dot_general(a, b, (((0,), (0,)), ((), ())), preferred_element_type=F32)


def mask_dot(mask, z, count):
    return sum(dot(mask, part) for part in split(z, count))


def head_table(heads, width):
    per_head = width // heads
    return (iota((heads, width), 1) // per_head == iota((heads, width), 0)).astype(BF16)


def expand(z, table, count=1):
    return sum(dot(part, table) for part in split(z, count))


def head_sum(z, table, count=1):
    return sum(dot_nt(part, table) for part in split(z, count))


def half_masks():
    lane = iota((1, LANES), 1)
    return (lane < LANES // 2).astype(BF16), (lane >= LANES // 2).astype(BF16)


def stacked(z, masks):
    return jnp.concatenate([z * masks[0], z * masks[1]], axis=0)


def one_above(z):
    columns = z.shape[1] // 2
    return jnp.concatenate([z[:, :columns], z[:, columns:]], axis=0)


def folded(z):
    rows = z.shape[0] // 2
    return jnp.where(iota((rows, LANES), 1) < LANES // 2, z[:rows], z[rows:])


def window_own(length):
    gap = iota((length, length), 0) - iota((length, length), 1)
    return ((gap >= 0) & (gap < WINDOW)).astype(BF16)


def window_own_t(length):
    gap = iota((length, length), 1) - iota((length, length), 0)
    return ((gap >= 0) & (gap < WINDOW)).astype(BF16)


def window_rim():
    return (iota((WINDOW, WINDOW), 0) < iota((WINDOW, WINDOW), 1)).astype(BF16)


def window_rim_t():
    return (iota((WINDOW, WINDOW), 1) < iota((WINDOW, WINDOW), 0)).astype(BF16)


def phi(raw, coef):
    return 0.125 * (raw + coef * raw * raw)


def is_odd(me_ref):
    return jax.lax.rem(me_ref[0], 2) == 1


def everywhere(flag, shape):
    return jnp.full(shape, flag.astype(jnp.int32)) == 1


def prep_kernel(heads, count, me_ref, q_ref, k_ref, v_ref, x_ref, g_ref, w_ref, coef_ref, rate_ref,
                wk_ref, qf_ref, small_ref, near_ref, far_ref, memory_ref, adjoint_ref,
                q_buf, k_buf, v_buf, x_buf, g_buf, w_buf, coef_buf, rate_buf, sems):
    length, width = x_ref.shape
    late = length - WINDOW
    copies = [
        pltpu.make_async_copy(source, target, sems.at[i])
        for i, (source, target) in enumerate(
            [
                (x_ref, x_buf), (w_ref, w_buf), (rate_ref, rate_buf), (k_ref, k_buf),
                (coef_ref, coef_buf), (q_ref, q_buf), (v_ref, v_buf), (g_ref, g_buf),
            ]
        )
    ]
    for copy in copies:
        copy.start()
    table = head_table(heads, width)
    lower = (iota((length, length), 1) <= iota((length, length), 0)).astype(BF16)
    copies[0].wait()
    copies[1].wait()
    x = x_buf[...]
    logits = sum(dot_nt(x, part) for part in split(w_buf[...], 2))
    decay_logit = logits[:, :heads]
    soft = jnp.maximum(decay_logit, 0.0) + jnp.log1p(jnp.exp(-jnp.abs(decay_logit)))
    slope = jax.nn.sigmoid(decay_logit)
    gamma = jax.nn.sigmoid(logits[:, heads:]) * (1.0 / WINDOW)
    copies[2].wait()
    total = mask_dot(lower, -rate_buf[...] * soft, 2)
    small_ref[...] = jnp.concatenate(
        [total, gamma, soft, slope, jnp.zeros((length, LANES - 4 * heads), F32)], axis=1
    )
    info = jnp.concatenate(
        [part.astype(F32) for part in split(total[:WINDOW], 3)]
        + [jnp.zeros((WINDOW, LANES - 3 * heads), F32)],
        axis=1,
    ).astype(BF16)
    copies[3].wait()
    copies[4].wait()
    coef = coef_buf[...]
    wk = (phi(k_buf[...].astype(F32), coef) * expand(gamma, table)).astype(BF16)
    wk_ref[...] = wk
    copies[5].wait()
    qf = phi(q_buf[...].astype(F32), coef).astype(BF16)
    qf_ref[...] = qf
    copies[6].wait()
    copies[7].wait()
    kept = mask_dot(window_own_t(length), jnp.exp(total[length - 1:] - total), 1)
    faded = jnp.exp(total[late:] - total[late - 1:late])
    scale = expand(jnp.concatenate([kept, faded], axis=0), table)
    carried = (wk.astype(F32) * scale[:length]).astype(BF16)
    faded = (g_buf[late:].astype(F32) * scale[length:]).astype(BF16)
    memory, adjoint = [], []
    for pair in range(width // LANES):
        at = slice(pair * LANES, (pair + 1) * LANES)
        memory.append(folded(dot_tn(carried[:, at], v_buf[:, at])))
        adjoint.append(folded(dot_tn(qf[late:, at], faded[:, at])))
    memory, adjoint = jnp.concatenate(memory, axis=1), jnp.concatenate(adjoint, axis=1)
    memory_ref[...] = memory
    adjoint_ref[...] = adjoint

    def pack(onward, back):
        onward[:WINDOW] = wk[late:]
        onward[WINDOW:2 * WINDOW] = v_buf[late:]
        back[:WINDOW] = qf[:WINDOW]
        back[WINDOW:2 * WINDOW] = g_buf[:WINDOW]
        onward[2 * WINDOW:2 * WINDOW + BAND] = jnp.zeros((BAND, width), BF16)
        back[2 * WINDOW:2 * WINDOW + BAND] = jnp.zeros((BAND, width), BF16)
        for step in range(WINDOW // BAND):
            band = info[step * BAND:(step + 1) * BAND]
            back[2 * WINDOW:2 * WINDOW + BAND, step * LANES:(step + 1) * LANES] = band

    odd = is_odd(me_ref)
    pl.when(odd)(lambda: pack(far_ref, near_ref))
    pl.when(jnp.logical_not(odd))(lambda: pack(near_ref, far_ref))
    near_ref[2 * WINDOW + BAND:] = jnp.where(everywhere(odd, memory.shape), adjoint, memory).astype(BF16)

    @pl.when((me_ref[0] == 0) | (me_ref[0] == count - 1))
    def _():
        far_ref[...] = jnp.zeros_like(far_ref)


def received(me_ref, near_ref, far_ref, fwd_ref, bwd_ref):
    odd = is_odd(me_ref)

    def keep(before, after):
        fwd_ref[...] = before[:2 * WINDOW + BAND]
        bwd_ref[...] = after[:2 * WINDOW + BAND]

    pl.when(odd)(lambda: keep(near_ref, far_ref))
    pl.when(jnp.logical_not(odd))(lambda: keep(far_ref, near_ref))


def next_decay(rim_ref, heads):
    info = jnp.concatenate(
        [
            rim_ref[2 * WINDOW:2 * WINDOW + BAND, step * LANES:(step + 1) * LANES]
            for step in range(WINDOW // BAND)
        ],
        axis=0,
    ).astype(F32)
    return info[:, :heads] + info[:, heads:2 * heads] + info[:, 2 * heads:3 * heads]


def join_kernel(heads, count, before_if_odd, me_ref, own_ref, edge_ref, small_ref, memory_ref, adjoint_ref, rim_ref,
                *rest):
    part_ref, out_ref, weight_ref = rest if len(rest) == 3 else (*rest, None)
    width = rim_ref.shape[1]
    length = small_ref.shape[0]
    table = head_table(heads, width)
    total = small_ref[:, :heads]
    last = total[length - 1:]
    middle = total[length - WINDOW - 1:length - WINDOW]
    next_total = next_decay(rim_ref, heads)
    before = is_odd(me_ref) if before_if_odd else jnp.logical_not(is_odd(me_ref))
    kept = mask_dot(window_rim_t(), jnp.exp(middle - total[:WINDOW]), 1)
    scale = jnp.where(everywhere(before, kept.shape), kept, jnp.exp(next_total))
    fade = jnp.exp(last - middle)
    weight = jnp.where(
        everywhere(before, fade.shape), jnp.exp(last), fade * jnp.exp(next_total[WINDOW - 1:])
    )
    scale = expand(jnp.concatenate([scale, fade, weight], axis=0), table)
    scaled = (rim_ref[WINDOW:2 * WINDOW].astype(F32) * scale[:WINDOW]).astype(BF16)
    fade, weight = scale[WINDOW:WINDOW + 1], scale[WINDOW + 1:]
    base = jnp.where(everywhere(before, memory_ref.shape), memory_ref[...], adjoint_ref[...])
    if weight_ref is None:
        base = base + weight * rim_ref[2 * WINDOW + BAND:].astype(F32)
    else:
        edge = (me_ref[0] == 0) | (me_ref[0] == count - 1)
        weight_ref[...] = jnp.where(everywhere(edge, weight.shape), 0.0, weight)
    for pair in range(width // LANES):
        at = slice(pair * LANES, (pair + 1) * LANES)
        part = folded(dot_tn(rim_ref[:WINDOW, at], scaled[:, at]))
        part_ref[:, at] = part
        out_ref[:, at] = (base[:, at] + fade[:, at] * part).astype(out_ref.dtype)


def pass_kernel(me_ref, base_ref, weight_ref, state_ref, out_ref):
    out_ref[...] = (base_ref[...] + weight_ref[...] * state_ref[...].astype(F32)).astype(BF16)


def decays(column_pair, row_pair, keep):
    gap = jnp.where(keep, column_pair - row_pair, -1e30)
    return jnp.exp(gap)


def own_kernel(heads, me_ref, small_ref, wk_ref, qf_ref, v_ref, g_ref, dq_ref, dwk_ref, dv_ref, dl_ref):
    length, width = wk_ref.shape
    table = head_table(heads, width)
    masks = half_masks()
    small = small_ref[...]
    total = small[:, :heads]
    total_t = jnp.transpose(small)[:heads]
    keep = iota((length, length), 1) <= iota((length, length), 0)
    own = window_own(length).astype(F32)
    empty = jnp.zeros_like(own)
    windows = jnp.concatenate(
        [jnp.concatenate([own, empty], axis=1), jnp.concatenate([empty, own], axis=1)], axis=0
    ).astype(BF16)
    pairs = [slice(pair * LANES, (pair + 1) * LANES) for pair in range(width // LANES)]
    held = []
    for pair, at in enumerate(pairs):
        decay = jnp.concatenate(
            [decays(total[:, i:i + 1], total_t[i:i + 1], keep) for i in (2 * pair, 2 * pair + 1)], axis=1
        )
        kernel = dot(decay.astype(BF16), windows)
        scores = dot_nt(qf_ref[:, at], stacked(wk_ref[:, at], masks))
        lifted = dot_nt(g_ref[:, at], stacked(v_ref[:, at], masks))
        held.append(
            (
                decay,
                (scores * kernel).astype(BF16),
                (lifted * kernel).astype(BF16),
                (lifted * scores).astype(BF16),
            )
        )
    columns = []
    products = []
    for (decay, weights, d_scores, d_kernel), at in zip(held, pairs):
        q, g = qf_ref[:, at], g_ref[:, at]
        products.append(dot(weights, stacked(v_ref[:, at], masks)) * g.astype(F32))
        dq_ref[:, at] = dot(d_scores, stacked(wk_ref[:, at], masks))
        dwk_ref[:, at] = dot_tn(one_above(d_scores), stacked(q, masks))
        dv_ref[:, at] = dot_tn(one_above(weights), stacked(g, masks))
        column = jnp.sum(dot_nt(d_kernel, windows) * decay, axis=0, keepdims=True)
        columns += [column[:, :length], column[:, length:]]
    column = jnp.concatenate(columns + [jnp.zeros((LANES - heads, length), F32)], axis=0)
    rows = head_sum(jnp.concatenate(products, axis=1), table)
    dl_ref[...] = rows - jnp.transpose(column)[:, :heads]


def edge_decay(total, heads):
    lane = iota((WINDOW, LANES), 1)
    first = lane < LANES // 2
    keep = jnp.where(first, lane, lane - LANES // 2) <= iota((WINDOW, LANES), 0)
    doubled = jnp.concatenate([total, total], axis=0)
    doubled = jnp.concatenate([doubled, jnp.zeros((2 * WINDOW, LANES - heads), F32)], axis=1)
    rows = jnp.transpose(doubled)[:heads]
    return lambda h: decays(
        jnp.where(first, total[:, h:h + 1], total[:, h + 1:h + 2]),
        jnp.where(first, rows[h:h + 1], rows[h + 1:h + 2]),
        keep,
    )


def scales_of(heads, small_ref, scales_ref):
    length = small_ref.shape[0]
    late = length - WINDOW
    total, gamma = small_ref[:, :heads], small_ref[:, heads:2 * heads]
    last, middle = total[length - 1:], total[late - 1:late]
    own = mask_dot(window_own_t(length), jnp.exp(last - total), 1)
    grown = jnp.exp(jnp.concatenate([total[:late], total[late:] - middle], axis=0))
    rest = [jnp.exp(middle), jnp.exp(last - middle), jnp.zeros((BAND - 2, heads), F32)]
    scales = jnp.concatenate([own, grown, gamma] + rest, axis=0)
    scales_ref[...] = expand(scales, head_table(heads, scales_ref.shape[1]))


def edge_kernel(heads, before_if_odd, me_ref, small_ref, wk_ref, qf_ref, v_ref, g_ref, rim_ref,
                first_ref, second_ref, dl_ref, *rest):
    length, width = wk_ref.shape
    late = length - WINDOW
    table = head_table(heads, width)
    masks = half_masks()
    pairs = [slice(pair * LANES, (pair + 1) * LANES) for pair in range(width // LANES)]
    cell = (iota((LANES, LANES), 0), iota((LANES, LANES), 1))
    same = (cell[0] < WINDOW) == (cell[1] < WINDOW)
    windows = (same & (cell[0] < cell[1])).astype(BF16)
    before = is_odd(me_ref) if before_if_odd else jnp.logical_not(is_odd(me_ref))
    if rest:
        scales_of(heads, small_ref, rest[0])

    @pl.when(before)
    def _():
        decay_at = edge_decay(small_ref[:WINDOW, :heads], heads)
        held = []
        for pair, at in enumerate(pairs):
            keys, values = stacked(rim_ref[:WINDOW, at], masks), stacked(rim_ref[WINDOW:2 * WINDOW, at], masks)
            decay = decay_at(2 * pair)
            kernel = dot(decay.astype(BF16), windows)
            scores = dot_nt(qf_ref[:WINDOW, at], keys)
            lifted = dot_nt(g_ref[:WINDOW, at], values)
            held.append(
                (
                    keys,
                    values,
                    decay,
                    (scores * kernel).astype(BF16),
                    (lifted * kernel).astype(BF16),
                    (lifted * scores).astype(BF16),
                )
            )
        columns, products = [], []
        for (keys, values, decay, weights, d_scores, d_kernel), at in zip(held, pairs):
            products.append(dot(weights, values) * g_ref[:WINDOW, at].astype(F32))
            first_ref[:, at] = dot(d_scores, keys)
            column = jnp.sum(dot_nt(d_kernel, windows) * decay, axis=0, keepdims=True)
            columns += [column[:, :WINDOW], column[:, WINDOW:]]
        column = jnp.concatenate(columns + [jnp.zeros((LANES - heads, WINDOW), F32)], axis=0)
        column = jnp.concatenate([column, jnp.zeros((LANES, LANES - WINDOW), F32)], axis=1)
        rows = head_sum(jnp.concatenate(products, axis=1), table)
        dl_ref[...] = rows - jnp.transpose(column)[:WINDOW, :heads]

    @pl.when(jnp.logical_not(before))
    def _():
        decay_at = edge_decay(next_decay(rim_ref, heads), heads)
        held = []
        for pair, at in enumerate(pairs):
            q, g = rim_ref[:WINDOW, at], rim_ref[WINDOW:2 * WINDOW, at]
            keys, values = stacked(wk_ref[late:, at], masks), stacked(v_ref[late:, at], masks)
            kernel = dot(decay_at(2 * pair).astype(BF16), windows)
            held.append(
                (q, g, (dot_nt(q, keys) * kernel).astype(BF16), (dot_nt(g, values) * kernel).astype(BF16))
            )
        for (q, g, weights, d_scores), at in zip(held, pairs):
            first_ref[:, at] = dot_tn(one_above(d_scores), stacked(q, masks))
            second_ref[:, at] = dot_tn(one_above(weights), stacked(g, masks))


def finish_kernel(heads, count, me_ref, q_ref, k_ref, x_ref, v_ref, g_ref, coef_ref, rate_ref,
                  small_ref, wk_ref, qf_ref, near_ref, far_ref, adjoint_ref,
                  dqf_ref, dwk_ref, dvl_ref, dl_ref, scales_ref,
                  near_first_ref, near_second_ref, near_dl_ref, far_first_ref, far_second_ref, far_dl_ref,
                  near_part_ref, far_part_ref, cross_ref, passed_ref,
                  dq_ref, dk_ref, dv_ref, logits_ref, sums_ref,
                  fwd_ref, bwd_ref, rim_dq_ref, rim_dwk_ref, rim_dv_ref, rim_dl_ref):
    length, width = wk_ref.shape
    late = length - WINDOW
    pairs = width // LANES
    received(me_ref, near_ref, far_ref, fwd_ref, bwd_ref)

    def edges(dq, dl, dwk, dv):
        rim_dq_ref[...], rim_dl_ref[...] = dq[...], dl[...]
        rim_dwk_ref[...], rim_dv_ref[...] = dwk[...], dv[...]

    far_edge = (far_first_ref, far_dl_ref, near_first_ref, near_second_ref)
    near_edge = (near_first_ref, near_dl_ref, far_first_ref, far_second_ref)
    pl.when(is_odd(me_ref))(lambda: edges(*near_edge))
    pl.when(jnp.logical_not(is_odd(me_ref)))(lambda: edges(*far_edge))
    table = head_table(heads, width)
    masks = half_masks()
    small = small_ref[...]
    total, gamma, soft, slope = (small[:, i * heads:(i + 1) * heads] for i in range(4))
    last, middle = total[length - 1:], total[late - 1:late]
    tail = jnp.exp(last - total)
    own = mask_dot(window_own_t(length), tail, 1)
    next_total = next_decay(bwd_ref, heads)
    next_middle = next_total[WINDOW - 1:]
    onward = mask_dot(window_rim_t(), jnp.exp(next_middle - next_total), 1)
    grown = jnp.exp(jnp.concatenate([total[:late], total[late:] - middle], axis=0))
    fade = jnp.exp(last - middle)
    onward_x = expand(jnp.concatenate([onward, jnp.exp(next_middle)], axis=0), table)
    onward_x, next_x = onward_x[:WINDOW], onward_x[WINDOW:]
    own_x, grown_x, gamma_x = (scales_ref.at[i * length:(i + 1) * length] for i in range(3))
    middle_x, fade_x = (scales_ref[i:i + 1] for i in range(3 * length, 3 * length + 2))

    me = me_ref[0]
    shape = (WINDOW, width)
    odd = everywhere(is_odd(me_ref), shape)
    edge = everywhere((me == 0) | (me == count - 1), shape)
    cross = jnp.where(edge, 0.0, cross_ref[...].astype(F32))
    passed = passed_ref[...].astype(F32)
    near_part, far_part = near_part_ref[...], far_part_ref[...]
    start = jnp.where(odd, passed, cross)
    later = jnp.where(odd, cross, passed)
    after = jnp.where(odd, far_part, near_part) + next_x * later
    halfway = middle_x * start + jnp.where(odd, near_part, far_part)
    half_after = adjoint_ref[...] + fade_x * after
    d_state = jnp.sum(head_sum(after * halfway, table), axis=0, keepdims=True)
    start, later, after, halfway, half_after = (
        z.astype(BF16) for z in (start, later, after, halfway, half_after)
    )

    own_products, rim_products, out_products, key_products, d_coef = [], [], [], [], []
    coef = coef_ref[...]
    for pair in range(pairs):
        at = slice(pair * LANES, (pair + 1) * LANES)
        m0, m1, a1, a0, b0 = (stacked(z[:, at], masks) for z in (start, halfway, after, half_after, later))
        qf, g, wk, v = qf_ref[:, at], g_ref[:, at], wk_ref[:, at], v_ref[:, at]
        from_q = jnp.concatenate([dot(qf[:late], m0), dot(qf[late:], m1)], axis=0)
        out_products.append(from_q * g.astype(F32))
        from_g = jnp.concatenate([dot_nt(g[:late], m0), dot_nt(g[late:], m1)], axis=0)
        dqf = dqf_ref[:, at] + grown_x[:, at] * from_g
        dqf = jnp.concatenate([dqf[:late] + rim_dq_ref[:, at], dqf[late:]], axis=0)
        from_keys = dot(wk, a1)
        own_products.append(from_keys * v.astype(F32))
        rim_products.append(dot(fwd_ref[:WINDOW, at], a0) * fwd_ref[WINDOW:2 * WINDOW, at].astype(F32))
        dwk = dwk_ref[:, at] + own_x[:, at] * dot_nt(v, a1)
        dv = dvl_ref[:, at] + own_x[:, at] * from_keys
        dwk = jnp.concatenate(
            [dwk[:late], dwk[late:] + rim_dwk_ref[:, at] + onward_x[:, at] * dot_nt(v[late:], b0)], axis=0
        )
        dv_ref[:late, at] = dv[:late].astype(BF16)
        dv_ref[late:, at] = (
            dv[late:] + rim_dv_ref[:, at] + onward_x[:, at] * dot(wk[late:], b0)
        ).astype(BF16)
        q, k = q_ref[:, at].astype(F32), k_ref[:, at].astype(F32)
        c = coef[:, at]
        key_products.append(dwk * phi(k, c))
        d_phi = dwk * gamma_x[:, at]
        dq_ref[:, at] = dqf
        dk_ref[:, at] = d_phi
        d_coef.append(jnp.sum(dqf * (0.125 * q * q) + d_phi * (0.125 * k * k), axis=0, keepdims=True))

    sums = jnp.concatenate(
        [
            jnp.concatenate(z, axis=1).astype(BF16)
            for z in (own_products, out_products, key_products, rim_products)
        ],
        axis=0,
    )
    sums = dot_nt(sums, table)
    d_own, d_out, d_gamma = (sums[i * length:(i + 1) * length] for i in range(3))
    d_rim = sums[3 * length:]
    d_tail = tail * mask_dot(window_own(length), d_own, 1)
    rim_tail = jnp.exp(middle - total[:late]) * mask_dot(window_rim(), d_rim, 1)
    at_end = jnp.sum(own * d_own, axis=0, keepdims=True) + fade * d_state
    d_total = dl_ref[...] + grown * d_out - d_tail
    d_total = jnp.concatenate([d_total[:late] + rim_dl_ref[...] - rim_tail, d_total[late:]], axis=0)
    d_total = d_total + jnp.where(iota((length, heads), 0) == length - 1, at_end, 0.0)
    upper = (iota((length, length), 1) >= iota((length, length), 0)).astype(BF16)
    d_decay = mask_dot(upper, d_total, 2)
    d_rate = -jnp.sum(d_decay * soft, axis=0, keepdims=True)
    d_logits = jnp.concatenate(
        [-rate_ref[...] * d_decay * slope, d_gamma * gamma * (1.0 - WINDOW * gamma)], axis=1
    )
    logits_ref[...] = d_logits
    gate = dot_tn(d_logits.astype(BF16), x_ref[...])
    d_rate = jnp.concatenate([d_rate, jnp.zeros((1, LANES - heads), F32)], axis=1)
    for i in range(pairs):
        sums_ref[i * 2 * heads:(i + 1) * 2 * heads] = gate[:, i * LANES:(i + 1) * LANES].astype(BF16)
    rest = d_coef + [d_rate, jnp.zeros((BAND - 1 - pairs, LANES), F32)]
    sums_ref[pairs * 2 * heads:] = jnp.concatenate(rest, axis=0).astype(BF16)


def outputs_kernel(me_ref, logits_ref, w_ref, q_ref, k_ref, coef_ref, dqf_ref, d_phi_ref, dv_ref,
                   dx_ref, dq_ref, dk_ref, dv_out, sem):
    copy = pltpu.make_async_copy(dv_ref, dv_out, sem)
    copy.start()
    coef = 0.25 * coef_ref[...]
    dq_ref[...] = (dqf_ref[...] * (0.125 + coef * q_ref[...].astype(F32))).astype(BF16)
    dk_ref[...] = (d_phi_ref[...] * (0.125 + coef * k_ref[...].astype(F32))).astype(BF16)
    high, low = (part.astype(F32) for part in split(logits_ref[...], 2))
    w_high, w_low = split(w_ref[...], 2)
    dx_ref[...] = dot(
        jnp.concatenate([high, low, high], axis=1).astype(BF16),
        jnp.concatenate([w_high, w_high, w_low], axis=0),
    ).astype(BF16)
    copy.wait()


def last_kernel(heads, me_ref, mine_ref, theirs_ref, gate_ref, coef_ref, rate_ref):
    blocks = gate_ref.shape[1] // LANES

    def write(sums_ref):
        rest = sums_ref[blocks * 2 * heads:].astype(F32)
        for i in range(blocks):
            at = slice(i * LANES, (i + 1) * LANES)
            gate_ref[:, at] = sums_ref[i * 2 * heads:(i + 1) * 2 * heads].astype(F32)
            coef_ref[:, at] = rest[i:i + 1]
        rate_ref[...] = rest[blocks:blocks + 1, :heads]

    pl.when(is_odd(me_ref))(lambda: write(mine_ref))
    pl.when(jnp.logical_not(is_odd(me_ref)))(lambda: write(theirs_ref))


def call(kernel, outs, operands, name, scratch=(), in_place=(), outside=(), flops=10**8, moved=3 * 10**6):
    specs = [pl.BlockSpec(memory_space=pltpu.SMEM)]
    specs += [
        pl.BlockSpec(memory_space=pltpu.HBM if i in in_place else pltpu.VMEM)
        for i in range(1, len(operands))
    ]
    operands = [
        pltpu.with_memory_space_constraint(z, pltpu.HBM) if i in in_place else z
        for i, z in enumerate(operands)
    ]
    return pl.pallas_call(
        kernel,
        out_shape=tuple(jax.ShapeDtypeStruct(*out) for out in outs),
        in_specs=specs,
        out_specs=tuple(
            pl.BlockSpec(memory_space=pltpu.HBM if i in outside else pltpu.VMEM) for i in range(len(outs))
        ),
        scratch_shapes=list(scratch),
        compiler_params=pltpu.CompilerParams(vmem_limit_bytes=32 * 2**20),
        cost_estimate=pl.CostEstimate(flops=flops, bytes_accessed=moved, transcendentals=10**6),
        name=name,
    )(*operands)


EVERYONE = ("dp", "seq")


def swapped(value, axis, distance):
    return lax.ppermute(value, axis, [(i, i ^ distance) for i in range(lax.axis_size(axis))])


def odd_swapped(value, distance, stage):
    count = lax.axis_size(EVERYONE)
    idle = 8 if stage == 2 and count > 8 else 2 if distance == 2 * stage else 4
    return lax.ppermute(value, EVERYONE, [(i, i ^ (distance if i % 2 else idle)) for i in range(count)])


def inner_swapped(value):
    dp, seq = (lax.axis_size(axis) for axis in EVERYONE)
    pairs = []
    for i in range(dp):
        for j in range(seq):
            inner = 0 < j < seq - 1
            pairs.append((i * seq + j, i * seq + seq - 1 - j if inner else (i ^ 1) * seq + j))
    return lax.ppermute(value, EVERYONE, pairs)


def on_device(queries, key_rows, value_rows, inputs, w_gate, poly_coef, decay_rate, cotangent):
    q, k, v, x, g = (z[0] for z in (queries, key_rows, value_rows, inputs, cotangent))
    length, width = x.shape
    heads = decay_rate.shape[0]
    count = lax.axis_size("seq")
    assert count == 4 and length == 2 * WINDOW
    me = lax.axis_index("seq").astype(jnp.int32).reshape(1)
    wide, small = ((length, width), BF16), ((length, LANES), F32)
    full, half, gain = ((length, width), F32), ((WINDOW, width), F32), ((length, heads), F32)
    rim, sent = ((2 * WINDOW + BAND, width), BF16), ((WINDOW, width), BF16)
    wk, qf, gates, near, far, memory, adjoint, q, k, v, x, g, wt, coef, rate = call(
        functools.partial(prep_kernel, heads, count),
        [wide, wide, small, ((3 * WINDOW + BAND, width), BF16), rim, half, half]
        + [wide] * 5
        + [((2 * heads, width), F32), ((1, width), F32), ((1, heads), F32)],
        (me, q, k, v, x, g, w_gate.T, poly_coef.reshape(1, width), decay_rate.reshape(1, heads)),
        "prep",
        scratch=[pltpu.SemaphoreType.DMA((8,))],
        in_place=range(1, 9),
    )
    near = swapped(near, "seq", 1)
    far = inner_swapped(far)
    near_part, cross = call(
        functools.partial(join_kernel, heads, count, True),
        [half, sent],
        (me, gates, gates, gates, memory, adjoint, near),
        "join_near",
    )
    cross = inner_swapped(cross)
    own = call(
        functools.partial(own_kernel, heads),
        [full, full, full, gain],
        (me, gates, wk, qf, v, g),
        "own",
        flops=7 * 10**8,
        moved=7 * 10**6,
    )
    edge = [half, half, ((WINDOW, heads), F32)]
    *near_edge, scales = call(
        functools.partial(edge_kernel, heads, True),
        edge + [((3 * length + BAND, width), F32)],
        (me, gates, wk, qf, v, g, near),
        "edge_near",
        flops=2 * 10**8,
        moved=5 * 10**6,
    )
    far_part, base, weight = call(
        functools.partial(join_kernel, heads, count, False),
        [half, half, ((1, width), F32)],
        (me, own[3], near_edge[2], gates, memory, adjoint, far),
        "join_far",
    )
    passed = call(pass_kernel, [sent], (me, base, weight, cross), "pass_on")[0]
    passed = swapped(passed, "seq", 1)
    far_edge = call(
        functools.partial(edge_kernel, heads, False),
        edge,
        (me, gates, wk, qf, v, g, far),
        "edge_far",
        flops=2 * 10**8,
        moved=3 * 10**6,
    )
    all_sums = ((width // LANES * 2 * heads + BAND, LANES), BF16)
    dqf, d_phi, dv, d_logits, sums = call(
        functools.partial(finish_kernel, heads, count),
        [full, full, wide, ((length, 2 * heads), F32), all_sums],
        (me, q, k, x, v, g, coef, rate, gates, wk, qf, near, far, adjoint, *own, scales, *near_edge, *far_edge,
         near_part, far_part, cross, passed),
        "finish",
        scratch=[pltpu.VMEM(*z) for z in (rim, rim, half, half, half, edge[2])],
    )
    dx, dq, dk, dv = call(
        outputs_kernel,
        [wide] * 4,
        (me, d_logits, wt, q, k, coef, dqf, d_phi, dv),
        "outputs",
        scratch=[pltpu.SemaphoreType.DMA],
        outside=(3,),
    )
    sums = sums.astype(F32) + swapped(sums, EVERYONE, 1).astype(F32)
    distance = 2
    while distance < lax.axis_size(EVERYONE):
        sums = sums.astype(BF16)
        if 2 * distance < lax.axis_size(EVERYONE):
            far, mid, one = (odd_swapped(sums, i * distance, distance).astype(F32) for i in (3, 2, 1))
            sums = (one + mid) + (far + sums.astype(F32))
        else:
            sums = sums.astype(F32) + odd_swapped(sums, distance, distance).astype(F32)
        if distance == 2:
            sums, dx, dq, dk, dv = lax.optimization_barrier((sums, dx, dq, dk, dv))
        distance *= 4
    sums = sums.astype(BF16)
    gate, d_coef, d_rate = call(
        functools.partial(last_kernel, heads),
        [((2 * heads, width), F32), ((1, width), F32), ((1, heads), F32)],
        (me, sums, swapped(sums, EVERYONE, 1)),
        "last",
    )
    return (dq[None], dk[None], dv[None], dx[None], gate.T, d_coef.reshape(width), d_rate.reshape(heads))


def solution(mesh):
    rows = P("dp", "seq", None)
    return jax.shard_map(
        on_device,
        mesh=mesh,
        in_specs=(rows, rows, rows, rows, P(), P(), P(), rows),
        out_specs=(rows, rows, rows, rows, P(), P(), P()),
        check_vma=False,
    )
```

```python
import functools

import jax
import jax.numpy as jnp
from jax import lax
from jax.experimental import pallas as pl
from jax.experimental.pallas import tpu as pltpu
from jax.sharding import PartitionSpec as P

WINDOW = 64
LANES = 128
BAND = 16
F32 = jnp.float32
BF16 = jnp.bfloat16


def iota(shape, dim):
    return lax.broadcasted_iota(jnp.int32, shape, dim)


def split(z, count):
    parts = []
    for _ in range(count):
        high = z.astype(BF16)
        parts.append(high)
        z = z - high.astype(F32)
    return parts


def dot(a, b):
    return lax.dot_general(a, b, (((1,), (0,)), ((), ())), preferred_element_type=F32)


def dot_nt(a, b):
    return lax.dot_general(a, b, (((1,), (1,)), ((), ())), preferred_element_type=F32)


def dot_tn(a, b):
    return lax.dot_general(a, b, (((0,), (0,)), ((), ())), preferred_element_type=F32)


def mask_dot(mask, z, count):
    return sum(dot(mask, part) for part in split(z, count))


def head_table(heads, width):
    per_head = width // heads
    return (iota((heads, width), 1) // per_head == iota((heads, width), 0)).astype(BF16)


def expand(z, table, count=1):
    return sum(dot(part, table) for part in split(z, count))


def head_sum(z, table, count=1):
    return sum(dot_nt(part, table) for part in split(z, count))


def half_masks():
    lane = iota((1, LANES), 1)
    return (lane < LANES // 2).astype(BF16), (lane >= LANES // 2).astype(BF16)


def stacked(z, masks):
    return jnp.concatenate([z * masks[0], z * masks[1]], axis=0)


def one_above(z):
    columns = z.shape[1] // 2
    return jnp.concatenate([z[:, :columns], z[:, columns:]], axis=0)


def folded(z):
    rows = z.shape[0] // 2
    return jnp.where(iota((rows, LANES), 1) < LANES // 2, z[:rows], z[rows:])


def window_own(length):
    gap = iota((length, length), 0) - iota((length, length), 1)
    return ((gap >= 0) & (gap < WINDOW)).astype(BF16)


def window_own_t(length):
    gap = iota((length, length), 1) - iota((length, length), 0)
    return ((gap >= 0) & (gap < WINDOW)).astype(BF16)


def window_rim():
    return (iota((WINDOW, WINDOW), 0) < iota((WINDOW, WINDOW), 1)).astype(BF16)


def window_rim_t():
    return (iota((WINDOW, WINDOW), 1) < iota((WINDOW, WINDOW), 0)).astype(BF16)


def phi(raw, coef):
    return 0.125 * (raw + coef * raw * raw)


def is_odd(me_ref):
    return jax.lax.rem(me_ref[0], 2) == 1


def everywhere(flag, shape):
    return jnp.full(shape, flag.astype(jnp.int32)) == 1


def prep_kernel(heads, count, me_ref, q_ref, k_ref, v_ref, x_ref, g_ref, w_ref, coef_ref, rate_ref,
                wk_ref, qf_ref, small_ref, near_ref, far_ref, memory_ref, adjoint_ref,
                q_buf, k_buf, v_buf, x_buf, g_buf, w_buf, coef_buf, rate_buf, sems):
    length, width = x_ref.shape
    late = length - WINDOW
    copies = [
        pltpu.make_async_copy(source, target, sems.at[i])
        for i, (source, target) in enumerate(
            [
                (x_ref, x_buf), (w_ref, w_buf), (rate_ref, rate_buf), (k_ref, k_buf),
                (coef_ref, coef_buf), (q_ref, q_buf), (v_ref, v_buf), (g_ref, g_buf),
            ]
        )
    ]
    for copy in copies:
        copy.start()
    table = head_table(heads, width)
    lower = (iota((length, length), 1) <= iota((length, length), 0)).astype(BF16)
    copies[0].wait()
    copies[1].wait()
    x = x_buf[...]
    logits = sum(dot_nt(x, part) for part in split(w_buf[...], 2))
    decay_logit = logits[:, :heads]
    soft = jnp.maximum(decay_logit, 0.0) + jnp.log1p(jnp.exp(-jnp.abs(decay_logit)))
    slope = jax.nn.sigmoid(decay_logit)
    gamma = jax.nn.sigmoid(logits[:, heads:]) * (1.0 / WINDOW)
    copies[2].wait()
    total = mask_dot(lower, -rate_buf[...] * soft, 3)
    small_ref[...] = jnp.concatenate(
        [total, gamma, soft, slope, jnp.zeros((length, LANES - 4 * heads), F32)], axis=1
    )
    info = jnp.concatenate(
        [part.astype(F32) for part in split(total[:WINDOW], 3)]
        + [jnp.zeros((WINDOW, LANES - 3 * heads), F32)],
        axis=1,
    ).astype(BF16)
    copies[3].wait()
    copies[4].wait()
    coef = coef_buf[...]
    wk = (phi(k_buf[...].astype(F32), coef) * expand(gamma, table)).astype(BF16)
    wk_ref[...] = wk
    copies[5].wait()
    qf = phi(q_buf[...].astype(F32), coef).astype(BF16)
    qf_ref[...] = qf
    copies[6].wait()
    copies[7].wait()
    kept = mask_dot(window_own_t(length), jnp.exp(total[length - 1:] - total), 2)
    faded = jnp.exp(total[late:] - total[late - 1:late])
    scale = expand(jnp.concatenate([kept, faded], axis=0), table)
    carried = (wk.astype(F32) * scale[:length]).astype(BF16)
    faded = (g_buf[late:].astype(F32) * scale[length:]).astype(BF16)
    memory, adjoint = [], []
    for pair in range(width // LANES):
        at = slice(pair * LANES, (pair + 1) * LANES)
        memory.append(folded(dot_tn(carried[:, at], v_buf[:, at])))
        adjoint.append(folded(dot_tn(qf[late:, at], faded[:, at])))
    memory, adjoint = jnp.concatenate(memory, axis=1), jnp.concatenate(adjoint, axis=1)
    memory_ref[...] = memory
    adjoint_ref[...] = adjoint

    def pack(onward, back):
        onward[:WINDOW] = wk[late:]
        onward[WINDOW:2 * WINDOW] = v_buf[late:]
        back[:WINDOW] = qf[:WINDOW]
        back[WINDOW:2 * WINDOW] = g_buf[:WINDOW]
        onward[2 * WINDOW:2 * WINDOW + BAND] = jnp.zeros((BAND, width), BF16)
        back[2 * WINDOW:2 * WINDOW + BAND] = jnp.zeros((BAND, width), BF16)
        for step in range(WINDOW // BAND):
            band = info[step * BAND:(step + 1) * BAND]
            back[2 * WINDOW:2 * WINDOW + BAND, step * LANES:(step + 1) * LANES] = band

    odd = is_odd(me_ref)
    pl.when(odd)(lambda: pack(far_ref, near_ref))
    pl.when(jnp.logical_not(odd))(lambda: pack(near_ref, far_ref))
    near_ref[2 * WINDOW + BAND:] = jnp.where(everywhere(odd, memory.shape), adjoint, memory).astype(BF16)

    @pl.when((me_ref[0] == 0) | (me_ref[0] == count - 1))
    def _():
        far_ref[...] = jnp.zeros_like(far_ref)


def received(me_ref, near_ref, far_ref, fwd_ref, bwd_ref):
    odd = is_odd(me_ref)

    def keep(before, after):
        fwd_ref[...] = before[:2 * WINDOW + BAND]
        bwd_ref[...] = after[:2 * WINDOW + BAND]

    pl.when(odd)(lambda: keep(near_ref, far_ref))
    pl.when(jnp.logical_not(odd))(lambda: keep(far_ref, near_ref))


def next_decay(rim_ref, heads):
    info = jnp.concatenate(
        [
            rim_ref[2 * WINDOW:2 * WINDOW + BAND, step * LANES:(step + 1) * LANES]
            for step in range(WINDOW // BAND)
        ],
        axis=0,
    ).astype(F32)
    return info[:, :heads] + info[:, heads:2 * heads] + info[:, 2 * heads:3 * heads]


def join_kernel(heads, count, before_if_odd, me_ref, own_ref, edge_ref, small_ref, memory_ref, adjoint_ref, rim_ref,
                *rest):
    part_ref, out_ref, weight_ref = rest if len(rest) == 3 else (*rest, None)
    width = rim_ref.shape[1]
    length = small_ref.shape[0]
    table = head_table(heads, width)
    total = small_ref[:, :heads]
    last = total[length - 1:]
    middle = total[length - WINDOW - 1:length - WINDOW]
    next_total = next_decay(rim_ref, heads)
    before = is_odd(me_ref) if before_if_odd else jnp.logical_not(is_odd(me_ref))
    kept = mask_dot(window_rim_t(), jnp.exp(middle - total[:WINDOW]), 2)
    scale = jnp.where(everywhere(before, kept.shape), kept, jnp.exp(next_total))
    fade = jnp.exp(last - middle)
    weight = jnp.where(
        everywhere(before, fade.shape), jnp.exp(last), fade * jnp.exp(next_total[WINDOW - 1:])
    )
    scale = expand(jnp.concatenate([scale, fade, weight], axis=0), table)
    scaled = (rim_ref[WINDOW:2 * WINDOW].astype(F32) * scale[:WINDOW]).astype(BF16)
    fade, weight = scale[WINDOW:WINDOW + 1], scale[WINDOW + 1:]
    base = jnp.where(everywhere(before, memory_ref.shape), memory_ref[...], adjoint_ref[...])
    if weight_ref is None:
        base = base + weight * rim_ref[2 * WINDOW + BAND:].astype(F32)
    else:
        edge = (me_ref[0] == 0) | (me_ref[0] == count - 1)
        weight_ref[...] = jnp.where(everywhere(edge, weight.shape), 0.0, weight)
    for pair in range(width // LANES):
        at = slice(pair * LANES, (pair + 1) * LANES)
        part = folded(dot_tn(rim_ref[:WINDOW, at], scaled[:, at]))
        part_ref[:, at] = part
        out_ref[:, at] = (base[:, at] + fade[:, at] * part).astype(out_ref.dtype)


def pass_kernel(me_ref, base_ref, weight_ref, state_ref, out_ref):
    out_ref[...] = (base_ref[...] + weight_ref[...] * state_ref[...].astype(F32)).astype(BF16)


def decays(column_pair, row_pair, keep):
    gap = jnp.where(keep, column_pair - row_pair, -1e30)
    return jnp.exp(gap)


def own_kernel(heads, me_ref, small_ref, wk_ref, qf_ref, v_ref, g_ref, dq_ref, dwk_ref, dv_ref, dl_ref):
    length, width = wk_ref.shape
    table = head_table(heads, width)
    masks = half_masks()
    small = small_ref[...]
    total = small[:, :heads]
    total_t = jnp.transpose(small)[:heads]
    keep = iota((length, length), 1) <= iota((length, length), 0)
    own = window_own(length).astype(F32)
    empty = jnp.zeros_like(own)
    windows = jnp.concatenate(
        [jnp.concatenate([own, empty], axis=1), jnp.concatenate([empty, own], axis=1)], axis=0
    ).astype(BF16)
    pairs = [slice(pair * LANES, (pair + 1) * LANES) for pair in range(width // LANES)]
    held = []
    for pair, at in enumerate(pairs):
        decay = jnp.concatenate(
            [decays(total[:, i:i + 1], total_t[i:i + 1], keep) for i in (2 * pair, 2 * pair + 1)], axis=1
        )
        kernel = dot(decay.astype(BF16), windows)
        scores = dot_nt(qf_ref[:, at], stacked(wk_ref[:, at], masks))
        lifted = dot_nt(g_ref[:, at], stacked(v_ref[:, at], masks))
        held.append(
            (
                decay,
                (scores * kernel).astype(BF16),
                (lifted * kernel).astype(BF16),
                (lifted * scores).astype(BF16),
            )
        )
    columns = []
    products = []
    for (decay, weights, d_scores, d_kernel), at in zip(held, pairs):
        q, g = qf_ref[:, at], g_ref[:, at]
        products.append(dot(weights, stacked(v_ref[:, at], masks)) * g.astype(F32))
        dq_ref[:, at] = dot(d_scores, stacked(wk_ref[:, at], masks))
        dwk_ref[:, at] = dot_tn(one_above(d_scores), stacked(q, masks))
        dv_ref[:, at] = dot_tn(one_above(weights), stacked(g, masks))
        column = jnp.sum(dot_nt(d_kernel, windows) * decay, axis=0, keepdims=True)
        columns += [column[:, :length], column[:, length:]]
    column = jnp.concatenate(columns + [jnp.zeros((LANES - heads, length), F32)], axis=0)
    rows = head_sum(jnp.concatenate(products, axis=1), table)
    dl_ref[...] = rows - jnp.transpose(column)[:, :heads]


def edge_decay(total, heads):
    lane = iota((WINDOW, LANES), 1)
    first = lane < LANES // 2
    keep = jnp.where(first, lane, lane - LANES // 2) <= iota((WINDOW, LANES), 0)
    doubled = jnp.concatenate([total, total], axis=0)
    doubled = jnp.concatenate([doubled, jnp.zeros((2 * WINDOW, LANES - heads), F32)], axis=1)
    rows = jnp.transpose(doubled)[:heads]
    return lambda h: decays(
        jnp.where(first, total[:, h:h + 1], total[:, h + 1:h + 2]),
        jnp.where(first, rows[h:h + 1], rows[h + 1:h + 2]),
        keep,
    )


def scales_of(heads, small_ref, scales_ref):
    length = small_ref.shape[0]
    late = length - WINDOW
    total, gamma = small_ref[:, :heads], small_ref[:, heads:2 * heads]
    last, middle = total[length - 1:], total[late - 1:late]
    own = mask_dot(window_own_t(length), jnp.exp(last - total), 2)
    grown = jnp.exp(jnp.concatenate([total[:late], total[late:] - middle], axis=0))
    rest = [jnp.exp(middle), jnp.exp(last - middle), jnp.zeros((BAND - 2, heads), F32)]
    scales = jnp.concatenate([own, grown, gamma] + rest, axis=0)
    scales_ref[...] = expand(scales, head_table(heads, scales_ref.shape[1]))


def edge_kernel(heads, before_if_odd, me_ref, small_ref, wk_ref, qf_ref, v_ref, g_ref, rim_ref,
                first_ref, second_ref, dl_ref, *rest):
    length, width = wk_ref.shape
    late = length - WINDOW
    table = head_table(heads, width)
    masks = half_masks()
    pairs = [slice(pair * LANES, (pair + 1) * LANES) for pair in range(width // LANES)]
    cell = (iota((LANES, LANES), 0), iota((LANES, LANES), 1))
    same = (cell[0] < WINDOW) == (cell[1] < WINDOW)
    windows = (same & (cell[0] < cell[1])).astype(BF16)
    before = is_odd(me_ref) if before_if_odd else jnp.logical_not(is_odd(me_ref))
    if rest:
        scales_of(heads, small_ref, rest[0])

    @pl.when(before)
    def _():
        decay_at = edge_decay(small_ref[:WINDOW, :heads], heads)
        held = []
        for pair, at in enumerate(pairs):
            keys, values = stacked(rim_ref[:WINDOW, at], masks), stacked(rim_ref[WINDOW:2 * WINDOW, at], masks)
            decay = decay_at(2 * pair)
            kernel = dot(decay.astype(BF16), windows)
            scores = dot_nt(qf_ref[:WINDOW, at], keys)
            lifted = dot_nt(g_ref[:WINDOW, at], values)
            held.append(
                (
                    keys,
                    values,
                    decay,
                    (scores * kernel).astype(BF16),
                    (lifted * kernel).astype(BF16),
                    (lifted * scores).astype(BF16),
                )
            )
        columns, products = [], []
        for (keys, values, decay, weights, d_scores, d_kernel), at in zip(held, pairs):
            products.append(dot(weights, values) * g_ref[:WINDOW, at].astype(F32))
            first_ref[:, at] = dot(d_scores, keys)
            column = jnp.sum(dot_nt(d_kernel, windows) * decay, axis=0, keepdims=True)
            columns += [column[:, :WINDOW], column[:, WINDOW:]]
        column = jnp.concatenate(columns + [jnp.zeros((LANES - heads, WINDOW), F32)], axis=0)
        column = jnp.concatenate([column, jnp.zeros((LANES, LANES - WINDOW), F32)], axis=1)
        rows = head_sum(jnp.concatenate(products, axis=1), table)
        dl_ref[...] = rows - jnp.transpose(column)[:WINDOW, :heads]

    @pl.when(jnp.logical_not(before))
    def _():
        decay_at = edge_decay(next_decay(rim_ref, heads), heads)
        held = []
        for pair, at in enumerate(pairs):
            q, g = rim_ref[:WINDOW, at], rim_ref[WINDOW:2 * WINDOW, at]
            keys, values = stacked(wk_ref[late:, at], masks), stacked(v_ref[late:, at], masks)
            kernel = dot(decay_at(2 * pair).astype(BF16), windows)
            held.append(
                (q, g, (dot_nt(q, keys) * kernel).astype(BF16), (dot_nt(g, values) * kernel).astype(BF16))
            )
        for (q, g, weights, d_scores), at in zip(held, pairs):
            first_ref[:, at] = dot_tn(one_above(d_scores), stacked(q, masks))
            second_ref[:, at] = dot_tn(one_above(weights), stacked(g, masks))


def finish_kernel(heads, count, me_ref, q_ref, k_ref, x_ref, v_ref, g_ref, coef_ref, rate_ref,
                  small_ref, wk_ref, qf_ref, near_ref, far_ref, adjoint_ref,
                  dqf_ref, dwk_ref, dvl_ref, dl_ref, scales_ref,
                  near_first_ref, near_second_ref, near_dl_ref, far_first_ref, far_second_ref, far_dl_ref,
                  near_part_ref, far_part_ref, cross_ref, passed_ref,
                  dq_ref, dk_ref, dv_ref, logits_ref, sums_ref,
                  fwd_ref, bwd_ref, rim_dq_ref, rim_dwk_ref, rim_dv_ref, rim_dl_ref):
    length, width = wk_ref.shape
    late = length - WINDOW
    pairs = width // LANES
    received(me_ref, near_ref, far_ref, fwd_ref, bwd_ref)

    def edges(dq, dl, dwk, dv):
        rim_dq_ref[...], rim_dl_ref[...] = dq[...], dl[...]
        rim_dwk_ref[...], rim_dv_ref[...] = dwk[...], dv[...]

    far_edge = (far_first_ref, far_dl_ref, near_first_ref, near_second_ref)
    near_edge = (near_first_ref, near_dl_ref, far_first_ref, far_second_ref)
    pl.when(is_odd(me_ref))(lambda: edges(*near_edge))
    pl.when(jnp.logical_not(is_odd(me_ref)))(lambda: edges(*far_edge))
    table = head_table(heads, width)
    masks = half_masks()
    small = small_ref[...]
    total, gamma, soft, slope = (small[:, i * heads:(i + 1) * heads] for i in range(4))
    last, middle = total[length - 1:], total[late - 1:late]
    tail = jnp.exp(last - total)
    own = mask_dot(window_own_t(length), tail, 2)
    next_total = next_decay(bwd_ref, heads)
    next_middle = next_total[WINDOW - 1:]
    onward = mask_dot(window_rim_t(), jnp.exp(next_middle - next_total), 2)
    grown = jnp.exp(jnp.concatenate([total[:late], total[late:] - middle], axis=0))
    fade = jnp.exp(last - middle)
    onward_x = expand(jnp.concatenate([onward, jnp.exp(next_middle)], axis=0), table)
    onward_x, next_x = onward_x[:WINDOW], onward_x[WINDOW:]
    own_x, grown_x, gamma_x = (scales_ref.at[i * length:(i + 1) * length] for i in range(3))
    middle_x, fade_x = (scales_ref[i:i + 1] for i in range(3 * length, 3 * length + 2))

    me = me_ref[0]
    shape = (WINDOW, width)
    odd = everywhere(is_odd(me_ref), shape)
    edge = everywhere((me == 0) | (me == count - 1), shape)
    cross = jnp.where(edge, 0.0, cross_ref[...].astype(F32))
    passed = passed_ref[...].astype(F32)
    near_part, far_part = near_part_ref[...], far_part_ref[...]
    start = jnp.where(odd, passed, cross)
    later = jnp.where(odd, cross, passed)
    after = jnp.where(odd, far_part, near_part) + next_x * later
    halfway = middle_x * start + jnp.where(odd, near_part, far_part)
    half_after = adjoint_ref[...] + fade_x * after
    d_state = jnp.sum(head_sum(after * halfway, table, 2), axis=0, keepdims=True)
    start, later, after, halfway, half_after = (
        z.astype(BF16) for z in (start, later, after, halfway, half_after)
    )

    own_products, rim_products, out_products, key_products, d_coef = [], [], [], [], []
    coef = coef_ref[...]
    for pair in range(pairs):
        at = slice(pair * LANES, (pair + 1) * LANES)
        m0, m1, a1, a0, b0 = (stacked(z[:, at], masks) for z in (start, halfway, after, half_after, later))
        qf, g, wk, v = qf_ref[:, at], g_ref[:, at], wk_ref[:, at], v_ref[:, at]
        from_q = jnp.concatenate([dot(qf[:late], m0), dot(qf[late:], m1)], axis=0)
        out_products.append(from_q * g.astype(F32))
        from_g = jnp.concatenate([dot_nt(g[:late], m0), dot_nt(g[late:], m1)], axis=0)
        dqf = dqf_ref[:, at] + grown_x[:, at] * from_g
        dqf = jnp.concatenate([dqf[:late] + rim_dq_ref[:, at], dqf[late:]], axis=0)
        from_keys = dot(wk, a1)
        own_products.append(from_keys * v.astype(F32))
        rim_products.append(dot(fwd_ref[:WINDOW, at], a0) * fwd_ref[WINDOW:2 * WINDOW, at].astype(F32))
        dwk = dwk_ref[:, at] + own_x[:, at] * dot_nt(v, a1)
        dv = dvl_ref[:, at] + own_x[:, at] * from_keys
        dwk = jnp.concatenate(
            [dwk[:late], dwk[late:] + rim_dwk_ref[:, at] + onward_x[:, at] * dot_nt(v[late:], b0)], axis=0
        )
        dv_ref[:late, at] = dv[:late].astype(BF16)
        dv_ref[late:, at] = (
            dv[late:] + rim_dv_ref[:, at] + onward_x[:, at] * dot(wk[late:], b0)
        ).astype(BF16)
        q, k = q_ref[:, at].astype(F32), k_ref[:, at].astype(F32)
        c = coef[:, at]
        key_products.append(dwk * phi(k, c))
        d_phi = dwk * gamma_x[:, at]
        dq_ref[:, at] = dqf
        dk_ref[:, at] = d_phi
        d_coef.append(jnp.sum(dqf * (0.125 * q * q) + d_phi * (0.125 * k * k), axis=0, keepdims=True))

    sums = jnp.concatenate(
        [
            jnp.concatenate(z, axis=1).astype(BF16)
            for z in (own_products, out_products, key_products, rim_products)
        ],
        axis=0,
    )
    sums = dot_nt(sums, table)
    d_own, d_out, d_gamma = (sums[i * length:(i + 1) * length] for i in range(3))
    d_rim = sums[3 * length:]
    d_tail = tail * mask_dot(window_own(length), d_own, 2)
    rim_tail = jnp.exp(middle - total[:late]) * mask_dot(window_rim(), d_rim, 2)
    at_end = jnp.sum(own * d_own, axis=0, keepdims=True) + fade * d_state
    d_total = dl_ref[...] + grown * d_out - d_tail
    d_total = jnp.concatenate([d_total[:late] + rim_dl_ref[...] - rim_tail, d_total[late:]], axis=0)
    d_total = d_total + jnp.where(iota((length, heads), 0) == length - 1, at_end, 0.0)
    upper = (iota((length, length), 1) >= iota((length, length), 0)).astype(BF16)
    d_decay = mask_dot(upper, d_total, 3)
    d_rate = -jnp.sum(d_decay * soft, axis=0, keepdims=True)
    d_logits = jnp.concatenate(
        [-rate_ref[...] * d_decay * slope, d_gamma * gamma * (1.0 - WINDOW * gamma)], axis=1
    )
    logits_ref[...] = d_logits
    gate = dot_tn(d_logits.astype(BF16), x_ref[...])
    d_rate = jnp.concatenate([d_rate, jnp.zeros((1, LANES - heads), F32)], axis=1)
    for i in range(pairs):
        sums_ref[i * 2 * heads:(i + 1) * 2 * heads] = gate[:, i * LANES:(i + 1) * LANES].astype(BF16)
    rest = d_coef + [d_rate, jnp.zeros((BAND - 1 - pairs, LANES), F32)]
    sums_ref[pairs * 2 * heads:] = jnp.concatenate(rest, axis=0).astype(BF16)


def outputs_kernel(me_ref, logits_ref, w_ref, q_ref, k_ref, coef_ref, dqf_ref, d_phi_ref, dv_ref,
                   dx_ref, dq_ref, dk_ref, dv_out, sem):
    copy = pltpu.make_async_copy(dv_ref, dv_out, sem)
    copy.start()
    coef = 0.25 * coef_ref[...]
    dq_ref[...] = (dqf_ref[...] * (0.125 + coef * q_ref[...].astype(F32))).astype(BF16)
    dk_ref[...] = (d_phi_ref[...] * (0.125 + coef * k_ref[...].astype(F32))).astype(BF16)
    high, low = (part.astype(F32) for part in split(logits_ref[...], 2))
    w_high, w_low = split(w_ref[...], 2)
    dx_ref[...] = dot(
        jnp.concatenate([high, low, high], axis=1).astype(BF16),
        jnp.concatenate([w_high, w_high, w_low], axis=0),
    ).astype(BF16)
    copy.wait()


def last_kernel(heads, me_ref, mine_ref, theirs_ref, gate_ref, coef_ref, rate_ref):
    blocks = gate_ref.shape[1] // LANES

    def write(sums_ref):
        rest = sums_ref[blocks * 2 * heads:].astype(F32)
        for i in range(blocks):
            at = slice(i * LANES, (i + 1) * LANES)
            gate_ref[:, at] = sums_ref[i * 2 * heads:(i + 1) * 2 * heads].astype(F32)
            coef_ref[:, at] = rest[i:i + 1]
        rate_ref[...] = rest[blocks:blocks + 1, :heads]

    pl.when(is_odd(me_ref))(lambda: write(mine_ref))
    pl.when(jnp.logical_not(is_odd(me_ref)))(lambda: write(theirs_ref))


def call(kernel, outs, operands, name, scratch=(), in_place=(), outside=(), flops=10**8, moved=3 * 10**6):
    specs = [pl.BlockSpec(memory_space=pltpu.SMEM)]
    specs += [
        pl.BlockSpec(memory_space=pltpu.HBM if i in in_place else pltpu.VMEM)
        for i in range(1, len(operands))
    ]
    operands = [
        pltpu.with_memory_space_constraint(z, pltpu.HBM) if i in in_place else z
        for i, z in enumerate(operands)
    ]
    return pl.pallas_call(
        kernel,
        out_shape=tuple(jax.ShapeDtypeStruct(*out) for out in outs),
        in_specs=specs,
        out_specs=tuple(
            pl.BlockSpec(memory_space=pltpu.HBM if i in outside else pltpu.VMEM) for i in range(len(outs))
        ),
        scratch_shapes=list(scratch),
        compiler_params=pltpu.CompilerParams(vmem_limit_bytes=32 * 2**20),
        cost_estimate=pl.CostEstimate(flops=flops, bytes_accessed=moved, transcendentals=10**6),
        name=name,
    )(*operands)


EVERYONE = ("dp", "seq")


def swapped(value, axis, distance):
    return lax.ppermute(value, axis, [(i, i ^ distance) for i in range(lax.axis_size(axis))])


def odd_swapped(value, distance, stage):
    count = lax.axis_size(EVERYONE)
    idle = 2 if distance == 2 * stage else 8 if stage == 2 and count > 8 else 4
    return lax.ppermute(value, EVERYONE, [(i, i ^ (distance if i % 2 else idle)) for i in range(count)])


def inner_swapped(value):
    dp, seq = (lax.axis_size(axis) for axis in EVERYONE)
    pairs = []
    for i in range(dp):
        for j in range(seq):
            inner = 0 < j < seq - 1
            pairs.append((i * seq + j, i * seq + seq - 1 - j if inner else (i ^ 1) * seq + j))
    return lax.ppermute(value, EVERYONE, pairs)


def on_device(queries, key_rows, value_rows, inputs, w_gate, poly_coef, decay_rate, cotangent):
    q, k, v, x, g = (z[0] for z in (queries, key_rows, value_rows, inputs, cotangent))
    length, width = x.shape
    heads = decay_rate.shape[0]
    count = lax.axis_size("seq")
    assert count == 4 and length == 2 * WINDOW
    me = lax.axis_index("seq").astype(jnp.int32).reshape(1)
    wide, small = ((length, width), BF16), ((length, LANES), F32)
    full, half, gain = ((length, width), F32), ((WINDOW, width), F32), ((length, heads), F32)
    rim, sent = ((2 * WINDOW + BAND, width), BF16), ((WINDOW, width), BF16)
    wk, qf, gates, near, far, memory, adjoint, q, k, v, x, g, wt, coef, rate = call(
        functools.partial(prep_kernel, heads, count),
        [wide, wide, small, ((3 * WINDOW + BAND, width), BF16), rim, half, half]
        + [wide] * 5
        + [((2 * heads, width), F32), ((1, width), F32), ((1, heads), F32)],
        (me, q, k, v, x, g, w_gate.T, poly_coef.reshape(1, width), decay_rate.reshape(1, heads)),
        "prep",
        scratch=[pltpu.SemaphoreType.DMA((8,))],
        in_place=range(1, 9),
    )
    near = swapped(near, "seq", 1)
    far = inner_swapped(far)
    near_part, cross = call(
        functools.partial(join_kernel, heads, count, True),
        [half, sent],
        (me, gates, gates, gates, memory, adjoint, near),
        "join_near",
    )
    cross = inner_swapped(cross)
    own = call(
        functools.partial(own_kernel, heads),
        [full, full, full, gain],
        (me, gates, wk, qf, v, g),
        "own",
        flops=7 * 10**8,
        moved=7 * 10**6,
    )
    edge = [half, half, ((WINDOW, heads), F32)]
    *near_edge, scales = call(
        functools.partial(edge_kernel, heads, True),
        edge + [((3 * length + BAND, width), F32)],
        (me, gates, wk, qf, v, g, near),
        "edge_near",
        flops=2 * 10**8,
        moved=5 * 10**6,
    )
    far_part, base, weight = call(
        functools.partial(join_kernel, heads, count, False),
        [half, half, ((1, width), F32)],
        (me, own[3], near_edge[2], gates, memory, adjoint, far),
        "join_far",
    )
    passed = call(pass_kernel, [sent], (me, base, weight, cross), "pass_on")[0]
    passed = swapped(passed, "seq", 1)
    far_edge = call(
        functools.partial(edge_kernel, heads, False),
        edge,
        (me, gates, wk, qf, v, g, far),
        "edge_far",
        flops=2 * 10**8,
        moved=3 * 10**6,
    )
    all_sums = ((width // LANES * 2 * heads + BAND, LANES), BF16)
    dqf, d_phi, dv, d_logits, sums = call(
        functools.partial(finish_kernel, heads, count),
        [full, full, wide, ((length, 2 * heads), F32), all_sums],
        (me, q, k, x, v, g, coef, rate, gates, wk, qf, near, far, adjoint, *own, scales, *near_edge, *far_edge,
         near_part, far_part, cross, passed),
        "finish",
        scratch=[pltpu.VMEM(*z) for z in (rim, rim, half, half, half, edge[2])],
    )
    dx, dq, dk, dv = call(
        outputs_kernel,
        [wide] * 4,
        (me, d_logits, wt, q, k, coef, dqf, d_phi, dv),
        "outputs",
        scratch=[pltpu.SemaphoreType.DMA],
        outside=(3,),
    )
    sums = sums.astype(F32) + swapped(sums, EVERYONE, 1).astype(F32)
    distance = 2
    while distance < lax.axis_size(EVERYONE):
        sums = sums.astype(BF16)
        if 2 * distance < lax.axis_size(EVERYONE):
            far, mid, one = (odd_swapped(sums, i * distance, distance).astype(F32) for i in (3, 2, 1))
            sums = (one + mid) + (far + sums.astype(F32))
        else:
            sums = sums.astype(F32) + odd_swapped(sums, distance, distance).astype(F32)
        if distance == 2:
            sums, dx, dq, dk, dv = lax.optimization_barrier((sums, dx, dq, dk, dv))
        distance *= 4
    sums = sums.astype(BF16)
    gate, d_coef, d_rate = call(
        functools.partial(last_kernel, heads),
        [((2 * heads, width), F32), ((1, width), F32), ((1, heads), F32)],
        (me, sums, swapped(sums, EVERYONE, 1)),
        "last",
    )
    return (dq[None], dk[None], dv[None], dx[None], gate.T, d_coef.reshape(width), d_rate.reshape(heads))


def solution(mesh):
    rows = P("dp", "seq", None)
    return jax.shard_map(
        on_device,
        mesh=mesh,
        in_specs=(rows, rows, rows, rows, P(), P(), P(), rows),
        out_specs=(rows, rows, rows, rows, P(), P(), P()),
        check_vma=False,
    )
```
